32 devices in a mesh: wide: 8 (over y, x, core), narrow: 4 (over z).
Axes of the slice: x: 2, y: 2, z: 4, core: 2. Of those that a mesh axis runs over, the one named last changes fastest.
Arguments:
- samples: bfloat16 [256, 128, 768], P(('wide', 'narrow')), may hold values from -6 to 6
- cotangent: bfloat16 [256, 128, 768], P(('wide', 'narrow')), may hold values from -6 to 6
- visible: int32 [256], P(('wide', 'narrow')), may hold values from 8 to 128, as said below
- master_attn: float32 [2359296], P(('wide', 'narrow')), may hold values from -0.57735027 to 0.57735027
- first_attn: float32 [2359296], P(('wide', 'narrow')), may hold values from -192 to 192
- second_attn: float32 [2359296], P(('wide', 'narrow')), may hold values from 983.04 to 3932.16
- master_mlp: float32 [4718592], P(('wide', 'narrow')), may hold values from -0.14433757 to 0.14433757
- first_mlp: float32 [4718592], P(('wide', 'narrow')), may hold values from -192 to 192
- second_mlp: float32 [4718592], P(('wide', 'narrow')), may hold values from 983.04 to 3932.16
- master_small: float32 [9216], P(('wide', 'narrow')), may hold values from -1 to 2
- first_small: float32 [9216], P(('wide', 'narrow')), may hold values from -384 to 384
- second_small: float32 [9216], P(('wide', 'narrow')), may hold values from 4259.84 to 16384
Outputs:
- output: bfloat16 [256, 128, 768], P(('wide', 'narrow'))
- grad_samples: bfloat16 [256, 128, 768], P(('wide', 'narrow'))
- new_attn: float32 [2359296], P(('wide', 'narrow'))
- new_first_attn: float32 [2359296], P(('wide', 'narrow'))
- new_second_attn: float32 [2359296], P(('wide', 'narrow'))
- new_mlp: float32 [4718592], P(('wide', 'narrow'))
- new_first_mlp: float32 [4718592], P(('wide', 'narrow'))
- new_second_mlp: float32 [4718592], P(('wide', 'narrow'))
- new_small: float32 [9216], P(('wide', 'narrow'))
- new_first_small: float32 [9216], P(('wide', 'narrow'))
- new_second_small: float32 [9216], P(('wide', 'narrow'))
The draws below stay inside these ranges and needn't reach their ends.
Inputs may be any that keep to these rules, and one draw needn't show every extreme that they name: Slots j < visible[s] of each sample are visible; the counts are heavy-tailed, and every draw has a sample with all 128 visible and one with 8.
All inputs are finite; a program needn't handle non-finite values.
Results may differ from the reference program's by a relative error of at most 0.013.
Values may be sent and summed in bfloat16 or wider, within the bound.
No kernel may reach another device: no remote copies, remote signals or barrier semaphores. Data moves between devices by JAX's collectives and lax.ppermute only.
A program may use at most 192 MiB of HBM per device.

```python
import math
from functools import partial
import jax
import jax.numpy as jnp
from jax import lax

D = 768
FF = 3072
H = 12
HD = 64
P_SIZE = 128
STEP = 10
SAMP_DEV = 8
SAMPLES = 256
ATTN_N = 2359296
MLP_N = 4718592
SMALL_N = 9216
N_NARROW = 4


def draw_visible(key, part):
    key = jax.random.fold_in(key, 1)
    keys = jax.random.split(key, 5)
    first = jax.random.randint(keys[0], (SAMPLES,), 1, P_SIZE + 1)
    second = jax.random.randint(keys[1], (SAMPLES,), 1, P_SIZE + 1)
    third = jax.random.randint(keys[2], (SAMPLES,), 1, P_SIZE + 1)
    counts = jnp.maximum(P_SIZE // 16, first * second * third // (P_SIZE * P_SIZE))
    top = jax.random.randint(keys[3], (), 0, SAMPLES)
    other = (top + 1 + jax.random.randint(keys[4], (), 0, SAMPLES - 1)) % SAMPLES
    counts = counts.at[top].set(P_SIZE)
    counts = counts.at[other].set(P_SIZE // 16)
    return counts.astype(jnp.int32)


def draw_master_attn(key, part):
    key = jax.random.fold_in(key, 2)
    base = jax.random.truncated_normal(key, -4.0, 4.0, (4 * D * D,), jnp.float32)
    place = jnp.arange(4 * D * D)
    factor = jnp.where(place < 3 * D * D, 1.0, 4.0) / D ** 0.5
    return base * factor


def draw_master_mlp(key, part):
    key = jax.random.fold_in(key, 3)
    base = jax.random.truncated_normal(key, -4.0, 4.0, (2 * D * FF,), jnp.float32)
    place = jnp.arange(2 * D * FF)
    factor = jnp.where(place < D * FF, 1.0 / D ** 0.5, 1.0 / FF ** 0.5)
    return base * factor


def draw_master_small(key, part):
    key = jax.random.fold_in(key, 4)
    base = jax.random.truncated_normal(key, -4.0, 4.0, (8 * D + FF,), jnp.float32)
    place = jnp.arange(8 * D + FF)
    gains = (place < D) | (place >= 5 * D) & (place < 6 * D)
    return jnp.where(gains, 1.0 + 0.1 * base, 0.2 * base)


def steps_of(own_key, shape, cuts, least, top_value):
    loudness = 1.0
    for axis_at, shards_of in cuts:
        heights = jax.random.uniform(jax.random.fold_in(jax.random.fold_in(own_key, 6), axis_at), (shards_of,), jnp.float32, least / len(cuts), top_value / len(cuts))
        loudness = loudness * jnp.repeat(jnp.exp(heights), shape[axis_at] // shards_of).reshape((-1,) + (1,) * (len(shape) - 1 - axis_at))
    return loudness


def gaussian(rng, dims, scale, bound, cuts=(), held_as=jnp.bfloat16):
    level = steps_of(rng, dims, cuts, -0.22, 0.18) if cuts else 1.0
    drawn = jax.random.normal(rng, dims, jnp.float32) * scale * level
    return jnp.minimum(jnp.maximum(drawn, -bound), bound).astype(held_as)


def setup_inputs(seed: int = 0) -> dict:
    key_of = jax.random.split(jax.random.key(seed), 13)
    return {
        "samples": gaussian(key_of[0], (SAMPLES, P_SIZE, D), 1.0, 6.0, ((0, 32),)),
        "cotangent": gaussian(key_of[1], (SAMPLES, P_SIZE, D), 1.0, 6.0, ((0, 32),)),
        "visible": draw_visible(jax.random.fold_in(key_of[12], 71), 0),
        "master_attn": draw_master_attn(jax.random.fold_in(key_of[12], 71), 0),
        "first_attn": gaussian(key_of[4], (ATTN_N,), (0.17 * (SAMPLES * P_SIZE) ** 0.5), 192.0, ((0, 32),), jnp.float32),
        "second_attn": jnp.clip(jnp.exp(math.log(3932.16) - 1.3862944 * jax.random.uniform(key_of[5], (ATTN_N,), jnp.float32) ** steps_of(key_of[5], (ATTN_N,), ((0, 32),), -0.2, 0.2)), 983.04, 3932.16),
        "master_mlp": draw_master_mlp(jax.random.fold_in(key_of[12], 71), 0),
        "first_mlp": gaussian(key_of[7], (MLP_N,), (0.17 * (SAMPLES * P_SIZE) ** 0.5), 192.0, ((0, 32),), jnp.float32),
        "second_mlp": jnp.clip(jnp.exp(math.log(3932.16) - 1.3862944 * jax.random.uniform(key_of[8], (MLP_N,), jnp.float32) ** steps_of(key_of[8], (MLP_N,), ((0, 32),), -0.2, 0.2)), 983.04, 3932.16),
        "master_small": draw_master_small(jax.random.fold_in(key_of[12], 71), 0),
        "first_small": gaussian(key_of[10], (SMALL_N,), (0.36 * (SAMPLES * P_SIZE) ** 0.5), 384.0, ((0, 32),), jnp.float32),
        "second_small": jnp.clip(jnp.exp(math.log(16384.0) - 1.3470737 * jax.random.uniform(key_of[11], (SMALL_N,), jnp.float32) ** steps_of(key_of[11], (SMALL_N,), ((0, 32),), -0.2, 0.2)), 4259.84, 16384.0),
    }


@jax.custom_vjp
def low(v):
    return lax.optimization_barrier(v.astype(jnp.bfloat16)).astype(jnp.float32)

@jax.custom_vjp
def low_back(v):
    return v

def low_keep(v):
    return (low(v), None)

def low_pass(kept, grad):
    return (grad,)

def back_keep(v):
    return (v, None)

def back_low(kept, grad):
    return (low(grad),)
low.defvjp(low_keep, low_pass)
low_back.defvjp(back_keep, back_low)
HIGH = lax.Precision.HIGHEST
eps_norm = 1e-06
rate_matrix = 0.03
rate_small = 0.2
eps_adam = 1e-08

def layer_norm(values, gain, bias):
    centre = values - lax.optimization_barrier(jnp.mean(values, -1, keepdims=True))
    spread = lax.optimization_barrier(jnp.mean(centre * centre, -1, keepdims=True))
    return centre * lax.rsqrt(spread + eps_norm) * gain + bias

def split_small(small):
    edges = [0, D, 2 * D, 3 * D, 4 * D, 5 * D, 6 * D, 7 * D, 7 * D + FF, 8 * D + FF]
    return [small[edges[i]:edges[i + 1]] for i in range(9)]

def group_forward(weights, block, counts):
    w_qkv, w_out, w_one, w_two, pieces = weights
    gain_one, bias_one, bias_query, bias_value, bias_out, gain_two, bias_two, bias_inner, bias_outer = pieces
    group = block.shape[0]
    rows = block.reshape(group * P_SIZE, D)
    valid = jnp.arange(P_SIZE)[None, :] < counts[:, None]
    first_in = low(layer_norm(rows, gain_one, bias_one))
    shift = jnp.concatenate([bias_query, jnp.zeros_like(bias_query), bias_value])
    qkv = low(low_back(jnp.dot(first_in, w_qkv, precision=HIGH) + shift)).reshape(group, P_SIZE, 3, H, HD)
    query = qkv[:, :, 0]
    keys = qkv[:, :, 1]
    values = qkv[:, :, 2]
    scores = low_back(jnp.einsum('sqhd,skhd->shqk', query, keys, precision=HIGH) * (1.0 / math.sqrt(HD)))
    scores = jnp.where(valid[:, None, None, :], scores, -1e+30)
    probs = low(jax.nn.softmax(scores, axis=-1))
    context = jnp.einsum('shqk,skhd->sqhd', probs, values, precision=HIGH)
    context = low(low_back(context)).reshape(group * P_SIZE, D)
    middle = rows + low_back(jnp.dot(context, w_out, precision=HIGH) + bias_out)
    second_in = low(layer_norm(middle, gain_two, bias_two))
    inner = low_back(jnp.dot(second_in, w_one, precision=HIGH) + bias_inner)
    active = low(jax.nn.gelu(inner, approximate=False))
    result = middle + low_back(jnp.dot(active, w_two, precision=HIGH) + bias_outer)
    result = result.reshape(group, P_SIZE, D)
    return jnp.where(valid[:, :, None], result, 0.0)

def forward_all(master_attn, master_mlp, master_small, rows, visible):
    attn_low = low(master_attn)
    mlp_low = low(master_mlp)
    small_low = low(master_small)
    weights = (attn_low[:3 * D * D].reshape(D, 3 * D), attn_low[3 * D * D:].reshape(D, D), mlp_low[:D * FF].reshape(D, FF), mlp_low[D * FF:].reshape(FF, D), split_small(small_low))
    group = SAMP_DEV * N_NARROW
    blocks = rows.reshape(-1, group, P_SIZE, D)
    counts = visible.reshape(-1, group)
    checked = jax.checkpoint(group_forward)

    def advance(carry, item):
        return (carry, checked(weights, item[0], item[1]))
    _, outs = lax.scan(advance, None, (blocks, counts))
    return outs.reshape(-1, P_SIZE, D)

def adamw(master, first, second, grad, decay, step_rate):
    first_new = 0.5 * first + 0.5 * grad
    second_new = 0.5 * second + 0.5 * grad * grad
    first_hat = first_new / (1.0 - 0.5 ** STEP)
    second_hat = second_new / (1.0 - 0.5 ** STEP)
    master_new = master - step_rate * (first_hat / (jnp.sqrt(second_hat) + eps_adam) + decay * master)
    return (master_new, first_new, second_new)

def reference(samples, cotangent, visible, master_attn, first_attn, second_attn, master_mlp, first_mlp, second_mlp, master_small, first_small, second_small):
    rows = samples.astype(jnp.float32)
    result, pullback = jax.vjp(partial(forward_all, visible=visible), master_attn, master_mlp, master_small, rows)
    grad_attn, grad_mlp, grad_small, grad_rows = pullback(cotangent.astype(jnp.float32))
    new_attn, new_first_attn, new_second_attn = adamw(master_attn, first_attn, second_attn, grad_attn, 0.1, rate_matrix)
    new_mlp, new_first_mlp, new_second_mlp = adamw(master_mlp, first_mlp, second_mlp, grad_mlp, 0.1, rate_matrix)
    new_small, new_first_small, new_second_small = adamw(master_small, first_small, second_small, grad_small, 0.0, rate_small)
    return (result.astype(jnp.bfloat16), grad_rows.astype(jnp.bfloat16), new_attn, new_first_attn, new_second_attn, new_mlp, new_first_mlp, new_second_mlp, new_small, new_first_small, new_second_small)
```

```python
import math

import jax
import jax.numpy as jnp
from jax import lax
from jax.sharding import PartitionSpec as P

D = 768
FF = 3072
H = 12
HD = 64
STEP = 10


eps_norm = 1e-06
rate_matrix = 0.03
rate_small = 0.2
eps_adam = 1e-08
inv_root_two = 0.7071067811865476
inv_root_tau = 0.3989422804014327


def split_small(small):
    edges = [0, D, 2 * D, 3 * D, 4 * D, 5 * D, 6 * D, 7 * D, 7 * D + FF, 8 * D + FF]
    return [small[edges[i] : edges[i + 1]] for i in range(9)]


def standard(values):
    centre = values - jnp.mean(values, -1, keepdims=True)
    factor = lax.rsqrt(jnp.mean(centre * centre, -1, keepdims=True) + eps_norm)
    return (centre * factor, factor)


def norm_backward(grad, normed, factor, gain):
    grad_gain = jnp.sum(grad * normed, 0)
    grad_bias = jnp.sum(grad, 0)
    scaled = grad * gain
    inner_mean = jnp.mean(scaled * normed, -1, keepdims=True)
    grad_input = factor * (scaled - jnp.mean(scaled, -1, keepdims=True) - normed * inner_mean)
    return (grad_gain, grad_bias, grad_input)


def masked_scores(query, keys, key_mask):
    raw = jnp.einsum("sqhd,skhd->shqk", query, keys, preferred_element_type=jnp.float32) * (
        1.0 / math.sqrt(HD)
    )
    return jnp.where(key_mask, raw, -1e30)


def adamw(master, first, second, grad, decay, step_rate):
    first_new = 0.5 * first + 0.5 * grad
    second_new = 0.5 * second + 0.5 * grad * grad
    first_hat = first_new / (1.0 - 0.5**STEP)
    second_hat = second_new / (1.0 - 0.5**STEP)
    master_new = master - step_rate * (
        first_hat / (jnp.sqrt(second_hat) + eps_adam) + decay * master
    )
    return (master_new, first_new, second_new)


def scatter_sum(grad):
    lanes = grad.astype(jnp.bfloat16).reshape(-1, 128)
    own = lax.psum_scatter(lanes, ("wide", "narrow"), scatter_dimension=0, tiled=True)
    return own.reshape(-1).astype(jnp.float32)


def on_device(
    samples,
    cotangent,
    visible,
    master_attn,
    first_attn,
    second_attn,
    master_mlp,
    first_mlp,
    second_mlp,
    master_small,
    first_small,
    second_small,
):
    count, length, width = samples.shape
    total_rows = count * length
    scale = 1.0 / math.sqrt(HD)
    attn_full, mlp_full, small_full = (
        lax.all_gather(master_attn.astype(jnp.bfloat16), ("wide", "narrow"), axis=0, tiled=True),
        lax.all_gather(master_mlp.astype(jnp.bfloat16), ("wide", "narrow"), axis=0, tiled=True),
        lax.all_gather(master_small.astype(jnp.bfloat16), ("wide", "narrow"), axis=0, tiled=True),
    )
    w_qkv = attn_full[: 3 * D * D].reshape(D, 3 * D)
    w_out = attn_full[3 * D * D :].reshape(D, D)
    (
        gain_one,
        bias_one,
        bias_query,
        bias_value,
        bias_out,
        gain_two,
        bias_two,
        bias_inner,
        bias_outer,
    ) = split_small(small_full.astype(jnp.float32))
    valid = jnp.arange(length)[None, :] < visible[:, None]
    key_mask = valid[:, None, None, :]
    row_mask = valid.reshape(total_rows, 1)
    rows = samples.astype(jnp.float32).reshape(total_rows, D)
    normed_one, factor_one = standard(rows)
    first_in = (normed_one * gain_one + bias_one).astype(jnp.bfloat16)
    shift = jnp.concatenate([bias_query, jnp.zeros_like(bias_query), bias_value])
    qkv = jnp.dot(first_in, w_qkv, preferred_element_type=jnp.float32) + shift
    qkv_low = qkv.astype(jnp.bfloat16).reshape(count, length, 3, H, HD)
    query = qkv_low[:, :, 0]
    keys = qkv_low[:, :, 1]
    values = qkv_low[:, :, 2]
    scores = masked_scores(query, keys, key_mask)
    top = jnp.max(scores, -1, keepdims=True)
    expo = jnp.exp(scores - top)
    totals = jnp.sum(expo, -1, keepdims=True)
    log_total = top + jnp.log(totals)
    probs_low = (expo / totals).astype(jnp.bfloat16)
    context = jnp.einsum("shqk,skhd->sqhd", probs_low, values, preferred_element_type=jnp.float32)
    context_low = context.astype(jnp.bfloat16).reshape(total_rows, D)
    middle = rows + jnp.dot(context_low, w_out, preferred_element_type=jnp.float32) + bias_out
    w_one = mlp_full[: D * FF].reshape(D, FF)
    w_two = mlp_full[D * FF :].reshape(FF, D)
    normed_two, factor_two = standard(middle)
    second_in = (normed_two * gain_two + bias_two).astype(jnp.bfloat16)
    inner = jnp.dot(second_in, w_one, preferred_element_type=jnp.float32) + bias_inner
    active = jax.nn.gelu(inner, approximate=False).astype(jnp.bfloat16)
    result = middle + jnp.dot(active, w_two, preferred_element_type=jnp.float32) + bias_outer
    output = jnp.where(row_mask, result, 0.0).reshape(count, length, D).astype(jnp.bfloat16)
    grad_result = jnp.where(row_mask, cotangent.astype(jnp.float32).reshape(total_rows, D), 0.0)
    grad_branch = grad_result.astype(jnp.bfloat16)
    grad_w_two = jnp.einsum("rf,rd->fd", active, grad_branch, preferred_element_type=jnp.float32)
    grad_bias_outer = jnp.sum(grad_branch, 0, dtype=jnp.float32)
    grad_active = jnp.einsum("rd,fd->rf", grad_branch, w_two, preferred_element_type=jnp.float32)
    slope = (
        0.5 * (1.0 + jax.scipy.special.erf(inner * inv_root_two))
        + inner * jnp.exp(-0.5 * inner * inner) * inv_root_tau
    )
    grad_inner = (grad_active * slope).astype(jnp.bfloat16)
    grad_w_one = jnp.einsum("rd,rf->df", second_in, grad_inner, preferred_element_type=jnp.float32)
    grad_bias_inner = jnp.sum(grad_inner, 0, dtype=jnp.float32)
    grad_second_in = jnp.einsum("rf,df->rd", grad_inner, w_one, preferred_element_type=jnp.float32)
    grad_gain_two, grad_bias_two, grad_middle_norm = norm_backward(
        grad_second_in, normed_two, factor_two, gain_two
    )
    grad_middle = grad_result + grad_middle_norm
    grad_mlp = jnp.concatenate([grad_w_one.reshape(-1), grad_w_two.reshape(-1)])
    grad_proj = grad_middle.astype(jnp.bfloat16)
    grad_w_out = jnp.einsum("rc,rd->cd", context_low, grad_proj, preferred_element_type=jnp.float32)
    grad_bias_out = jnp.sum(grad_proj, 0, dtype=jnp.float32)
    grad_context = jnp.einsum("rd,cd->rc", grad_proj, w_out, preferred_element_type=jnp.float32)
    grad_context = grad_context.astype(jnp.bfloat16).reshape(count, length, H, HD)
    probs = jnp.exp(masked_scores(query, keys, key_mask) - log_total)
    probs_again = probs.astype(jnp.bfloat16)
    grad_values = jnp.einsum(
        "shqk,sqhd->skhd", probs_again, grad_context, preferred_element_type=jnp.float32
    )
    grad_probs = jnp.einsum(
        "sqhd,skhd->shqk", grad_context, values, preferred_element_type=jnp.float32
    )
    inner_sum = jnp.sum(grad_probs * probs, -1, keepdims=True)
    grad_scores = (probs * (grad_probs - inner_sum)).astype(jnp.bfloat16)
    grad_query = (
        jnp.einsum("shqk,skhd->sqhd", grad_scores, keys, preferred_element_type=jnp.float32) * scale
    )
    grad_keys = (
        jnp.einsum("shqk,sqhd->skhd", grad_scores, query, preferred_element_type=jnp.float32)
        * scale
    )
    grad_qkv = (
        jnp.stack([grad_query, grad_keys, grad_values], 2)
        .reshape(total_rows, 3 * D)
        .astype(jnp.bfloat16)
    )
    grad_w_qkv = jnp.einsum("rd,re->de", first_in, grad_qkv, preferred_element_type=jnp.float32)
    grad_bias_qkv = jnp.sum(grad_qkv, 0, dtype=jnp.float32)
    grad_first_in = jnp.einsum("re,de->rd", grad_qkv, w_qkv, preferred_element_type=jnp.float32)
    grad_gain_one, grad_bias_one, grad_rows_norm = norm_backward(
        grad_first_in, normed_one, factor_one, gain_one
    )
    grad_rows = grad_middle + grad_rows_norm
    grad_samples = grad_rows.reshape(count, length, D).astype(jnp.bfloat16)
    grad_attn = jnp.concatenate([grad_w_qkv.reshape(-1), grad_w_out.reshape(-1)])
    grad_small = jnp.concatenate(
        [
            grad_gain_one,
            grad_bias_one,
            grad_bias_qkv[:D],
            grad_bias_qkv[2 * D :],
            grad_bias_out,
            grad_gain_two,
            grad_bias_two,
            grad_bias_inner,
            grad_bias_outer,
        ]
    )
    summed_attn, summed_mlp, summed_small = (
        scatter_sum(grad_attn),
        scatter_sum(grad_mlp),
        lax.psum_scatter(grad_small, ("wide", "narrow"), scatter_dimension=0, tiled=True),
    )
    new_attn, new_first_attn, new_second_attn = adamw(
        master_attn, first_attn, second_attn, summed_attn, 0.1, rate_matrix
    )
    new_mlp, new_first_mlp, new_second_mlp = adamw(
        master_mlp, first_mlp, second_mlp, summed_mlp, 0.1, rate_matrix
    )
    new_small, new_first_small, new_second_small = adamw(
        master_small, first_small, second_small, summed_small, 0.0, rate_small
    )
    return (
        output,
        grad_samples,
        new_attn,
        new_first_attn,
        new_second_attn,
        new_mlp,
        new_first_mlp,
        new_second_mlp,
        new_small,
        new_first_small,
        new_second_small,
    )


def solution(mesh):
    in_specs = (
        P(("wide", "narrow"), None, None),
        P(("wide", "narrow"), None, None),
        P(("wide", "narrow")),
        P(("wide", "narrow")),
        P(("wide", "narrow")),
        P(("wide", "narrow")),
        P(("wide", "narrow")),
        P(("wide", "narrow")),
        P(("wide", "narrow")),
        P(("wide", "narrow")),
        P(("wide", "narrow")),
        P(("wide", "narrow")),
    )
    out_specs = (
        P(("wide", "narrow"), None, None),
        P(("wide", "narrow"), None, None),
        P(("wide", "narrow")),
        P(("wide", "narrow")),
        P(("wide", "narrow")),
        P(("wide", "narrow")),
        P(("wide", "narrow")),
        P(("wide", "narrow")),
        P(("wide", "narrow")),
        P(("wide", "narrow")),
        P(("wide", "narrow")),
    )
    return jax.shard_map(
        on_device, mesh=mesh, in_specs=in_specs, out_specs=out_specs, check_vma=False
    )
```

```python
import math

import jax
import jax.numpy as jnp
from jax import lax
from jax.experimental import pallas as pl
from jax.experimental.pallas import tpu as pltpu
from jax.sharding import PartitionSpec as P

D = 768
FF = 3072
H = 12
HD = 64
STEP = 10


eps_norm = 1e-06
rate_matrix = 0.03
rate_small = 0.2
eps_adam = 1e-08
inv_root_two = 0.7071067811865476
inv_root_tau = 0.3989422804014327


def split_small(small):
    edges = [0, D, 2 * D, 3 * D, 4 * D, 5 * D, 6 * D, 7 * D, 7 * D + FF, 8 * D + FF]
    return [small[edges[i] : edges[i + 1]] for i in range(9)]


def standard(values):
    centre = values - jnp.mean(values, -1, keepdims=True)
    factor = lax.rsqrt(jnp.mean(centre * centre, -1, keepdims=True) + eps_norm)
    return (centre * factor, factor)


def norm_backward(grad, normed, factor, gain):
    grad_gain = jnp.sum(grad * normed, 0)
    grad_bias = jnp.sum(grad, 0)
    scaled = grad * gain
    inner_mean = jnp.mean(scaled * normed, -1, keepdims=True)
    grad_input = factor * (scaled - jnp.mean(scaled, -1, keepdims=True) - normed * inner_mean)
    return (grad_gain, grad_bias, grad_input)


def masked_scores(query, keys, key_mask):
    raw = jnp.einsum("sqhd,skhd->shqk", query, keys, preferred_element_type=jnp.float32) * (
        1.0 / math.sqrt(HD)
    )
    return jnp.where(key_mask, raw, -1e30)


def adamw(master, first, second, grad, decay, step_rate):
    first_new = 0.5 * first + 0.5 * grad
    second_new = 0.5 * second + 0.5 * grad * grad
    first_hat = first_new / (1.0 - 0.5**STEP)
    second_hat = second_new / (1.0 - 0.5**STEP)
    master_new = master - step_rate * (
        first_hat / (jnp.sqrt(second_hat) + eps_adam) + decay * master
    )
    return (master_new, first_new, second_new)


def scatter_sum(grad):
    lanes = grad.astype(jnp.bfloat16).reshape(-1, 128)
    own = lax.psum_scatter(lanes, ("wide", "narrow"), scatter_dimension=0, tiled=True)
    return own.reshape(-1).astype(jnp.float32)


def on_device(
    samples,
    cotangent,
    visible,
    master_attn,
    first_attn,
    second_attn,
    master_mlp,
    first_mlp,
    second_mlp,
    master_small,
    first_small,
    second_small,
):
    count, length, width = samples.shape
    total_rows = count * length
    scale = 1.0 / math.sqrt(HD)
    attn_full, mlp_full, small_full = (
        lax.all_gather(master_attn.astype(jnp.bfloat16), ("wide", "narrow"), axis=0, tiled=True),
        lax.all_gather(master_mlp.astype(jnp.bfloat16), ("wide", "narrow"), axis=0, tiled=True),
        lax.all_gather(master_small.astype(jnp.bfloat16), ("wide", "narrow"), axis=0, tiled=True),
    )
    w_qkv = attn_full[: 3 * D * D].reshape(D, 3 * D)
    w_out = attn_full[3 * D * D :].reshape(D, D)
    (
        gain_one,
        bias_one,
        bias_query,
        bias_value,
        bias_out,
        gain_two,
        bias_two,
        bias_inner,
        bias_outer,
    ) = split_small(small_full.astype(jnp.float32))
    valid = jnp.arange(length)[None, :] < visible[:, None]
    key_mask = valid[:, None, None, :]
    row_mask = valid.reshape(total_rows, 1)
    rows = samples.astype(jnp.float32).reshape(total_rows, D)
    normed_one, factor_one = standard(rows)
    first_in = (normed_one * gain_one + bias_one).astype(jnp.bfloat16)
    shift = jnp.concatenate([bias_query, jnp.zeros_like(bias_query), bias_value])
    qkv = jnp.dot(first_in, w_qkv, preferred_element_type=jnp.float32) + shift
    qkv_low = qkv.astype(jnp.bfloat16).reshape(count, length, 3, H, HD)
    query = qkv_low[:, :, 0]
    keys = qkv_low[:, :, 1]
    values = qkv_low[:, :, 2]
    scores = masked_scores(query, keys, key_mask)
    top = jnp.max(scores, -1, keepdims=True)
    expo = jnp.exp(scores - top)
    totals = jnp.sum(expo, -1, keepdims=True)
    log_total = top + jnp.log(totals)
    probs_low = (expo / totals).astype(jnp.bfloat16)
    context = jnp.einsum("shqk,skhd->sqhd", probs_low, values, preferred_element_type=jnp.float32)
    context_low = context.astype(jnp.bfloat16).reshape(total_rows, D)
    middle = rows + jnp.dot(context_low, w_out, preferred_element_type=jnp.float32) + bias_out
    w_one = mlp_full[: D * FF].reshape(D, FF)
    w_two = mlp_full[D * FF :].reshape(FF, D)
    normed_two, factor_two = standard(middle)
    second_in = (normed_two * gain_two + bias_two).astype(jnp.bfloat16)
    inner = jnp.dot(second_in, w_one, preferred_element_type=jnp.float32) + bias_inner
    active = jax.nn.gelu(inner, approximate=False).astype(jnp.bfloat16)
    result = middle + jnp.dot(active, w_two, preferred_element_type=jnp.float32) + bias_outer
    output = jnp.where(row_mask, result, 0.0).reshape(count, length, D).astype(jnp.bfloat16)
    grad_result = jnp.where(row_mask, cotangent.astype(jnp.float32).reshape(total_rows, D), 0.0)
    grad_branch = grad_result.astype(jnp.bfloat16)
    grad_w_two = jnp.einsum("rf,rd->fd", active, grad_branch, preferred_element_type=jnp.float32)
    grad_bias_outer = jnp.sum(grad_branch, 0, dtype=jnp.float32)
    grad_active = jnp.einsum("rd,fd->rf", grad_branch, w_two, preferred_element_type=jnp.float32)
    slope = (
        0.5 * (1.0 + jax.scipy.special.erf(inner * inv_root_two))
        + inner * jnp.exp(-0.5 * inner * inner) * inv_root_tau
    )
    grad_inner = (grad_active * slope).astype(jnp.bfloat16)
    grad_w_one = jnp.einsum("rd,rf->df", second_in, grad_inner, preferred_element_type=jnp.float32)
    grad_bias_inner = jnp.sum(grad_inner, 0, dtype=jnp.float32)
    grad_second_in = jnp.einsum("rf,df->rd", grad_inner, w_one, preferred_element_type=jnp.float32)
    grad_gain_two, grad_bias_two, grad_middle_norm = norm_backward(
        grad_second_in, normed_two, factor_two, gain_two
    )
    grad_middle = grad_result + grad_middle_norm
    grad_mlp = jnp.concatenate([grad_w_one.reshape(-1), grad_w_two.reshape(-1)])
    grad_proj = grad_middle.astype(jnp.bfloat16)
    grad_w_out = jnp.einsum("rc,rd->cd", context_low, grad_proj, preferred_element_type=jnp.float32)
    grad_bias_out = jnp.sum(grad_proj, 0, dtype=jnp.float32)
    grad_context = jnp.einsum("rd,cd->rc", grad_proj, w_out, preferred_element_type=jnp.float32)
    grad_context = grad_context.astype(jnp.bfloat16).reshape(count, length, H, HD)
    probs = jnp.exp(masked_scores(query, keys, key_mask) - log_total)
    probs_again = probs.astype(jnp.bfloat16)
    grad_values = jnp.einsum(
        "shqk,sqhd->skhd", probs_again, grad_context, preferred_element_type=jnp.float32
    )
    grad_probs = jnp.einsum(
        "sqhd,skhd->shqk", grad_context, values, preferred_element_type=jnp.float32
    )
    inner_sum = jnp.sum(grad_probs * probs, -1, keepdims=True)
    grad_scores = (probs * (grad_probs - inner_sum)).astype(jnp.bfloat16)
    grad_query = (
        jnp.einsum("shqk,skhd->sqhd", grad_scores, keys, preferred_element_type=jnp.float32) * scale
    )
    grad_keys = (
        jnp.einsum("shqk,sqhd->skhd", grad_scores, query, preferred_element_type=jnp.float32)
        * scale
    )
    grad_qkv = (
        jnp.stack([grad_query, grad_keys, grad_values], 2)
        .reshape(total_rows, 3 * D)
        .astype(jnp.bfloat16)
    )
    grad_w_qkv = jnp.einsum("rd,re->de", first_in, grad_qkv, preferred_element_type=jnp.float32)
    grad_bias_qkv = jnp.sum(grad_qkv, 0, dtype=jnp.float32)
    grad_first_in = jnp.einsum("re,de->rd", grad_qkv, w_qkv, preferred_element_type=jnp.float32)
    grad_gain_one, grad_bias_one, grad_rows_norm = norm_backward(
        grad_first_in, normed_one, factor_one, gain_one
    )
    grad_rows = grad_middle + grad_rows_norm
    grad_samples = grad_rows.reshape(count, length, D).astype(jnp.bfloat16)
    grad_attn = jnp.concatenate([grad_w_qkv.reshape(-1), grad_w_out.reshape(-1)])
    grad_small = jnp.concatenate(
        [
            grad_gain_one,
            grad_bias_one,
            grad_bias_qkv[:D],
            grad_bias_qkv[2 * D :],
            grad_bias_out,
            grad_gain_two,
            grad_bias_two,
            grad_bias_inner,
            grad_bias_outer,
        ]
    )
    summed_attn, summed_mlp, summed_small = (
        scatter_sum(grad_attn),
        scatter_sum(grad_mlp),
        lax.psum_scatter(grad_small, ("wide", "narrow"), scatter_dimension=0, tiled=True),
    )
    new_attn, new_first_attn, new_second_attn = adamw(
        master_attn, first_attn, second_attn, summed_attn, 0.1, rate_matrix
    )
    new_mlp, new_first_mlp, new_second_mlp = adamw(
        master_mlp, first_mlp, second_mlp, summed_mlp, 0.1, rate_matrix
    )
    new_small, new_first_small, new_second_small = adamw(
        master_small, first_small, second_small, summed_small, 0.0, rate_small
    )
    return (
        output,
        grad_samples,
        new_attn,
        new_first_attn,
        new_second_attn,
        new_mlp,
        new_first_mlp,
        new_second_mlp,
        new_small,
        new_first_small,
        new_second_small,
    )


bf16 = jnp.bfloat16
f32 = jnp.float32
BLOCK = 256
BIN = 128
AXES = ("wide", "narrow")
ROW = 128
SMALL_ROWS = 72


def place_of(i):
    wide, z = divmod(i, 4)
    return wide // 4, (wide // 2) % 2, wide % 2, z


def index_of(y, x, c, z):
    return ((y * 2 + x) * 2 + c) * 4 + z


def pairs_of(move):
    return [(i, index_of(*move(*place_of(i)))) for i in range(32)]


TO_X = pairs_of(lambda y, x, c, z: (y, 1 - x, c, z))
TO_Y = pairs_of(lambda y, x, c, z: (1 - y, x, c, z))
TO_CORE = pairs_of(lambda y, x, c, z: (y, x, 1 - c, z))
TO_Z = [pairs_of(lambda y, x, c, z, k=k: (y, x, c, z ^ k)) for k in range(4)]
SWAP_ATTN = pairs_of(lambda y, x, c, z: (y, x, c if y and x else 1 - c, z))
SWAP_MLP = pairs_of(lambda y, x, c, z: (y, x, c if y else 1 - c, z))


def send(value, pairs):
    return lax.ppermute(value, AXES, pairs)


def dot(a, b, dims=((1,), (0,))):
    return lax.dot_general(a, b, (dims, ((), ())), preferred_element_type=f32)


def at_rows(ref, start, size):
    return ref[pl.ds(start, size), :]


def attn_block(core, j):
    return (j // 3) * 6 + 3 * core + j % 3


def mlp_block(core, j):
    return (j // 6) * 12 + 6 * core + j % 6


def cut_masters(idx, attn, mlp, keep_a, send_a, keep_m, send_m, half_a, half_m):
    wide, core = idx[0], idx[3]

    @pl.when(wide < 6)
    def _():
        for c in range(2):
            for j in range(9):
                rows = attn[pl.ds(attn_block(c, j), 32, stride=18), :]
                half_a[c, j * 32 : (j + 1) * 32, :] = rows.astype(bf16)

    @pl.when(wide >= 6)
    def _():
        for j in range(6):
            rows = attn[pl.ds(j, 96, stride=6), :]
            half_a[j // 3, (j % 3) * 96 : (j % 3 + 1) * 96, :] = rows.astype(bf16)

    @pl.when(wide < 4)
    def _():
        for c in range(2):
            for j in range(12):
                rows = mlp[pl.ds(mlp_block(c, j), 48, stride=24), :]
                half_m[c, j * 48 : (j + 1) * 48, :] = rows.astype(bf16)

    @pl.when(wide >= 4)
    def _():
        for j in range(6):
            rows = mlp[pl.ds(j, 192, stride=6), :]
            half_m[j // 3, (j % 3) * 192 : (j % 3 + 1) * 192, :] = rows.astype(bf16)

    first_a = jnp.where(wide < 6, core, 0)
    first_m = jnp.where(wide < 4, core, 0)
    keep_a[...] = half_a[first_a]
    send_a[...] = half_a[1 - first_a]
    keep_m[...] = half_m[first_m]
    send_m[...] = half_m[1 - first_m]


def pack_rows(idx, vis_own, vis_other, x_own, x_other, cot_own, cot_other, x_out, cot_out, meta, fill):
    core = idx[3]
    for b in range(16):
        fill[b] = 0
    bins = jnp.int32(0)
    for s in range(16):
        mine = core == s // 8
        seen = jnp.where(mine, vis_own[s % 8], vis_other[s % 8])
        need = ((seen + 15) >> 4) << 4
        chosen = jnp.int32(15)
        for b in reversed(range(s + 1)):
            chosen = jnp.where(fill[b] + need <= BIN, b, chosen)
        start = chosen * BIN + fill[chosen]
        fill[chosen] = fill[chosen] + need
        bins = jnp.maximum(bins, chosen + 1)
        meta[8 + s] = start
        meta[24 + s] = seen
    blocks = (bins + 1) >> 1
    meta[0] = blocks

    def clear(b, carry):
        at = pl.ds(pl.multiple_of(b * BLOCK, BLOCK), BLOCK)
        x_out[at, :] = jnp.zeros((BLOCK, D), bf16)
        cot_out[at, :] = jnp.zeros((BLOCK, D), bf16)
        return carry

    lax.fori_loop(0, blocks, clear, 0)
    row = lax.broadcasted_iota(jnp.int32, (16, D), 0)
    for s in range(16):
        start, seen = meta[8 + s], meta[24 + s]

        def fetch(x_in, cot_in):
            def chunk(k, carry):
                src = pl.ds(pl.multiple_of(k * 16, 16), 16)
                dst = pl.ds(pl.multiple_of(start + k * 16, 16), 16)
                x_out[dst, :] = x_in[s % 8, src, :]
                grad = cot_in[s % 8, src, :].astype(f32)
                cot_out[dst, :] = jnp.where(row + k * 16 < seen, grad, 0.0).astype(bf16)
                return carry

            lax.fori_loop(0, (seen + 15) >> 4, chunk, 0)

        @pl.when(core == s // 8)
        def _():
            fetch(x_own, cot_own)

        @pl.when(core != s // 8)
        def _():
            fetch(x_other, cot_other)


def owner_of(idx, column, k):
    y, x, z = idx[1], idx[2], idx[4]
    yy = 1 - y if column >= 2 else y
    xx = 1 - x if column % 2 else x
    return yy * 2 + xx, jnp.bitwise_xor(z, k)


def core_of(idx, part):
    return 1 - idx[3] if part else idx[3]


def lanes_of(small, first, count):
    rows = [small[q // 9, q % 9 : q % 9 + 1, :] for q in range(first, first + count)]
    return jnp.concatenate(rows, axis=1)


def same_sample(meta, which):
    lane = lax.broadcasted_iota(jnp.int32, (8, BIN), 1)
    line = lax.broadcasted_iota(jnp.int32, (BIN, BIN), 0)
    of_key = jnp.full((8, BIN), -2, jnp.int32)
    of_query = jnp.full((BIN, BIN), -1, jnp.int32)
    for s in range(16):
        start = meta[8 + s] - which * BIN
        stop = start + meta[24 + s]
        of_key = jnp.where((lane >= start) & (lane < stop), s, of_key)
        of_query = jnp.where((line >= start) & (line < stop), s, of_query)
    return of_query == of_key[0:1, :]


def halves(pair):
    lane = lax.broadcasted_iota(jnp.int32, pair.shape, 1)
    wide = pair.astype(f32)
    return jnp.concatenate(
        [jnp.where(lane < HD, wide, 0.0), jnp.where(lane >= HD, wide, 0.0)], axis=0
    ).astype(bf16)


def probabilities(query, keys, mask):
    scores = dot(halves(query), keys, ((1,), (1,))) * (1.0 / math.sqrt(HD))
    scores = jnp.where(mask, scores, -1e30)
    expo = jnp.exp(scores - jnp.max(scores, -1, keepdims=True))
    return expo * (1.0 / jnp.sum(expo, -1, keepdims=True))


def side_by_side(stacked):
    return jnp.concatenate([stacked[:BIN], stacked[BIN:]], axis=1)


def attn_forward(meta, idx, x_ref, *refs):
    pieces = refs[:16]
    qkv_ref, context_ref, part_ref, w_qkv, w_out, vecs, shift, inner_bias, small = refs[16:]

    @pl.when(pl.program_id(0) == 0)
    def _():
        small[...] = jnp.zeros(small.shape, f32)
        for n, piece in enumerate(pieces):
            chip, z = owner_of(idx, n // 4, n % 4)

            @pl.when(chip < 3)
            def _():
                for part in range(2):
                    owner = (chip * 2 + core_of(idx, part)) * 4 + z
                    to = pl.ds(pl.multiple_of(owner * 32, 32), 32)
                    for j in range(9):
                        at = part * 288 + j * 32
                        w_qkv[to, j * ROW : (j + 1) * ROW] = piece[at : at + 32, :]

            @pl.when(chip == 3)
            def _():
                to = pl.ds(pl.multiple_of(z * 96, 32), 96)
                for j in range(6):
                    w_out[to, j * ROW : (j + 1) * ROW] = piece[j * 96 : (j + 1) * 96, :]

            for part in range(2):
                group = chip * 2 + core_of(idx, part)
                at = 576 + part * 16
                small[group] = small[group] + piece[at : at + 16, :].astype(f32)
        for n, first in enumerate((0, 6, 24, 30, 36, 66)):
            vecs[n : n + 1, :] = lanes_of(small, first, 6)
        vecs[6:8, :] = jnp.zeros((2, D), f32)
        own = idx[3] == 0
        query_bias = jnp.where(own, lanes_of(small, 12, 3), lanes_of(small, 15, 3))
        value_bias = jnp.where(own, lanes_of(small, 18, 3), lanes_of(small, 21, 3))
        shift[...] = jnp.concatenate([query_bias, jnp.zeros((1, D // 2), f32), value_bias], axis=1)
        low = jnp.where(own, lanes_of(small, 42, 6), lanes_of(small, 48, 6))
        high = jnp.where(own, lanes_of(small, 54, 6), lanes_of(small, 60, 6))
        inner_bias[...] = jnp.concatenate([low, high], axis=1)

    @pl.when(pl.program_id(0) < meta[0])
    def _():
        normed, _ = standard(x_ref[...].astype(f32))
        first_in = (normed * vecs[0:1, :] + vecs[1:2, :]).astype(bf16)
        qkv_ref[...] = (dot(first_in, w_qkv[...]) + shift[...]).astype(bf16)
        for b in range(BLOCK // BIN):
            mask = same_sample(meta, pl.program_id(0) * (BLOCK // BIN) + b)
            mask = jnp.concatenate([mask, mask], axis=0)
            rows = slice(b * BIN, (b + 1) * BIN)
            for h in range(3):
                query, keys, values = (
                    qkv_ref[rows, (3 * t + h) * ROW : (3 * t + h + 1) * ROW] for t in range(3)
                )
                probs = probabilities(query, keys, mask).astype(bf16)
                context = dot(side_by_side(probs), halves(values))
                context_ref[rows, h * ROW : (h + 1) * ROW] = context.astype(bf16)
        part_ref[...] = dot(context_ref[...], w_out[...]).astype(bf16)


ERF_TOP = (0.00022905065861350646, 0.0034082910107109506, 0.050955695062380861, 0.18520832239976145, 1.128379143519084)
ERF_BOTTOM = (-1.1791602954361697e-7, 0.000023547966471313185, 0.0010179625278914885, 0.014070470171167667,
              0.11098505178285362, 0.49746925110067538, 1.0)


def error_function(v):
    v = jnp.clip(v, -3.832506856900711, 3.832506856900711)
    square = v * v
    top, bottom = jnp.full_like(v, ERF_TOP[0]), jnp.full_like(v, ERF_BOTTOM[0])
    for a in ERF_TOP[1:]:
        top = top * square + a
    for b in ERF_BOTTOM[1:]:
        bottom = bottom * square + b
    return v * top / bottom


def middle_of(x_ref, part_own, part_other, vecs):
    parts = part_own[...].astype(f32) + part_other[...].astype(f32)
    return x_ref[...].astype(f32) + parts + vecs[2:3, :]


def mlp_both(meta, idx, x_ref, part_own, part_other, cot_ref, vecs, inner_bias, *refs):
    pieces = refs[:16]
    (active_ref, back_ref, w_two, sums, inner_sum) = refs[16:21]
    outs = refs[21:29]
    w_one, acc_one, acc_two = refs[29:]
    step = pl.program_id(0)

    @pl.when(step == 0)
    def _():
        acc_one[...] = jnp.zeros(acc_one.shape, f32)
        acc_two[...] = jnp.zeros(acc_two.shape, f32)
        sums[...] = jnp.zeros(sums.shape, f32)
        inner_sum[...] = jnp.zeros(inner_sum.shape, f32)
        for n, piece in enumerate(pieces):
            chip, z = owner_of(idx, n // 4, n % 4)

            @pl.when(chip < 2)
            def _():
                for part in range(2):
                    owner = (chip * 2 + core_of(idx, part)) * 4 + z
                    to = pl.ds(pl.multiple_of(owner * 48, 16), 48)
                    for j in range(12):
                        at = part * 576 + j * 48
                        w_one[to, j * ROW : (j + 1) * ROW] = piece[at : at + 48, :]

            @pl.when(chip >= 2)
            def _():
                to = pl.ds(pl.multiple_of((chip - 2) * D + z * 192, 64), 192)
                for j in range(6):
                    w_two[to, j * ROW : (j + 1) * ROW] = piece[j * 192 : (j + 1) * 192, :]

    @pl.when(pl.program_id(0) < meta[0])
    def _():
        normed, _ = standard(middle_of(x_ref, part_own, part_other, vecs))
        second_in = (normed * vecs[3:4, :] + vecs[4:5, :]).astype(bf16)
        grad = cot_ref[...]
        back = jnp.zeros((BLOCK, D), f32)
        for n in range(2):
            cols = slice(n * D, (n + 1) * D)
            inner = dot(second_in, w_one[:, cols]) + inner_bias[:, cols]
            bell = 0.5 * (1.0 + error_function(inner * inv_root_two))
            active = (inner * bell).astype(bf16)
            active_ref[:, cols] = active
            slope = bell + inner * jnp.exp(-0.5 * inner * inner) * inv_root_tau
            grad_inner = (dot(grad, w_two[cols, :], ((1,), (1,))) * slope).astype(bf16)
            acc_two[cols, :] += dot(active, grad, ((0,), (0,)))
            acc_one[:, cols] += dot(second_in, grad_inner, ((0,), (0,)))
            inner_sum[:, cols] += jnp.sum(grad_inner.astype(f32), 0, keepdims=True)
            back = back + dot(grad_inner, w_one[:, cols], ((1,), (1,)))
        back_ref[...] = back.astype(bf16)
        sums[0:1, :] += jnp.sum(back * normed, 0, keepdims=True)
        sums[1:2, :] += jnp.sum(back, 0, keepdims=True)
        sums[2:3, :] += jnp.sum(grad.astype(f32), 0, keepdims=True)

    @pl.when(step == pl.num_programs(0) - 1)
    def _():
        for n in range(16):
            chip, z = owner_of(idx, n // 4, n % 4)
            out, k = outs[n // 2], n % 2

            @pl.when(chip < 2)
            def _():
                for part in range(2):
                    owner = (chip * 2 + core_of(idx, part)) * 4 + z
                    rows = pl.ds(pl.multiple_of(owner * 48, 16), 48)
                    for j in range(12):
                        at = part * 576 + j * 48
                        out[k, at : at + 48, :] = acc_one[rows, j * ROW : (j + 1) * ROW].astype(bf16)

            @pl.when(chip >= 2)
            def _():
                rows = pl.ds(pl.multiple_of((chip - 2) * D + z * 192, 64), 192)
                for j in range(6):
                    out[k, j * 192 : (j + 1) * 192, :] = acc_two[rows, j * ROW : (j + 1) * ROW].astype(bf16)


def mlp_out(meta, active_ref, w_two, part_ref):
    @pl.when(pl.program_id(0) < meta[0])
    def _():
        part_ref[...] = dot(active_ref[...], w_two[...]).astype(bf16)


def attn_backward(meta, idx, x_ref, part_own, part_other, cot_ref, back_own, back_other, qkv_ref, context_ref,
                  w_qkv, w_out, vecs, sums_in, inner_sum, *refs):
    grad_ref, back_ref = refs[:2]
    outs = refs[2:10]
    acc_qkv, acc_out, sums, small, grads = refs[10:]
    step = pl.program_id(0)

    @pl.when(step == 0)
    def _():
        acc_qkv[...] = jnp.zeros(acc_qkv.shape, f32)
        acc_out[...] = jnp.zeros(acc_out.shape, f32)
        sums[...] = jnp.zeros(sums.shape, f32)

    @pl.when(pl.program_id(0) < meta[0])
    def _():
        normed, factor = standard(middle_of(x_ref, part_own, part_other, vecs))
        scaled = (back_own[...].astype(f32) + back_other[...].astype(f32)) * vecs[3:4, :]
        through = scaled - jnp.mean(scaled, -1, keepdims=True)
        through = through - normed * jnp.mean(scaled * normed, -1, keepdims=True)
        grad_middle = cot_ref[...].astype(f32) + factor * through
        grad_ref[...] = grad_middle
        grad_proj = grad_middle.astype(bf16)
        context = context_ref[...]
        acc_out[...] += dot(context, grad_proj, ((0,), (0,)))
        sums[2:3, :] += jnp.sum(grad_proj.astype(f32), 0, keepdims=True)
        grad_context = dot(grad_proj, w_out[...], ((1,), (1,))).astype(bf16)
        scale = 1.0 / math.sqrt(HD)
        for b in range(BLOCK // BIN):
            mask = same_sample(meta, step * (BLOCK // BIN) + b)
            mask = jnp.concatenate([mask, mask], axis=0)
            rows = slice(b * BIN, (b + 1) * BIN)
            for h in range(3):
                cols = [slice((3 * t + h) * ROW, (3 * t + h + 1) * ROW) for t in range(3)]
                query, keys, values = (qkv_ref[rows, cols[t]] for t in range(3))
                probs = probabilities(query, keys, mask)
                grad_out = halves(grad_context[rows, h * ROW : (h + 1) * ROW])
                grad_values = dot(probs.astype(bf16), grad_out, ((0,), (0,)))
                grad_probs = dot(grad_out, values, ((1,), (1,)))
                total = jnp.sum(grad_probs * probs, -1, keepdims=True)
                grad_scores = (probs * (grad_probs - total)).astype(bf16)
                grad_query = dot(side_by_side(grad_scores), halves(keys)) * scale
                grad_keys = dot(grad_scores, halves(query), ((0,), (0,))) * scale
                grads[rows, cols[0]] = grad_query.astype(bf16)
                grads[rows, cols[1]] = grad_keys.astype(bf16)
                grads[rows, cols[2]] = grad_values.astype(bf16)
        normed, _ = standard(x_ref[...].astype(f32))
        first_in = (normed * vecs[0:1, :] + vecs[1:2, :]).astype(bf16)
        grad_qkv = grads[...]
        acc_qkv[...] += dot(first_in, grad_qkv, ((0,), (0,)))
        back = dot(grad_qkv, w_qkv[...], ((1,), (1,)))
        back_ref[...] = back.astype(bf16)
        sums[0:1, :] += jnp.sum(back * normed, 0, keepdims=True)
        sums[1:2, :] += jnp.sum(back, 0, keepdims=True)
        sums[3:4, 0 : D // 2] += jnp.sum(grad_qkv[:, 0 : D // 2].astype(f32), 0, keepdims=True)
        sums[3:4, D // 2 : D] += jnp.sum(grad_qkv[:, D : D + D // 2].astype(f32), 0, keepdims=True)

    @pl.when(step == pl.num_programs(0) - 1)
    def _():
        small[...] = jnp.zeros(small.shape, f32)
        first = idx[3] == 0
        once = jnp.where(first, 1.0, 0.0)

        def put(at, rows):
            for j in range(rows.shape[1] // ROW):
                q = at + j
                small[q // 9, q % 9 : q % 9 + 1, :] = rows[:, j * ROW : (j + 1) * ROW]

        put(0, sums[0:1, :])
        put(6, sums[1:2, :])
        put(24, sums[2:3, :] * once)
        put(30, sums_in[0:1, :])
        put(36, sums_in[1:2, :])
        put(66, sums_in[2:3, :] * once)
        for c in range(2):

            @pl.when(idx[3] == c)
            def _():
                put(12 + 3 * c, sums[3:4, 0 : D // 2])
                put(18 + 3 * c, sums[3:4, D // 2 : D])
                put(42 + 6 * c, inner_sum[:, 0:D])
                put(54 + 6 * c, inner_sum[:, D : 2 * D])

        for n in range(16):
            chip, z = owner_of(idx, n // 4, n % 4)
            out, k = outs[n // 2], n % 2

            @pl.when(chip < 3)
            def _():
                for part in range(2):
                    owner = (chip * 2 + core_of(idx, part)) * 4 + z
                    rows = pl.ds(pl.multiple_of(owner * 32, 32), 32)
                    for j in range(9):
                        at = part * 288 + j * 32
                        out[k, at : at + 32, :] = acc_qkv[rows, j * ROW : (j + 1) * ROW].astype(bf16)

            @pl.when(chip == 3)
            def _():
                rows = pl.ds(pl.multiple_of(z * 96, 32), 96)
                for j in range(6):
                    out[k, j * 96 : (j + 1) * 96, :] = acc_out[rows, j * ROW : (j + 1) * ROW].astype(bf16)

            for part in range(2):
                group = chip * 2 + core_of(idx, part)
                out[k, 576 + part * 16 : 592 + part * 16, :] = small[group].astype(bf16)


def finish_rows(meta, idx, x_ref, part_own, part_other, out_own, out_other, grad_ref, back_own, back_other, vecs,
                output, grad_samples, packed_out, packed_grad):
    step = pl.program_id(0)
    @pl.when(pl.program_id(0) < meta[0])
    def _():
        at = pl.ds(pl.multiple_of(step * BLOCK, BLOCK), BLOCK)
        parts = out_own[...].astype(f32) + out_other[...].astype(f32)
        result = middle_of(x_ref, part_own, part_other, vecs) + parts + vecs[5:6, :]
        packed_out[at, :] = result.astype(bf16)
        normed, factor = standard(x_ref[...].astype(f32))
        scaled = (back_own[...].astype(f32) + back_other[...].astype(f32)) * vecs[0:1, :]
        through = scaled - jnp.mean(scaled, -1, keepdims=True)
        through = through - normed * jnp.mean(scaled * normed, -1, keepdims=True)
        packed_grad[at, :] = (grad_ref[...] + factor * through).astype(bf16)

    @pl.when(step == pl.num_programs(0) - 1)
    def _():
        output[...] = jnp.zeros(output.shape, bf16)
        grad_samples[...] = jnp.zeros(grad_samples.shape, bf16)
        row = lax.broadcasted_iota(jnp.int32, (16, D), 0)
        for s in range(8):
            start, seen = meta[8 + idx[3] * 8 + s], meta[24 + idx[3] * 8 + s]

            def chunk(k, carry):
                src = pl.ds(pl.multiple_of(start + k * 16, 16), 16)
                dst = pl.ds(pl.multiple_of(k * 16, 16), 16)
                keep = row + k * 16 < seen
                for packed, out in ((packed_out, output), (packed_grad, grad_samples)):
                    out[s, dst, :] = jnp.where(keep, packed[src, :].astype(f32), 0.0).astype(bf16)
                return carry

            lax.fori_loop(0, (seen + 15) >> 4, chunk, 0)


def update_refs(master, first, second, grad, outs, decay, step_rate):
    for out, new in zip(outs, adamw(master[...], first[...], second[...], grad, decay, step_rate)):
        out[...] = new


def step_mlp(idx, master, first, second, keep, other, new, new_first, new_second, half, grad):
    wide, core = idx[0], idx[3]
    mine = jnp.where(wide < 4, core, 0)
    half[mine] = keep[...]
    half[1 - mine] = other[...]

    @pl.when(wide < 4)
    def _():
        for c in range(2):
            for j in range(12):
                grad[pl.ds(mlp_block(c, j), 48, stride=24), :] = half[c, j * 48 : (j + 1) * 48, :]

    @pl.when(wide >= 4)
    def _():
        for j in range(6):
            grad[pl.ds(j, 192, stride=6), :] = half[j // 3, (j % 3) * 192 : (j % 3 + 1) * 192, :]

    update_refs(master, first, second, grad[...], (new, new_first, new_second), 0.1, rate_matrix)


def step_attn(idx, master, first, second, keep, other, master_s, first_s, second_s, keep_s, other_s,
              new, new_first, new_second, new_s, new_first_s, new_second_s, half, grad):
    wide, core = idx[0], idx[3]
    mine = jnp.where(wide < 6, core, 0)
    half[mine] = keep[...]
    half[1 - mine] = other[...]

    @pl.when(wide < 6)
    def _():
        for c in range(2):
            for j in range(9):
                grad[pl.ds(attn_block(c, j), 32, stride=18), :] = half[c, j * 32 : (j + 1) * 32, :]

    @pl.when(wide >= 6)
    def _():
        for j in range(6):
            grad[pl.ds(j, 96, stride=6), :] = half[j // 3, (j % 3) * 96 : (j % 3 + 1) * 96, :]

    update_refs(master, first, second, grad[...], (new, new_first, new_second), 0.1, rate_matrix)
    update_refs(master_s, first_s, second_s, keep_s[...] + other_s[...], (new_s, new_first_s, new_second_s), 0.0, rate_small)


def gather_chips(piece):
    by = {(0, 0): piece}
    by[1, 0] = send(piece, TO_X)
    by[2, 0] = send(piece, TO_Y)
    by[0, 1] = send(piece, TO_Z[1])
    by[3, 0] = send(by[2, 0], TO_X)
    by[0, 2] = send(piece, TO_Z[2])
    by[0, 3] = send(piece, TO_Z[3])
    for k in (1, 2, 3):
        by[1, k] = send(by[0, k], TO_X)
        by[2, k] = send(by[0, k], TO_Y)
        by[3, k] = send(by[1, k], TO_Y) if k % 2 else send(by[2, k], TO_X)
    return [by[column, k] for column in range(4) for k in range(4)]


def plus(*terms):
    return sum(t.astype(f32) for t in terms)


def scatter_chips(own_low, own_high, x_low, x_high, y_low, y_high, both_low, both_high):
    from_x = send(both_low, TO_X)
    from_y = send(both_high, TO_Y)
    x_low_in = send(x_low, TO_X)
    y_high_in = send(y_high, TO_Y)
    y_low_in = send(plus(y_low, from_x).astype(bf16), TO_Y)
    x_high_in = send(plus(x_high, from_y).astype(bf16), TO_X)
    low = plus(own_low, x_low_in, y_low_in)
    high = plus(own_high, x_high_in, y_high_in)
    others = [send(t.astype(bf16), TO_Z[k]) for k, t in ((1, low[1]), (2, high[0]), (3, high[1]))]
    return plus(low[0], *others)


SMEM = pl.BlockSpec(memory_space=pltpu.SMEM)


def whole(shape):
    return pl.BlockSpec(shape, lambda i, *_: (0,) * len(shape))


def once_in(shape):
    return pl.BlockSpec(shape, lambda i, *_: (0,) * len(shape), pipeline_mode=pl.Buffered(1))


def rows_spec(width):
    return pl.BlockSpec((BLOCK, width), lambda i, meta, *_: (jnp.minimum(i, meta[0] - 1), 0))


def array(shape, dtype=bf16):
    return jax.ShapeDtypeStruct(shape, dtype)


def params(mib):
    return pltpu.CompilerParams(vmem_limit_bytes=mib << 20)


def cost(flops, nbytes):
    return pl.CostEstimate(flops=flops, bytes_accessed=nbytes, transcendentals=0)


def over_blocks(body, steps, scalars, in_specs, out_specs, out_shape, scratch, mib, flops, nbytes, name):
    return pl.pallas_call(
        body,
        grid_spec=pltpu.PrefetchScalarGridSpec(
            num_scalar_prefetch=scalars, grid=(steps,), in_specs=in_specs, out_specs=out_specs, scratch_shapes=scratch
        ),
        out_shape=out_shape,
        compiler_params=params(mib),
        cost_estimate=cost(flops, nbytes),
        name=name,
    )


def at_once(body, in_specs, out_specs, out_shape, scratch, mib, flops, nbytes, name):
    return pl.pallas_call(
        body,
        in_specs=in_specs,
        out_specs=out_specs,
        out_shape=out_shape,
        scratch_shapes=scratch,
        compiler_params=params(mib),
        cost_estimate=cost(flops, nbytes),
        name=name,
    )


VMEM = pl.BlockSpec(memory_space=pltpu.VMEM)


def on_core(
    samples,
    cotangent,
    visible,
    master_attn,
    first_attn,
    second_attn,
    master_mlp,
    first_mlp,
    second_mlp,
    master_small,
    first_small,
    second_small,
):
    count, length, _ = samples.shape
    rows = 2 * count * length
    wide, z = lax.axis_index("wide"), lax.axis_index("narrow")
    idx = jnp.stack([wide, wide // 4, (wide // 2) % 2, wide % 2, z]).astype(jnp.int32)

    def lanes(flat):
        return flat.reshape(-1, ROW)

    def spread(vector):
        return lanes(lax.dynamic_update_slice(jnp.zeros((16 * ROW,), f32), vector, (z * 288,)))

    small_low = spread(master_small).astype(bf16)
    half_a, half_m = (288, ROW), (576, ROW)
    keep_a, send_a, keep_m, send_m = at_once(
        cut_masters, [SMEM, VMEM, VMEM], [VMEM] * 4,
        [array(half_a), array(half_a), array(half_m), array(half_m)],
        [pltpu.VMEM((2, *half_a), bf16), pltpu.VMEM((2, *half_m), bf16)], 16, 10**9, 2 * 10**6, "cut_masters",
    )(idx, lanes(master_attn), lanes(master_mlp))
    piece_a = jnp.concatenate([keep_a, send(send_a, SWAP_ATTN), small_low, send(small_low, TO_CORE)])
    pieces_a = gather_chips(piece_a)
    piece_m = jnp.concatenate([keep_m, send(send_m, SWAP_MLP)])
    pieces_m = gather_chips(piece_m)

    x, cot, meta = at_once(
        pack_rows, [SMEM, SMEM, SMEM] + [VMEM] * 4, [VMEM, VMEM, SMEM],
        [array((rows, D)), array((rows, D)), array((64,), jnp.int32)],
        [pltpu.SMEM((16,), jnp.int32)], 32, 10**9, 12 * 10**6, "pack_rows",
    )(idx, visible, send(visible, TO_CORE), samples, send(samples, TO_CORE), cotangent, send(cotangent, TO_CORE))
    steps = rows // BLOCK

    row_d, row_half, row_qkv, row_inner = rows_spec(D), rows_spec(D // 2), rows_spec(3 * D // 2), rows_spec(FF // 2)
    qkv, context, part, w_qkv, w_out, vecs, shift, inner_bias = over_blocks(
        attn_forward, steps, 2, [row_d] + [once_in((608, ROW))] * 16,
        [row_qkv, row_half, row_d, whole((D, 3 * D // 2)), whole((D // 2, D)), whole((8, D)), whole((1, 3 * D // 2)), whole((1, FF // 2))],
        [array((rows, 3 * D // 2)), array((rows, D // 2)), array((rows, D)), array((D, 3 * D // 2)), array((D // 2, D)),
         array((8, D), f32), array((1, 3 * D // 2), f32), array((1, FF // 2), f32)],
        [pltpu.VMEM((8, 16, ROW), f32)], 32, 5 * 10**9, 10**7, "attn_forward",
    )(meta, idx, x, *pieces_a)
    part_other = send(part, TO_CORE)

    pair_m = (2, 1152, ROW)
    mlp = over_blocks(
        mlp_both, steps, 2, [row_d] * 4 + [once_in((8, D)), once_in((1, FF // 2))] + [once_in((1152, ROW))] * 16,
        [row_inner, row_d, whole((FF // 2, D)), whole((8, D)), whole((1, FF // 2))] + [whole(pair_m)] * 8,
        [array((rows, FF // 2)), array((rows, D)), array((FF // 2, D)), array((8, D), f32), array((1, FF // 2), f32)] + [array(pair_m)] * 8,
        [pltpu.VMEM((D, FF // 2), bf16), pltpu.VMEM((D, FF // 2), f32), pltpu.VMEM((FF // 2, D), f32)],
        56, 10**10, 2 * 10**7, "mlp_both",
    )(meta, idx, x, part, part_other, cot, vecs, inner_bias, *pieces_m)
    active, back, w_two, sums, inner_sum = mlp[:5]
    back_other = send(back, TO_CORE)
    summed_m = scatter_chips(*mlp[5:])

    out_part = over_blocks(
        mlp_out, steps, 1, [row_inner, once_in((FF // 2, D))], row_d, array((rows, D)), [], 16, 10**9, 10**7, "mlp_out",
    )(meta, active, w_two)
    out_other = send(out_part, TO_CORE)

    pair_a = (2, 608, ROW)
    attn = over_blocks(
        attn_backward, steps, 2,
        [row_d] * 6 + [row_qkv, row_half, once_in((D, 3 * D // 2)), once_in((D // 2, D)), once_in((8, D)), once_in((8, D)), once_in((1, FF // 2))],
        [row_d, row_d] + [whole(pair_a)] * 8,
        [array((rows, D), f32), array((rows, D))] + [array(pair_a)] * 8,
        [pltpu.VMEM((D, 3 * D // 2), f32), pltpu.VMEM((D // 2, D), f32), pltpu.VMEM((8, D), f32), pltpu.VMEM((8, 16, ROW), f32),
         pltpu.VMEM((BLOCK, 3 * D // 2), bf16)],
        40, 8 * 10**9, 10**7, "attn_backward",
    )(meta, idx, x, part, part_other, cot, back, back_other, qkv, context, w_qkv, w_out, vecs, sums, inner_sum)
    grad_middle, first_back = attn[:2]
    first_other = send(first_back, TO_CORE)
    summed_a = scatter_chips(*attn[2:])

    output, grad_samples = over_blocks(
        finish_rows, steps, 2, [row_d] * 8 + [once_in((8, D))],
        [whole((count, length, D))] * 2, [array((count, length, D))] * 2,
        [pltpu.VMEM((rows, D), bf16)] * 2, 32, 10**9, 10**7, "finish_rows",
    )(meta, idx, x, part, part_other, out_part, out_other, grad_middle, first_back, first_other, vecs)

    shape_m, shape_a, shape_s = (1152, ROW), (576, ROW), (16, ROW)
    new_mlp = at_once(
        step_mlp, [SMEM] + [VMEM] * 5, [VMEM] * 3, [array(shape_m, f32)] * 3,
        [pltpu.VMEM((2, *half_m), f32), pltpu.VMEM(shape_m, f32)], 16, 10**9, 4 * 10**6, "step_mlp",
    )(idx, lanes(master_mlp), lanes(first_mlp), lanes(second_mlp), summed_m[:576], send(summed_m[576:], SWAP_MLP))
    new_attn = at_once(
        step_attn, [SMEM] + [VMEM] * 10, [VMEM] * 6, [array(shape_a, f32)] * 3 + [array(shape_s, f32)] * 3,
        [pltpu.VMEM((2, *half_a), f32), pltpu.VMEM(shape_a, f32)], 16, 10**9, 2 * 10**6, "step_attn",
    )(idx, lanes(master_attn), lanes(first_attn), lanes(second_attn), summed_a[:288], send(summed_a[288:576], SWAP_ATTN),
      spread(master_small), spread(first_small), spread(second_small), summed_a[576:592], send(summed_a[592:], TO_CORE))
    new_small = [lax.dynamic_slice(v.reshape(-1), (z * 288,), (288,)) for v in new_attn[3:]]
    return (output, grad_samples, *(v.reshape(-1) for v in new_attn[:3]), *(v.reshape(-1) for v in new_mlp), *new_small)


def solution(mesh):
    in_specs = (
        P(("wide", "narrow"), None, None),
        P(("wide", "narrow"), None, None),
        P(("wide", "narrow")),
        P(("wide", "narrow")),
        P(("wide", "narrow")),
        P(("wide", "narrow")),
        P(("wide", "narrow")),
        P(("wide", "narrow")),
        P(("wide", "narrow")),
        P(("wide", "narrow")),
        P(("wide", "narrow")),
        P(("wide", "narrow")),
    )
    out_specs = (
        P(("wide", "narrow"), None, None),
        P(("wide", "narrow"), None, None),
        P(("wide", "narrow")),
        P(("wide", "narrow")),
        P(("wide", "narrow")),
        P(("wide", "narrow")),
        P(("wide", "narrow")),
        P(("wide", "narrow")),
        P(("wide", "narrow")),
        P(("wide", "narrow")),
        P(("wide", "narrow")),
    )
    small_slice = mesh.shape["wide"] == 8 and mesh.shape["narrow"] == 4
    return jax.shard_map(
        on_core if small_slice else on_device, mesh=mesh, in_specs=in_specs, out_specs=out_specs, check_vma=False
    )
```

```python
import functools
import math

import jax
import jax.numpy as jnp
from jax import lax
from jax.experimental import pallas as pl
from jax.experimental.pallas import tpu as pltpu
from jax.sharding import PartitionSpec as P

D = 768
FF = 3072
H = 12
HD = 64
STEP = 10


eps_norm = 1e-06
rate_matrix = 0.03
rate_small = 0.2
eps_adam = 1e-08
inv_root_two = 0.7071067811865476
inv_root_tau = 0.3989422804014327


def split_small(small):
    edges = [0, D, 2 * D, 3 * D, 4 * D, 5 * D, 6 * D, 7 * D, 7 * D + FF, 8 * D + FF]
    return [small[edges[i] : edges[i + 1]] for i in range(9)]


def standard(values):
    centre = values - jnp.mean(values, -1, keepdims=True)
    factor = lax.rsqrt(jnp.mean(centre * centre, -1, keepdims=True) + eps_norm)
    return (centre * factor, factor)


def norm_backward(grad, normed, factor, gain):
    grad_gain = jnp.sum(grad * normed, 0)
    grad_bias = jnp.sum(grad, 0)
    scaled = grad * gain
    inner_mean = jnp.mean(scaled * normed, -1, keepdims=True)
    grad_input = factor * (scaled - jnp.mean(scaled, -1, keepdims=True) - normed * inner_mean)
    return (grad_gain, grad_bias, grad_input)


def masked_scores(query, keys, key_mask):
    raw = jnp.einsum("sqhd,skhd->shqk", query, keys, preferred_element_type=jnp.float32) * (
        1.0 / math.sqrt(HD)
    )
    return jnp.where(key_mask, raw, -1e30)


def adamw(master, first, second, grad, decay, step_rate):
    first_new = 0.5 * first + 0.5 * grad
    second_new = 0.5 * second + 0.5 * grad * grad
    first_hat = first_new / (1.0 - 0.5**STEP)
    second_hat = second_new / (1.0 - 0.5**STEP)
    master_new = master - step_rate * (
        first_hat / (jnp.sqrt(second_hat) + eps_adam) + decay * master
    )
    return (master_new, first_new, second_new)


def scatter_sum(grad):
    lanes = grad.astype(jnp.bfloat16).reshape(-1, 128)
    own = lax.psum_scatter(lanes, ("wide", "narrow"), scatter_dimension=0, tiled=True)
    return own.reshape(-1).astype(jnp.float32)


def on_device(
    samples,
    cotangent,
    visible,
    master_attn,
    first_attn,
    second_attn,
    master_mlp,
    first_mlp,
    second_mlp,
    master_small,
    first_small,
    second_small,
):
    count, length, width = samples.shape
    total_rows = count * length
    scale = 1.0 / math.sqrt(HD)
    attn_full, mlp_full, small_full = (
        lax.all_gather(master_attn.astype(jnp.bfloat16), ("wide", "narrow"), axis=0, tiled=True),
        lax.all_gather(master_mlp.astype(jnp.bfloat16), ("wide", "narrow"), axis=0, tiled=True),
        lax.all_gather(master_small.astype(jnp.bfloat16), ("wide", "narrow"), axis=0, tiled=True),
    )
    w_qkv = attn_full[: 3 * D * D].reshape(D, 3 * D)
    w_out = attn_full[3 * D * D :].reshape(D, D)
    (
        gain_one,
        bias_one,
        bias_query,
        bias_value,
        bias_out,
        gain_two,
        bias_two,
        bias_inner,
        bias_outer,
    ) = split_small(small_full.astype(jnp.float32))
    valid = jnp.arange(length)[None, :] < visible[:, None]
    key_mask = valid[:, None, None, :]
    row_mask = valid.reshape(total_rows, 1)
    rows = samples.astype(jnp.float32).reshape(total_rows, D)
    normed_one, factor_one = standard(rows)
    first_in = (normed_one * gain_one + bias_one).astype(jnp.bfloat16)
    shift = jnp.concatenate([bias_query, jnp.zeros_like(bias_query), bias_value])
    qkv = jnp.dot(first_in, w_qkv, preferred_element_type=jnp.float32) + shift
    qkv_low = qkv.astype(jnp.bfloat16).reshape(count, length, 3, H, HD)
    query = qkv_low[:, :, 0]
    keys = qkv_low[:, :, 1]
    values = qkv_low[:, :, 2]
    scores = masked_scores(query, keys, key_mask)
    top = jnp.max(scores, -1, keepdims=True)
    expo = jnp.exp(scores - top)
    totals = jnp.sum(expo, -1, keepdims=True)
    log_total = top + jnp.log(totals)
    probs_low = (expo / totals).astype(jnp.bfloat16)
    context = jnp.einsum("shqk,skhd->sqhd", probs_low, values, preferred_element_type=jnp.float32)
    context_low = context.astype(jnp.bfloat16).reshape(total_rows, D)
    middle = rows + jnp.dot(context_low, w_out, preferred_element_type=jnp.float32) + bias_out
    w_one = mlp_full[: D * FF].reshape(D, FF)
    w_two = mlp_full[D * FF :].reshape(FF, D)
    normed_two, factor_two = standard(middle)
    second_in = (normed_two * gain_two + bias_two).astype(jnp.bfloat16)
    inner = jnp.dot(second_in, w_one, preferred_element_type=jnp.float32) + bias_inner
    active = jax.nn.gelu(inner, approximate=False).astype(jnp.bfloat16)
    result = middle + jnp.dot(active, w_two, preferred_element_type=jnp.float32) + bias_outer
    output = jnp.where(row_mask, result, 0.0).reshape(count, length, D).astype(jnp.bfloat16)
    grad_result = jnp.where(row_mask, cotangent.astype(jnp.float32).reshape(total_rows, D), 0.0)
    grad_branch = grad_result.astype(jnp.bfloat16)
    grad_w_two = jnp.einsum("rf,rd->fd", active, grad_branch, preferred_element_type=jnp.float32)
    grad_bias_outer = jnp.sum(grad_branch, 0, dtype=jnp.float32)
    grad_active = jnp.einsum("rd,fd->rf", grad_branch, w_two, preferred_element_type=jnp.float32)
    slope = (
        0.5 * (1.0 + jax.scipy.special.erf(inner * inv_root_two))
        + inner * jnp.exp(-0.5 * inner * inner) * inv_root_tau
    )
    grad_inner = (grad_active * slope).astype(jnp.bfloat16)
    grad_w_one = jnp.einsum("rd,rf->df", second_in, grad_inner, preferred_element_type=jnp.float32)
    grad_bias_inner = jnp.sum(grad_inner, 0, dtype=jnp.float32)
    grad_second_in = jnp.einsum("rf,df->rd", grad_inner, w_one, preferred_element_type=jnp.float32)
    grad_gain_two, grad_bias_two, grad_middle_norm = norm_backward(
        grad_second_in, normed_two, factor_two, gain_two
    )
    grad_middle = grad_result + grad_middle_norm
    grad_mlp = jnp.concatenate([grad_w_one.reshape(-1), grad_w_two.reshape(-1)])
    grad_proj = grad_middle.astype(jnp.bfloat16)
    grad_w_out = jnp.einsum("rc,rd->cd", context_low, grad_proj, preferred_element_type=jnp.float32)
    grad_bias_out = jnp.sum(grad_proj, 0, dtype=jnp.float32)
    grad_context = jnp.einsum("rd,cd->rc", grad_proj, w_out, preferred_element_type=jnp.float32)
    grad_context = grad_context.astype(jnp.bfloat16).reshape(count, length, H, HD)
    probs = jnp.exp(masked_scores(query, keys, key_mask) - log_total)
    probs_again = probs.astype(jnp.bfloat16)
    grad_values = jnp.einsum(
        "shqk,sqhd->skhd", probs_again, grad_context, preferred_element_type=jnp.float32
    )
    grad_probs = jnp.einsum(
        "sqhd,skhd->shqk", grad_context, values, preferred_element_type=jnp.float32
    )
    inner_sum = jnp.sum(grad_probs * probs, -1, keepdims=True)
    grad_scores = (probs * (grad_probs - inner_sum)).astype(jnp.bfloat16)
    grad_query = (
        jnp.einsum("shqk,skhd->sqhd", grad_scores, keys, preferred_element_type=jnp.float32) * scale
    )
    grad_keys = (
        jnp.einsum("shqk,sqhd->skhd", grad_scores, query, preferred_element_type=jnp.float32)
        * scale
    )
    grad_qkv = (
        jnp.stack([grad_query, grad_keys, grad_values], 2)
        .reshape(total_rows, 3 * D)
        .astype(jnp.bfloat16)
    )
    grad_w_qkv = jnp.einsum("rd,re->de", first_in, grad_qkv, preferred_element_type=jnp.float32)
    grad_bias_qkv = jnp.sum(grad_qkv, 0, dtype=jnp.float32)
    grad_first_in = jnp.einsum("re,de->rd", grad_qkv, w_qkv, preferred_element_type=jnp.float32)
    grad_gain_one, grad_bias_one, grad_rows_norm = norm_backward(
        grad_first_in, normed_one, factor_one, gain_one
    )
    grad_rows = grad_middle + grad_rows_norm
    grad_samples = grad_rows.reshape(count, length, D).astype(jnp.bfloat16)
    grad_attn = jnp.concatenate([grad_w_qkv.reshape(-1), grad_w_out.reshape(-1)])
    grad_small = jnp.concatenate(
        [
            grad_gain_one,
            grad_bias_one,
            grad_bias_qkv[:D],
            grad_bias_qkv[2 * D :],
            grad_bias_out,
            grad_gain_two,
            grad_bias_two,
            grad_bias_inner,
            grad_bias_outer,
        ]
    )
    summed_attn, summed_mlp, summed_small = (
        scatter_sum(grad_attn),
        scatter_sum(grad_mlp),
        lax.psum_scatter(grad_small, ("wide", "narrow"), scatter_dimension=0, tiled=True),
    )
    new_attn, new_first_attn, new_second_attn = adamw(
        master_attn, first_attn, second_attn, summed_attn, 0.1, rate_matrix
    )
    new_mlp, new_first_mlp, new_second_mlp = adamw(
        master_mlp, first_mlp, second_mlp, summed_mlp, 0.1, rate_matrix
    )
    new_small, new_first_small, new_second_small = adamw(
        master_small, first_small, second_small, summed_small, 0.0, rate_small
    )
    return (
        output,
        grad_samples,
        new_attn,
        new_first_attn,
        new_second_attn,
        new_mlp,
        new_first_mlp,
        new_second_mlp,
        new_small,
        new_first_small,
        new_second_small,
    )


bf16 = jnp.bfloat16
f32 = jnp.float32
BLOCK = 256
BIN = 128
AXES = ("wide", "narrow")
ROW = 128
SMALL_ROWS = 72


def place_of(i):
    wide, z = divmod(i, 4)
    return wide // 4, (wide // 2) % 2, wide % 2, z


def index_of(y, x, c, z):
    return ((y * 2 + x) * 2 + c) * 4 + z


def pairs_of(move):
    return [(i, index_of(*move(*place_of(i)))) for i in range(32)]


TO_X = pairs_of(lambda y, x, c, z: (y, 1 - x, c, z))
TO_Y = pairs_of(lambda y, x, c, z: (1 - y, x, c, z))
TO_CORE = pairs_of(lambda y, x, c, z: (y, x, 1 - c, z))
TO_Z = [pairs_of(lambda y, x, c, z, k=k: (y, x, c, z ^ k)) for k in range(4)]


def send(value, pairs):
    return lax.ppermute(value, AXES, pairs)


def dot(a, b, dims=((1,), (0,))):
    return lax.dot_general(a, b, (dims, ((), ())), preferred_element_type=f32)


def at_rows(ref, start, size):
    return ref[pl.ds(start, size), :]


def attn_block(core, j):
    return (j // 3) * 6 + 3 * core + j % 3


def mlp_block(core, j):
    return (j // 6) * 12 + 6 * core + j % 6


def shifted(idx, vector, out):
    lane = lax.broadcasted_iota(jnp.int32, (3, ROW), 1)
    out[...] = jnp.zeros(out.shape, f32)
    for k in range(4):

        @pl.when(idx[4] == k)
        def _():
            turned = pltpu.roll(vector[...], 32 * k, 1) if k else vector[...]
            at = 2 * k
            out[at : at + 3, :] = jnp.where(lane >= 32 * k, turned, 0.0)
            if k:
                out[at + 1 : at + 4, :] += jnp.where(lane < 32 * k, turned, 0.0)


def cut_masters(idx, attn, mlp, small, keep_a, send_a, keep_m, send_m, place, half_a, half_m):
    wide, core = idx[0], idx[3]

    @pl.when(wide < 6)
    def _():
        for c in range(2):
            for j in range(9):
                rows = attn[pl.ds(attn_block(c, j), 32, stride=18), :]
                half_a[c, j * 32 : (j + 1) * 32, :] = rows.astype(bf16)

    @pl.when(wide >= 6)
    def _():
        for j in range(6):
            rows = attn[pl.ds(j, 96, stride=6), :]
            half_a[j // 3, (j % 3) * 96 : (j % 3 + 1) * 96, :] = rows.astype(bf16)

    @pl.when(wide < 4)
    def _():
        for c in range(2):
            for j in range(12):
                rows = mlp[pl.ds(mlp_block(c, j), 48, stride=24), :]
                half_m[c, j * 48 : (j + 1) * 48, :] = rows.astype(bf16)

    @pl.when(wide >= 4)
    def _():
        for j in range(6):
            rows = mlp[pl.ds(j, 192, stride=6), :]
            half_m[j // 3, (j % 3) * 192 : (j % 3 + 1) * 192, :] = rows.astype(bf16)

    first_a = jnp.where(wide < 6, core, 0)
    first_m = jnp.where(wide < 4, core, 0)
    keep_a[0:288, :] = half_a[first_a]
    send_a[0:288, :] = half_a[1 - first_a]
    keep_m[...] = half_m[first_m]
    send_m[...] = half_m[1 - first_m]
    shifted(idx, small, place)
    keep_a[288:304, :] = place[...].astype(bf16)
    send_a[288:304, :] = place[...].astype(bf16)


def pack_rows(idx, vis_own, vis_other, x_own, x_other, cot_own, cot_other, x_out, cot_out, meta, fill):
    core = idx[3]
    for b in range(16):
        fill[b] = 0
    bins = jnp.int32(0)
    for s in range(16):
        mine = core == s // 8
        seen = jnp.where(mine, vis_own[s % 8], vis_other[s % 8])
        need = ((seen + 15) >> 4) << 4
        chosen = jnp.int32(15)
        for b in reversed(range(s + 1)):
            chosen = jnp.where(fill[b] + need <= BIN, b, chosen)
        start = chosen * BIN + fill[chosen]
        fill[chosen] = fill[chosen] + need
        bins = jnp.maximum(bins, chosen + 1)
        meta[8 + s] = start
        meta[24 + s] = seen
    blocks = (bins + 1) >> 1
    meta[0] = blocks

    def clear(b, carry):
        at = pl.ds(pl.multiple_of(b * BLOCK, BLOCK), BLOCK)
        x_out[at, :] = jnp.zeros((BLOCK, D), bf16)
        cot_out[at, :] = jnp.zeros((BLOCK, D), bf16)
        return carry

    lax.fori_loop(0, blocks, clear, 0)
    row = lax.broadcasted_iota(jnp.int32, (16, D), 0)
    for s in range(16):
        start, seen = meta[8 + s], meta[24 + s]

        def fetch(x_in, cot_in):
            def chunk(k, carry):
                src = pl.ds(pl.multiple_of(k * 16, 16), 16)
                dst = pl.ds(pl.multiple_of(start + k * 16, 16), 16)
                x_out[dst, :] = x_in[s % 8, src, :]
                grad = cot_in[s % 8, src, :].astype(f32)
                cot_out[dst, :] = jnp.where(row + k * 16 < seen, grad, 0.0).astype(bf16)
                return carry

            lax.fori_loop(0, (seen + 15) >> 4, chunk, 0)

        @pl.when(core == s // 8)
        def _():
            fetch(x_own, cot_own)

        @pl.when(core != s // 8)
        def _():
            fetch(x_other, cot_other)


def owner_of(idx, column, k):
    y, x, z = idx[1], idx[2], idx[4]
    yy = 1 - y if column >= 2 else y
    xx = 1 - x if column % 2 else x
    return yy * 2 + xx, jnp.bitwise_xor(z, k)


def pair_of(n):
    return n // 4 * 2 + n % 2


def core_of(idx, part):
    return 1 - idx[3] if part else idx[3]


def lanes_of(small, first, count):
    rows = [small[q // 9, q % 9 : q % 9 + 1, :] for q in range(first, first + count)]
    return jnp.concatenate(rows, axis=1)


def same_sample(meta, which):
    lane = lax.broadcasted_iota(jnp.int32, (8, BIN), 1)
    line = lax.broadcasted_iota(jnp.int32, (BIN, BIN), 0)
    of_key = jnp.full((8, BIN), -2, jnp.int32)
    of_query = jnp.full((BIN, BIN), -1, jnp.int32)
    for s in range(16):
        start = meta[8 + s] - which * BIN
        stop = start + meta[24 + s]
        of_key = jnp.where((lane >= start) & (lane < stop), s, of_key)
        of_query = jnp.where((line >= start) & (line < stop), s, of_query)
    return of_query == of_key[0:1, :]


def halves(pair):
    lane = lax.broadcasted_iota(jnp.int32, pair.shape, 1)
    wide = pair.astype(f32)
    return jnp.concatenate(
        [jnp.where(lane < HD, wide, 0.0), jnp.where(lane >= HD, wide, 0.0)], axis=0
    ).astype(bf16)


def probabilities(query, keys, mask):
    scores = dot(halves(query), keys, ((1,), (1,))) * (1.0 / math.sqrt(HD))
    scores = jnp.where(mask, scores, -1e30)
    expo = jnp.exp(scores - jnp.max(scores, -1, keepdims=True))
    return expo * (1.0 / jnp.sum(expo, -1, keepdims=True))


def probabilities_by_key(both, keys, mask):
    scores = dot(keys, both, ((1,), (1,))) * (1.0 / math.sqrt(HD))
    scores = jnp.where(mask, scores, -1e30)
    expo = jnp.exp(scores - jnp.max(scores, 0, keepdims=True))
    return expo * (1.0 / jnp.sum(expo, 0, keepdims=True))


def one_above_other(wide):
    return jnp.concatenate([wide[:, :BIN], wide[:, BIN:]], axis=0)


def side_by_side(stacked):
    return jnp.concatenate([stacked[:BIN], stacked[BIN:]], axis=1)


def attn_forward(phase, meta, idx, x_ref, *refs):
    pairs = refs[:8]
    qkv_ref, context_ref, part_ref, w_qkv, w_out, vecs, shift, inner_bias, small = refs[8:]

    if phase == 0:
        small[...] = jnp.zeros(small.shape, f32)
        for n in range(16):
            piece = pairs[pair_of(n)].at[n % 4 // 2]
            chip, z = owner_of(idx, n // 4, n % 4)

            @pl.when(chip < 3)
            def _():
                for part in range(2):
                    owner = (chip * 2 + core_of(idx, part)) * 4 + z
                    to = pl.ds(pl.multiple_of(owner * 32, 32), 32)
                    for j in range(9):
                        at = part * 288 + j * 32
                        w_qkv[to, j * ROW : (j + 1) * ROW] = piece[at : at + 32, :]

            @pl.when(chip == 3)
            def _():
                to = pl.ds(pl.multiple_of(z * 96, 32), 96)
                for j in range(6):
                    w_out[to, j * ROW : (j + 1) * ROW] = piece[j * 96 : (j + 1) * 96, :]

            for part in range(2):
                group = chip * 2 + core_of(idx, part)
                at = 576 + part * 16
                small[group] = small[group] + piece[at : at + 16, :].astype(f32)
        for n, first in enumerate((0, 6, 24, 30, 36, 66)):
            vecs[n : n + 1, :] = lanes_of(small, first, 6)
        vecs[6:8, :] = jnp.zeros((2, D), f32)
        own = idx[3] == 0
        query_bias = jnp.where(own, lanes_of(small, 12, 3), lanes_of(small, 15, 3))
        value_bias = jnp.where(own, lanes_of(small, 18, 3), lanes_of(small, 21, 3))
        shift[...] = jnp.concatenate([query_bias, jnp.zeros((1, D // 2), f32), value_bias], axis=1)
        low = jnp.where(own, lanes_of(small, 42, 6), lanes_of(small, 48, 6))
        high = jnp.where(own, lanes_of(small, 54, 6), lanes_of(small, 60, 6))
        inner_bias[...] = jnp.concatenate([low, high], axis=1)

    if phase == 1:
        normed, _ = standard(x_ref[...].astype(f32))
        first_in = (normed * vecs[0:1, :] + vecs[1:2, :]).astype(bf16)
        qkv_ref[...] = (dot(first_in, w_qkv[...]) + shift[...]).astype(bf16)
        for b in range(BLOCK // BIN):
            mask = same_sample(meta, pl.program_id(0) * (BLOCK // BIN) + b)
            mask = jnp.concatenate([mask, mask], axis=0)
            rows = slice(b * BIN, (b + 1) * BIN)
            for h in range(3):
                query, keys, values = (
                    qkv_ref[rows, (3 * t + h) * ROW : (3 * t + h + 1) * ROW] for t in range(3)
                )
                probs = probabilities(query, keys, mask).astype(bf16)
                context = dot(side_by_side(probs), halves(values))
                context_ref[rows, h * ROW : (h + 1) * ROW] = context.astype(bf16)
        part_ref[...] = dot(context_ref[...], w_out[...]).astype(bf16)


ERF_TOP = (0.00022905065861350646, 0.0034082910107109506, 0.050955695062380861, 0.18520832239976145, 1.128379143519084)
ERF_BOTTOM = (-1.1791602954361697e-7, 0.000023547966471313185, 0.0010179625278914885, 0.014070470171167667,
              0.11098505178285362, 0.49746925110067538, 1.0)


def error_function(v):
    v = jnp.clip(v, -3.832506856900711, 3.832506856900711)
    square = v * v
    top, bottom = jnp.full_like(v, ERF_TOP[0]), jnp.full_like(v, ERF_BOTTOM[0])
    for a in ERF_TOP[1:]:
        top = top * square + a
    for b in ERF_BOTTOM[1:]:
        bottom = bottom * square + b
    return v * top / bottom


def middle_of(x_ref, part_own, part_other, vecs):
    parts = part_own[...].astype(f32) + part_other[...].astype(f32)
    return x_ref[...].astype(f32) + parts + vecs[2:3, :]


def mlp_both(phase, meta, idx, x_ref, part_own, part_other, cot_ref, vecs, inner_bias, *refs):
    pieces = refs[:16]
    (active_ref, back_ref, w_two, sums, inner_sum) = refs[16:21]
    outs = refs[21:29]
    w_one, acc_one, acc_two = refs[29:]

    if phase == 0:
        acc_one[...] = jnp.zeros(acc_one.shape, f32)
        acc_two[...] = jnp.zeros(acc_two.shape, f32)
        sums[...] = jnp.zeros(sums.shape, f32)
        inner_sum[...] = jnp.zeros(inner_sum.shape, f32)
        for n, piece in enumerate(pieces):
            chip, z = owner_of(idx, n // 4, n % 4)

            @pl.when(chip < 2)
            def _():
                for part in range(2):
                    owner = (chip * 2 + core_of(idx, part)) * 4 + z
                    to = pl.ds(pl.multiple_of(owner * 48, 16), 48)
                    for j in range(12):
                        at = part * 576 + j * 48
                        w_one[to, j * ROW : (j + 1) * ROW] = piece[at : at + 48, :]

            @pl.when(chip >= 2)
            def _():
                to = pl.ds(pl.multiple_of((chip - 2) * D + z * 192, 64), 192)
                for j in range(6):
                    w_two[to, j * ROW : (j + 1) * ROW] = piece[j * 192 : (j + 1) * 192, :]

    if phase == 1:
        normed, _ = standard(middle_of(x_ref, part_own, part_other, vecs))
        second_in = (normed * vecs[3:4, :] + vecs[4:5, :]).astype(bf16)
        grad = cot_ref[...]
        back = jnp.zeros((BLOCK, D), f32)
        for n in range(2):
            cols = slice(n * D, (n + 1) * D)
            inner = dot(second_in, w_one[:, cols]) + inner_bias[:, cols]
            bell = 0.5 * (1.0 + error_function(inner * inv_root_two))
            active = (inner * bell).astype(bf16)
            active_ref[:, cols] = active
            slope = bell + inner * jnp.exp(-0.5 * inner * inner) * inv_root_tau
            grad_inner = (dot(grad, w_two[cols, :], ((1,), (1,))) * slope).astype(bf16)
            acc_two[cols, :] += dot(active, grad, ((0,), (0,)))
            acc_one[:, cols] += dot(second_in, grad_inner, ((0,), (0,)))
            inner_sum[:, cols] += jnp.sum(grad_inner.astype(f32), 0, keepdims=True)
            back = back + dot(grad_inner, w_one[:, cols], ((1,), (1,)))
        back_ref[...] = back.astype(bf16)
        sums[0:1, :] += jnp.sum(back * normed, 0, keepdims=True)
        sums[1:2, :] += jnp.sum(back, 0, keepdims=True)
        sums[2:3, :] += jnp.sum(grad.astype(f32), 0, keepdims=True)

    if phase == 2:
        for n in range(16):
            chip, z = owner_of(idx, n // 4, n % 4)
            out, k = outs[pair_of(n)], n % 4 // 2

            @pl.when(chip < 2)
            def _():
                for part in range(2):
                    owner = (chip * 2 + core_of(idx, part)) * 4 + z
                    rows = pl.ds(pl.multiple_of(owner * 48, 16), 48)
                    for j in range(12):
                        at = part * 576 + j * 48
                        out[k, at : at + 48, :] = acc_one[rows, j * ROW : (j + 1) * ROW].astype(bf16)

            @pl.when(chip >= 2)
            def _():
                rows = pl.ds(pl.multiple_of((chip - 2) * D + z * 192, 64), 192)
                for j in range(6):
                    out[k, j * 192 : (j + 1) * 192, :] = acc_two[rows, j * ROW : (j + 1) * ROW].astype(bf16)


def hand_on(phase, meta, idx, source, target):
    if phase == 1:
        target[...] = source[...]


def mlp_out(phase, meta, idx, active_ref, w_two, part_ref):
    if phase == 1:
        part_ref[...] = dot(active_ref[...], w_two[...]).astype(bf16)


def middle_backward(phase, meta, idx, x_ref, part_own, part_other, cot_ref, back_own, back_other, context_ref, w_out, vecs,
                    grad_ref, grad_context_ref, acc_out, sums):
    if phase == 0:
        acc_out[...] = jnp.zeros(acc_out.shape, f32)
        sums[...] = jnp.zeros(sums.shape, f32)

    if phase == 1:
        normed, factor = standard(middle_of(x_ref, part_own, part_other, vecs))
        scaled = (back_own[...].astype(f32) + back_other[...].astype(f32)) * vecs[3:4, :]
        through = scaled - jnp.mean(scaled, -1, keepdims=True)
        through = through - normed * jnp.mean(scaled * normed, -1, keepdims=True)
        grad_middle = cot_ref[...].astype(f32) + factor * through
        grad_ref[...] = grad_middle
        grad_proj = grad_middle.astype(bf16)
        acc_out[...] += dot(context_ref[...], grad_proj, ((0,), (0,)))
        sums[0:1, :] += jnp.sum(grad_proj.astype(f32), 0, keepdims=True)
        grad_context_ref[...] = dot(grad_proj, w_out[...], ((1,), (1,))).astype(bf16)


def heads_backward(phase, meta, idx, qkv_ref, grad_context_ref, grads):
    if phase == 1:
        scale = 1.0 / math.sqrt(HD)
        for b in range(BLOCK // BIN):
            mask = same_sample(meta, pl.program_id(0) * (BLOCK // BIN) + b)
            mask = jnp.concatenate([mask, mask], axis=1)
            rows = slice(b * BIN, (b + 1) * BIN)
            for h in range(3):
                cols = [slice((3 * t + h) * ROW, (3 * t + h + 1) * ROW) for t in range(3)]
                query, keys, values = (qkv_ref[rows, cols[t]] for t in range(3))
                both = halves(query)
                probs = probabilities_by_key(both, keys, mask)
                grad_out = halves(grad_context_ref[rows, h * ROW : (h + 1) * ROW])
                grad_values = dot(probs.astype(bf16), grad_out)
                grad_probs = dot(values, grad_out, ((1,), (1,)))
                total = jnp.sum(grad_probs * probs, 0, keepdims=True)
                grad_scores = (probs * (grad_probs - total)).astype(bf16)
                grad_keys = dot(grad_scores, both) * scale
                grad_query = dot(one_above_other(grad_scores), halves(keys), ((0,), (0,))) * scale
                grads[rows, cols[0]] = grad_query.astype(bf16)
                grads[rows, cols[1]] = grad_keys.astype(bf16)
                grads[rows, cols[2]] = grad_values.astype(bf16)


def first_backward(phase, meta, idx, x_ref, grads, w_qkv, acc_out, vecs, sums_in, inner_sum, sums_out, *refs):
    back_ref = refs[0]
    outs = refs[1:9]
    acc_qkv, sums, small = refs[9:]

    if phase == 0:
        acc_qkv[...] = jnp.zeros(acc_qkv.shape, f32)
        sums[...] = jnp.zeros(sums.shape, f32)

    if phase == 1:
        normed, _ = standard(x_ref[...].astype(f32))
        first_in = (normed * vecs[0:1, :] + vecs[1:2, :]).astype(bf16)
        grad_qkv = grads[...]
        acc_qkv[...] += dot(first_in, grad_qkv, ((0,), (0,)))
        back = dot(grad_qkv, w_qkv[...], ((1,), (1,)))
        back_ref[...] = back.astype(bf16)
        sums[0:1, :] += jnp.sum(back * normed, 0, keepdims=True)
        sums[1:2, :] += jnp.sum(back, 0, keepdims=True)
        sums[3:4, 0 : D // 2] += jnp.sum(grad_qkv[:, 0 : D // 2].astype(f32), 0, keepdims=True)
        sums[3:4, D // 2 : D] += jnp.sum(grad_qkv[:, D : D + D // 2].astype(f32), 0, keepdims=True)

    if phase == 2:
        small[...] = jnp.zeros(small.shape, f32)
        once = jnp.where(idx[3] == 0, 1.0, 0.0)

        def put(at, rows):
            for j in range(rows.shape[1] // ROW):
                q = at + j
                small[q // 9, q % 9 : q % 9 + 1, :] = rows[:, j * ROW : (j + 1) * ROW]

        put(0, sums[0:1, :])
        put(6, sums[1:2, :])
        put(24, sums_out[0:1, :] * once)
        put(30, sums_in[0:1, :])
        put(36, sums_in[1:2, :])
        put(66, sums_in[2:3, :] * once)
        for c in range(2):

            @pl.when(idx[3] == c)
            def _():
                put(12 + 3 * c, sums[3:4, 0 : D // 2])
                put(18 + 3 * c, sums[3:4, D // 2 : D])
                put(42 + 6 * c, inner_sum[:, 0:D])
                put(54 + 6 * c, inner_sum[:, D : 2 * D])

        for n in range(16):
            chip, z = owner_of(idx, n // 4, n % 4)
            out, k = outs[pair_of(n)], n % 4 // 2

            @pl.when(chip < 3)
            def _():
                for part in range(2):
                    owner = (chip * 2 + core_of(idx, part)) * 4 + z
                    rows = pl.ds(pl.multiple_of(owner * 32, 32), 32)
                    for j in range(9):
                        at = part * 288 + j * 32
                        out[k, at : at + 32, :] = acc_qkv[rows, j * ROW : (j + 1) * ROW].astype(bf16)

            @pl.when(chip == 3)
            def _():
                rows = pl.ds(pl.multiple_of(z * 96, 32), 96)
                for j in range(6):
                    out[k, j * 96 : (j + 1) * 96, :] = acc_out[rows, j * ROW : (j + 1) * ROW].astype(bf16)

            for part in range(2):
                group = chip * 2 + core_of(idx, part)
                out[k, 576 + part * 16 : 592 + part * 16, :] = small[group].astype(bf16)


def finish_rows(phase, meta, idx, x_ref, part_own, part_other, out_own, out_other, grad_ref, back_own, back_other, vecs,
                output, grad_samples, packed_out, packed_grad):
    if phase == 1:
        at = pl.ds(pl.multiple_of(pl.program_id(0) * BLOCK, BLOCK), BLOCK)
        parts = out_own[...].astype(f32) + out_other[...].astype(f32)
        result = middle_of(x_ref, part_own, part_other, vecs) + parts + vecs[5:6, :]
        packed_out[at, :] = result.astype(bf16)
        normed, factor = standard(x_ref[...].astype(f32))
        scaled = (back_own[...].astype(f32) + back_other[...].astype(f32)) * vecs[0:1, :]
        through = scaled - jnp.mean(scaled, -1, keepdims=True)
        through = through - normed * jnp.mean(scaled * normed, -1, keepdims=True)
        packed_grad[at, :] = (grad_ref[...] + factor * through).astype(bf16)

    if phase == 2:
        output[...] = jnp.zeros(output.shape, bf16)
        grad_samples[...] = jnp.zeros(grad_samples.shape, bf16)
        row = lax.broadcasted_iota(jnp.int32, (16, D), 0)
        for s in range(8):
            start, seen = meta[8 + idx[3] * 8 + s], meta[24 + idx[3] * 8 + s]

            def chunk(k, carry):
                src = pl.ds(pl.multiple_of(start + k * 16, 16), 16)
                dst = pl.ds(pl.multiple_of(k * 16, 16), 16)
                keep = row + k * 16 < seen
                for packed, out in ((packed_out, output), (packed_grad, grad_samples)):
                    out[s, dst, :] = jnp.where(keep, packed[src, :].astype(f32), 0.0).astype(bf16)
                return carry

            lax.fori_loop(0, (seen + 15) >> 4, chunk, 0)


def update_refs(master, first, second, grad, outs, decay, step_rate):
    for out, new in zip(outs, adamw(master[...], first[...], second[...], grad, decay, step_rate)):
        out[...] = new


def step_mlp(idx, master, first, second, keep, mine, other, new, new_first, new_second, half, grad):
    wide, core = idx[0], idx[3]
    at = jnp.where(wide < 4, core, 0)
    half[at] = keep[...]

    @pl.when(wide < 4)
    def _():
        half[1 - at] = other[...]

    @pl.when(wide >= 4)
    def _():
        half[1 - at] = mine[...]

    @pl.when(wide < 4)
    def _():
        for c in range(2):
            for j in range(12):
                grad[pl.ds(mlp_block(c, j), 48, stride=24), :] = half[c, j * 48 : (j + 1) * 48, :]

    @pl.when(wide >= 4)
    def _():
        for j in range(6):
            grad[pl.ds(j, 192, stride=6), :] = half[j // 3, (j % 3) * 192 : (j % 3 + 1) * 192, :]

    update_refs(master, first, second, grad[...], (new, new_first, new_second), 0.1, rate_matrix)


def step_attn(idx, master, first, second, keep, mine, other, master_s, first_s, second_s, keep_s, other_s,
              new, new_first, new_second, new_s, new_first_s, new_second_s, half, grad, place, small_grad):
    wide, core = idx[0], idx[3]
    at = jnp.where(wide < 6, core, 0)
    half[at] = keep[...]

    @pl.when(wide < 6)
    def _():
        half[1 - at] = other[...]

    @pl.when(wide >= 6)
    def _():
        half[1 - at] = mine[...]

    @pl.when(wide < 6)
    def _():
        for c in range(2):
            for j in range(9):
                grad[pl.ds(attn_block(c, j), 32, stride=18), :] = half[c, j * 32 : (j + 1) * 32, :]

    @pl.when(wide >= 6)
    def _():
        for j in range(6):
            grad[pl.ds(j, 96, stride=6), :] = half[j // 3, (j % 3) * 96 : (j % 3 + 1) * 96, :]

    update_refs(master, first, second, grad[...], (new, new_first, new_second), 0.1, rate_matrix)
    place[...] = keep_s[...] + other_s[...]
    lane = lax.broadcasted_iota(jnp.int32, (3, ROW), 1)
    for k in range(4):

        @pl.when(idx[4] == k)
        def _():
            at = 2 * k
            both = jnp.where(lane >= 32 * k, place[at : at + 3, :], place[at + 1 : at + 4, :])
            small_grad[...] = pltpu.roll(both, ROW - 32 * k, 1) if k else both

    update_refs(master_s, first_s, second_s, small_grad[...], (new_s, new_first_s, new_second_s), 0.0, rate_small)


def plus(*terms):
    return sum(t.astype(f32) for t in terms)


def nothing(idx, out):
    out[...] = jnp.zeros(out.shape, f32)


def lay_attn(idx, keep, mine, other, piece):
    piece[0:288, :] = keep[0:288, :]
    piece[576:592, :] = keep[288:304, :]
    piece[592:608, :] = other[288:304, :]

    @pl.when(idx[0] < 6)
    def _():
        piece[288:576, :] = other[0:288, :]

    @pl.when(idx[0] >= 6)
    def _():
        piece[288:576, :] = mine[0:288, :]


def lay_mlp(idx, keep, mine, other, piece):
    piece[0:576, :] = keep[...]

    @pl.when(idx[0] < 4)
    def _():
        piece[576:1152, :] = other[...]

    @pl.when(idx[0] >= 4)
    def _():
        piece[576:1152, :] = mine[...]


def lay_out(*refs):
    at = 0
    for ref in refs[:-1]:
        refs[-1][at : at + ref.shape[0], :] = ref[...]
        at += ref.shape[0]


def pair_up(first, second, pair):
    pair[0] = first[...]
    pair[1] = second[...]


def add_low(*refs):
    refs[-1][...] = plus(*(r[...] for r in refs[:-1])).astype(bf16)


def add_near_far(*refs):
    terms, (near, far) = refs[:-2], refs[-2:]
    near[...] = plus(*(r[0] for r in terms))
    far[...] = plus(*(r[1] for r in terms)).astype(bf16)


def add_last(half, near, other, *outs):
    total = near[...] + other[...].astype(f32)
    outs[0][...] = total[:half]
    outs[1][...] = total[half : 2 * half]
    for n, out in enumerate(outs[2:]):
        out[...] = total[2 * half + 16 * n : 2 * half + 16 * n + 16]


SENDS = {
    "cv": ("visible", TO_CORE),
    "cs": ("samples", TO_CORE),
    "cc": ("cotangent", TO_CORE),
    "sa": ("send_a", TO_CORE),
    "sm": ("send_m", TO_CORE),
    "z2a": ("pa", TO_Z[2]),
    "zOa": ("Ea", TO_Z[1]),
    "xEa": ("Ea", TO_X),
    "yEa": ("Ea", TO_Y),
    "xOa": ("zOa", TO_X),
    "yOa": ("zOa", TO_Y),
    "dEa": ("yEa", TO_X),
    "dOa": ("xOa", TO_Y),
    "z1m": ("pm", TO_Z[1]),
    "z2m": ("pm2", TO_Z[2]),
    "z3m": ("z2m", TO_Z[1]),
    "x0m": ("pm", TO_X),
    "y0m": ("pm", TO_Y),
    "x1m": ("z1m", TO_X),
    "y1m": ("z1m", TO_Y),
    "x2m": ("z2m", TO_X),
    "y2m": ("z2m", TO_Y),
    "x3m": ("z3m", TO_X),
    "y3m": ("z3m", TO_Y),
    "d0m": ("y0m", TO_X),
    "d1m": ("d0m", TO_Z[1]),
    "d2m": ("x2m", TO_Y),
    "d3m": ("d2m", TO_Z[1]),
    "pt": ("part", TO_CORE),
    "bk": ("back", TO_CORE),
    "ot": ("out_part", TO_CORE),
    "fb": ("first_back_2", TO_CORE),
}
for group in "am":
    SENDS |= {
        "rE" + group: ("dE" + group + "_grad", TO_X),
        "rO" + group: ("dO" + group + "_grad", TO_Y),
        "pE" + group: ("xE" + group + "_grad", TO_X),
        "pO" + group: ("yO" + group + "_grad", TO_Y),
        "qE" + group: ("aE" + group, TO_Y),
        "qO" + group: ("aO" + group, TO_X),
        "wO" + group: ("so" + group, TO_Z[1]),
        "w2" + group: ("far" + group, TO_Z[2]),
        "g" + group: ("other" + group, TO_CORE),
    }
SENDS["gs"] = ("other_small", TO_CORE)
PAIR_NAMES = ("E{}_grad", "O{}_grad", "xE{}_grad", "xO{}_grad", "yE{}_grad", "yO{}_grad", "dE{}_grad", "dO{}_grad")

AFTER = {
    "pa": ("cs", "cc", "cv"),
    "pm": ("pa",),
    "Ea": ("meta",),
    "pm2": ("Ea",),
    "fwd": ("x1m", "y1m", "x0m", "y0m"),
    "there": ("x3m", "y3m", "d1m", "d2m", "d3m", "x2m", "d0m", "vecs"),
    "mlp": ("there",),
    "bw1": ("out_part",),
    "aEm": ("grad_context",),
    "aOm": ("grad_context",),
    "bw2": ("aEm", "aOm"),
    "bw3": ("ot",),
    "som": ("first_back",),
    "hand": ("som",),
    "aEa": ("farm",),
    "fin": ("soa",),
    "sza": ("output",),
    "sua": ("done_m",),
}

ORDER = (
    "+cv", "+cs", "+cc", "=cut", "+sa", "+sm", "=pack", "=pa", "+z2a", "=pm", "+z1m", "+x0m", "+y0m",
    "=Ea", "=pm2", "+z2m", "+zOa", "+xEa", "+yEa", "+x1m", "+y1m", "+dEa", "+yOa", "+z3m", "+xOa", "+y2m", "+x2m",
    "+d0m", "+dOa", "+y3m", "+x3m", "+d2m", "=fwd", "+pt", "+d1m", "+d3m", "=there",
    "=mlp", "+rEm", "+rOm", "+bk", "=mout", "+ot", "=bw1", "=aEm", "=aOm", "+qOm", "+qEm", "+pEm", "+pOm", "=bw2",
    "=bw3", "+rEa", "+rOa", "=som", "=hand", "+fb", "+wOm", "=szm", "+w2m", "=aEa", "=aOa", "+qOa", "+qEa", "+pEa", "+pOa",
    "=soa", "+wOa", "=fin", "=sum", "+gm", "=om", "=sza", "+w2a", "=sua", "+ga", "+gs", "=oa",
)


SMEM = pl.BlockSpec(memory_space=pltpu.SMEM)
VMEM = pl.BlockSpec(memory_space=pltpu.VMEM)
ANY = pl.BlockSpec(memory_space=pl.ANY)


def array(shape, dtype=bf16):
    return jax.ShapeDtypeStruct(shape, dtype)


def large(shape, dtype=bf16):
    return pltpu.HBM(shape, dtype)


def params(mib):
    return pltpu.CompilerParams(vmem_limit_bytes=mib << 20)


SCALE = 10**9
COSTS = {
    "attn_forward": 11, "mlp_both": 23, "mlp_out": 20, "middle_backward": 8, "heads_backward": 25, "first_backward": 25,
    "finish_rows": 8, "pack_rows": 6, "all_there": 60,
}


def cost(name):
    return pl.CostEstimate(flops=COSTS.get(name, 1) * SCALE, bytes_accessed=1, transcendentals=0)


def in_hbm(value):
    return pltpu.with_memory_space_constraint(value, pltpu.HBM)


def full(value):
    return pl.BlockSpec(value.shape, lambda i: (0,) * len(value.shape))


def over_blocks(body, rows_in, fixed_in, rows_out, fixed_out, scratch, mib, name, after=()):
    many = rows_in + [w for w, _, _ in rows_out]
    n_in, n_out = len(rows_in), len(rows_out)

    def kernel(meta, idx, *refs):
        refs = refs[: n_in + fixed_in] + refs[n_in + fixed_in + len(after) :]
        rows, fixed, lines, rest = (
            refs[:n_in], refs[n_in : n_in + fixed_in], refs[n_in + fixed_in :][:n_out], refs[n_in + fixed_in + n_out :]
        )
        body(0, meta, idx, *rows, *fixed, *lines, *rest)

        def one(*blocks):
            body(1, meta, idx, *blocks[:n_in], *fixed, *blocks[n_in:], *rest)

        specs = [pl.BlockSpec((BLOCK, w), lambda i: (i, 0)) for w in many]
        pltpu.emit_pipeline(one, grid=(meta[0],), in_specs=specs[:n_in], out_specs=specs[n_in:])(*rows, *lines)
        body(2, meta, idx, *rows, *fixed, *lines, *rest)

    def called(meta, idx, *args):
        return pl.pallas_call(
            kernel,
            grid=(1,),
            in_specs=[SMEM, SMEM] + [ANY] * n_in + [full(a) for a in args[n_in:]] + [ANY] * len(after),
            out_specs=[ANY] * n_out + [full(a) for a in fixed_out],
            out_shape=[large((n, w), t) for w, t, n in rows_out] + fixed_out,
            scratch_shapes=scratch,
            compiler_params=params(mib),
            cost_estimate=cost(name),
            name=name,
        )(meta, idx, *args, *after)

    return called


def at_once(body, scalars, outs, scratch, mib, name, after=(), copied=False):
    def kernel(*refs):
        n = len(refs) - len(scratch) - len(outs) - len(after)
        body(*refs[:n], *refs[n + len(after) :])

    def called(*args):
        grid = {"grid": (1,)} if copied else {}
        blocks = [full(a) if copied else VMEM for a in args[scalars:]]
        arrays = [in_hbm(a) for a in args[scalars:]] if copied else args[scalars:]
        return pl.pallas_call(
            kernel,
            in_specs=[SMEM] * scalars + blocks + [ANY] * len(after),
            out_specs=[SMEM if a.dtype == jnp.int32 else full(a) if copied else VMEM for a in outs],
            out_shape=outs,
            scratch_shapes=scratch,
            compiler_params=params(mib),
            cost_estimate=cost(name),
            name=name,
            **grid,
        )(*args[:scalars], *arrays, *after)

    return called


def on_core(
    samples,
    cotangent,
    visible,
    master_attn,
    first_attn,
    second_attn,
    master_mlp,
    first_mlp,
    second_mlp,
    master_small,
    first_small,
    second_small,
):
    count, length, _ = samples.shape
    rows = 2 * count * length
    wide, z = lax.axis_index("wide"), lax.axis_index("narrow")
    idx = jnp.stack([wide, wide // 4, (wide // 2) % 2, wide % 2, z]).astype(jnp.int32)

    def lanes(flat):
        return flat.reshape(-1, ROW)

    def three_rows(vector):
        return lanes(jnp.pad(vector, (0, 3 * ROW - vector.shape[0])))

    half_a, half_m = (288, ROW), (576, ROW)
    shape_m, shape_a, shape_s = (1152, ROW), (576, ROW), (16, ROW)
    pair_a, pair_m = (2, 608, ROW), (2, 1152, ROW)

    def after(name):
        return tuple(v[n] for n in AFTER.get(name, ()))

    v = {"visible": visible, "samples": samples, "cotangent": cotangent}

    def hbm(*names):
        return tuple(v[n] if n in SENDS else in_hbm(v[n]) for n in names)

    def cut():
        swap_a = (304, ROW)
        v["keep_a"], v["send_a"], v["keep_m"], v["send_m"] = at_once(
            cut_masters, 1, [array(swap_a), array(swap_a), array(half_m), array(half_m)],
            [pltpu.VMEM(shape_s, f32), pltpu.VMEM((2, *half_a), bf16), pltpu.VMEM((2, *half_m), bf16)], 8, "cut_masters", after("cut"), True,
        )(idx, lanes(master_attn), lanes(master_mlp), three_rows(master_small))

    def piece_a():
        v["pa"] = at_once(lay_attn, 1, [array((608, ROW))], [], 8, "piece_attn", after("pa"))(
            idx, v["keep_a"], v["send_a"], v["sa"]
        )[0]

    def even_a():
        v["Ea"] = at_once(
            pair_up, 0, [array(pair_a)], [], 8, "pair_up", after("Ea")
        )(v["pa"], v["z2a"])[0]

    def piece_m():
        v["pm"] = at_once(lay_mlp, 1, [array(shape_m)], [], 8, "piece_mlp", after("pm"))(
            idx, v["keep_m"], v["send_m"], v["sm"]
        )[0]

    def again_m():
        v["pm2"] = at_once(lay_out, 0, [array(shape_m)], [], 8, "piece_again", after("pm2"))(v["pm"])[0]

    def pack():
        v["x"], v["cot"], v["meta"] = at_once(
            pack_rows, 3, [large((rows, D)), large((rows, D)), array((64,), jnp.int32)],
            [pltpu.SMEM((16,), jnp.int32)], 32, "pack_rows", after("pack"),
        )(idx, visible, v["cv"], in_hbm(samples), v["cs"], in_hbm(cotangent), v["cc"])

    def forward():
        outs = [large((D, 3 * D // 2)), large((D // 2, D)), array((8, D), f32), array((1, 3 * D // 2), f32), array((1, FF // 2), f32)]
        (v["qkv"], v["context"], v["part"], v["w_qkv"], v["w_out"], v["vecs"], shift, v["inner_bias"]) = over_blocks(
            attn_forward, [D], 8, [(3 * D // 2, bf16, rows), (D // 2, bf16, rows), (D, bf16, rows)], outs,
            [pltpu.VMEM((8, 16, ROW), f32)], 24, "attn_forward", after("fwd"),
        )(v["meta"], idx, *hbm("x"), v["Ea"], *(v[n] for n in ("zOa", "xEa", "xOa", "yEa", "yOa", "dEa", "dOa")))

    def there():
        v["there"] = at_once(nothing, 1, [array((8, ROW), f32)], [], 4, "all_there", after("there"))(idx)[0]

    def middle():
        return hbm("x", "part", "pt")

    def mlp():
        pieces = [v["pm"] if c + k == "z0" else v[c + k + "m"] for c in "zxyd" for k in "0123"]
        done = over_blocks(
            mlp_both, [D] * 4, 18, [(FF // 2, bf16, rows), (D, bf16, rows)],
            [large((FF // 2, D)), array((8, D), f32), array((1, FF // 2), f32)] + [array(pair_m)] * 8,
            [pltpu.VMEM((D, FF // 2), bf16), pltpu.VMEM((D, FF // 2), f32), pltpu.VMEM((FF // 2, D), f32)],
            48, "mlp_both", after("mlp"),
        )(v["meta"], idx, *middle(), *hbm("cot"), v["vecs"], v["inner_bias"], *pieces)
        v["active"], v["back"], v["w_two"], v["sums"], v["inner_sum"] = done[:5]
        v.update(zip((n.format("m") for n in PAIR_NAMES), done[5:]))

    def out_rows():
        v["out_part"] = over_blocks(mlp_out, [FF // 2], 1, [(D, bf16, rows)], [], [], 16, "mlp_out", after("mout"))(
            v["meta"], idx, *hbm("active", "w_two")
        )[0]

    def backward_1():
        v["grad_middle"], v["grad_context"], v["acc_out"], v["sums_out"] = over_blocks(
            middle_backward, [D] * 6 + [D // 2], 2, [(D, f32, rows), (D // 2, bf16, rows)],
            [large((D // 2, D), f32), array((8, D), f32)], [], 16, "middle_backward", after("bw1"),
        )(v["meta"], idx, *middle(), *hbm("cot", "back", "bk", "context", "w_out"), v["vecs"])

    def backward_2():
        v["grad_qkv"] = over_blocks(
            heads_backward, [3 * D // 2, D // 2], 0, [(3 * D // 2, bf16, rows)], [], [], 16, "heads_backward", after("bw2"),
        )(v["meta"], idx, *hbm("qkv", "grad_context"))[0]

    def backward_3():
        done = over_blocks(
            first_backward, [D, 3 * D // 2], 6, [(D, bf16, rows)], [array(pair_a)] * 8,
            [pltpu.VMEM((D, 3 * D // 2), f32), pltpu.VMEM((8, D), f32), pltpu.VMEM((8, 16, ROW), f32)],
            20, "first_backward", after("bw3"),
        )(v["meta"], idx, *hbm("x", "grad_qkv"), *hbm("w_qkv", "acc_out"), *(v[n] for n in ("vecs", "sums", "inner_sum", "sums_out")))
        v["first_back"] = done[0]
        v.update(zip((n.format("a") for n in PAIR_NAMES), done[1:]))

    def again_back():
        v["first_back_2"] = over_blocks(hand_on, [D], 0, [(D, bf16, rows)], [], [], 8, "hand_on", after("hand"))(
            v["meta"], idx, *hbm("first_back")
        )[0]

    def finish():
        v["output"], v["grad_samples"] = over_blocks(
            finish_rows, [D] * 8, 1, [], [large((count, length, D))] * 2, [pltpu.VMEM((rows, D), bf16)] * 2, 24, "finish_rows", after("fin"),
        )(v["meta"], idx, *middle(), *hbm("out_part", "ot", "grad_middle", "first_back", "fb"), v["vecs"])

    def adds(g):
        pair, half = (pair_a, 288) if g == "a" else (pair_m, 576)

        def add(body, terms, outs, name):
            return at_once(
                body, 0, outs, [], 24, name + g, after(name + g)
            )(*(v[t] for t in terms))

        def even_in():
            v["aE" + g] = add(add_low, [f"yE{g}_grad", "rE" + g], [array(pair)], "aE")[0]

        def odd_in():
            v["aO" + g] = add(add_low, [f"xO{g}_grad", "rO" + g], [array(pair)], "aO")[0]

        def odd_sum():
            v["so" + g] = add(add_low, [f"O{g}_grad", "pO" + g, "qO" + g], [array(pair)], "so")[0]

        def even_sum():
            v["near" + g], v["far" + g] = add(
                add_near_far, [f"E{g}_grad", "pE" + g, "qE" + g, "wO" + g], [array(pair[1:], f32), array(pair[1:])], "sz"
            )

        def last_sum():
            outs = [array((half, ROW), f32)] * 2 + ([array(shape_s, f32)] * 2 if g == "a" else [])
            done = add(functools.partial(add_last, half), ["near" + g, "w2" + g], outs, "su")
            v["own" + g], v["other" + g] = done[:2]
            if g == "a":
                v["own_small"], v["other_small"] = done[2:]

        return {"aE" + g: even_in, "aO" + g: odd_in, "so" + g: odd_sum, "sz" + g: even_sum, "su" + g: last_sum}

    def optimize_m():
        v["new_mlp"] = at_once(
            step_mlp, 1, [array(shape_m, f32)] * 3,
            [pltpu.VMEM((2, *half_m), f32), pltpu.VMEM(shape_m, f32)], 16, "step_mlp", after("om"),
        )(idx, lanes(master_mlp), lanes(first_mlp), lanes(second_mlp), v["ownm"], v["otherm"], v["gm"])
        v["done_m"] = v["new_mlp"][0]

    def optimize_a():
        v["new_attn"] = at_once(
            step_attn, 1, [array(shape_a, f32)] * 3 + [array((3, ROW), f32)] * 3,
            [pltpu.VMEM((2, *half_a), f32), pltpu.VMEM(shape_a, f32), pltpu.VMEM(shape_s, f32), pltpu.VMEM((3, ROW), f32)], 16, "step_attn", after("oa"),
        )(idx, lanes(master_attn), lanes(first_attn), lanes(second_attn), v["owna"], v["othera"], v["ga"],
          three_rows(master_small), three_rows(first_small), three_rows(second_small), v["own_small"], v["gs"])

    works = {"cut": cut, "pa": piece_a, "Ea": even_a, "pm": piece_m, "pm2": again_m, "pack": pack, "there": there, "fwd": forward, "mlp": mlp, "mout": out_rows,
             "bw1": backward_1, "bw2": backward_2, "bw3": backward_3, "hand": again_back, "fin": finish, "om": optimize_m, "oa": optimize_a, **adds("m"), **adds("a")}
    for step in ORDER:
        kind, name = step[0], step[1:]
        if kind == "+":
            source, pairs = SENDS[name]
            v[name] = send(v[source], pairs)
        elif kind == "=":
            works[name]()

    new_mlp, new_attn, output, grad_samples = v["new_mlp"], v["new_attn"], v["output"], v["grad_samples"]
    new_small = [a.reshape(-1)[:288] for a in new_attn[3:]]
    return (output, grad_samples, *(v.reshape(-1) for v in new_attn[:3]), *(v.reshape(-1) for v in new_mlp), *new_small)


def solution(mesh):
    in_specs = (
        P(("wide", "narrow"), None, None),
        P(("wide", "narrow"), None, None),
        P(("wide", "narrow")),
        P(("wide", "narrow")),
        P(("wide", "narrow")),
        P(("wide", "narrow")),
        P(("wide", "narrow")),
        P(("wide", "narrow")),
        P(("wide", "narrow")),
        P(("wide", "narrow")),
        P(("wide", "narrow")),
        P(("wide", "narrow")),
    )
    out_specs = (
        P(("wide", "narrow"), None, None),
        P(("wide", "narrow"), None, None),
        P(("wide", "narrow")),
        P(("wide", "narrow")),
        P(("wide", "narrow")),
        P(("wide", "narrow")),
        P(("wide", "narrow")),
        P(("wide", "narrow")),
        P(("wide", "narrow")),
        P(("wide", "narrow")),
        P(("wide", "narrow")),
    )
    small_slice = mesh.shape["wide"] == 8 and mesh.shape["narrow"] == 4
    return jax.shard_map(
        on_core if small_slice else on_device, mesh=mesh, in_specs=in_specs, out_specs=out_specs, check_vma=False
    )
```

```python
import functools
import math

import jax
import jax.numpy as jnp
from jax import lax
from jax.experimental import pallas as pl
from jax.experimental.pallas import tpu as pltpu
from jax.sharding import PartitionSpec as P

D = 768
FF = 3072
H = 12
HD = 64
STEP = 10


eps_norm = 1e-06
rate_matrix = 0.03
rate_small = 0.2
eps_adam = 1e-08
inv_root_two = 0.7071067811865476
inv_root_tau = 0.3989422804014327


def split_small(small):
    edges = [0, D, 2 * D, 3 * D, 4 * D, 5 * D, 6 * D, 7 * D, 7 * D + FF, 8 * D + FF]
    return [small[edges[i] : edges[i + 1]] for i in range(9)]


def standard(values):
    centre = values - jnp.mean(values, -1, keepdims=True)
    factor = lax.rsqrt(jnp.mean(centre * centre, -1, keepdims=True) + eps_norm)
    return (centre * factor, factor)


def norm_backward(grad, normed, factor, gain):
    grad_gain = jnp.sum(grad * normed, 0)
    grad_bias = jnp.sum(grad, 0)
    scaled = grad * gain
    inner_mean = jnp.mean(scaled * normed, -1, keepdims=True)
    grad_input = factor * (scaled - jnp.mean(scaled, -1, keepdims=True) - normed * inner_mean)
    return (grad_gain, grad_bias, grad_input)


def masked_scores(query, keys, key_mask):
    raw = jnp.einsum("sqhd,skhd->shqk", query, keys, preferred_element_type=jnp.float32) * (
        1.0 / math.sqrt(HD)
    )
    return jnp.where(key_mask, raw, -1e30)


def adamw(master, first, second, grad, decay, step_rate):
    first_new = 0.5 * first + 0.5 * grad
    second_new = 0.5 * second + 0.5 * grad * grad
    first_hat = first_new / (1.0 - 0.5**STEP)
    second_hat = second_new / (1.0 - 0.5**STEP)
    master_new = master - step_rate * (
        first_hat / (jnp.sqrt(second_hat) + eps_adam) + decay * master
    )
    return (master_new, first_new, second_new)


def scatter_sum(grad):
    lanes = grad.astype(jnp.bfloat16).reshape(-1, 128)
    own = lax.psum_scatter(lanes, ("wide", "narrow"), scatter_dimension=0, tiled=True)
    return own.reshape(-1).astype(jnp.float32)


def on_device(
    samples,
    cotangent,
    visible,
    master_attn,
    first_attn,
    second_attn,
    master_mlp,
    first_mlp,
    second_mlp,
    master_small,
    first_small,
    second_small,
):
    count, length, width = samples.shape
    total_rows = count * length
    scale = 1.0 / math.sqrt(HD)
    attn_full, mlp_full, small_full = (
        lax.all_gather(master_attn.astype(jnp.bfloat16), ("wide", "narrow"), axis=0, tiled=True),
        lax.all_gather(master_mlp.astype(jnp.bfloat16), ("wide", "narrow"), axis=0, tiled=True),
        lax.all_gather(master_small.astype(jnp.bfloat16), ("wide", "narrow"), axis=0, tiled=True),
    )
    w_qkv = attn_full[: 3 * D * D].reshape(D, 3 * D)
    w_out = attn_full[3 * D * D :].reshape(D, D)
    (
        gain_one,
        bias_one,
        bias_query,
        bias_value,
        bias_out,
        gain_two,
        bias_two,
        bias_inner,
        bias_outer,
    ) = split_small(small_full.astype(jnp.float32))
    valid = jnp.arange(length)[None, :] < visible[:, None]
    key_mask = valid[:, None, None, :]
    row_mask = valid.reshape(total_rows, 1)
    rows = samples.astype(jnp.float32).reshape(total_rows, D)
    normed_one, factor_one = standard(rows)
    first_in = (normed_one * gain_one + bias_one).astype(jnp.bfloat16)
    shift = jnp.concatenate([bias_query, jnp.zeros_like(bias_query), bias_value])
    qkv = jnp.dot(first_in, w_qkv, preferred_element_type=jnp.float32) + shift
    qkv_low = qkv.astype(jnp.bfloat16).reshape(count, length, 3, H, HD)
    query = qkv_low[:, :, 0]
    keys = qkv_low[:, :, 1]
    values = qkv_low[:, :, 2]
    scores = masked_scores(query, keys, key_mask)
    top = jnp.max(scores, -1, keepdims=True)
    expo = jnp.exp(scores - top)
    totals = jnp.sum(expo, -1, keepdims=True)
    log_total = top + jnp.log(totals)
    probs_low = (expo / totals).astype(jnp.bfloat16)
    context = jnp.einsum("shqk,skhd->sqhd", probs_low, values, preferred_element_type=jnp.float32)
    context_low = context.astype(jnp.bfloat16).reshape(total_rows, D)
    middle = rows + jnp.dot(context_low, w_out, preferred_element_type=jnp.float32) + bias_out
    w_one = mlp_full[: D * FF].reshape(D, FF)
    w_two = mlp_full[D * FF :].reshape(FF, D)
    normed_two, factor_two = standard(middle)
    second_in = (normed_two * gain_two + bias_two).astype(jnp.bfloat16)
    inner = jnp.dot(second_in, w_one, preferred_element_type=jnp.float32) + bias_inner
    active = jax.nn.gelu(inner, approximate=False).astype(jnp.bfloat16)
    result = middle + jnp.dot(active, w_two, preferred_element_type=jnp.float32) + bias_outer
    output = jnp.where(row_mask, result, 0.0).reshape(count, length, D).astype(jnp.bfloat16)
    grad_result = jnp.where(row_mask, cotangent.astype(jnp.float32).reshape(total_rows, D), 0.0)
    grad_branch = grad_result.astype(jnp.bfloat16)
    grad_w_two = jnp.einsum("rf,rd->fd", active, grad_branch, preferred_element_type=jnp.float32)
    grad_bias_outer = jnp.sum(grad_branch, 0, dtype=jnp.float32)
    grad_active = jnp.einsum("rd,fd->rf", grad_branch, w_two, preferred_element_type=jnp.float32)
    slope = (
        0.5 * (1.0 + jax.scipy.special.erf(inner * inv_root_two))
        + inner * jnp.exp(-0.5 * inner * inner) * inv_root_tau
    )
    grad_inner = (grad_active * slope).astype(jnp.bfloat16)
    grad_w_one = jnp.einsum("rd,rf->df", second_in, grad_inner, preferred_element_type=jnp.float32)
    grad_bias_inner = jnp.sum(grad_inner, 0, dtype=jnp.float32)
    grad_second_in = jnp.einsum("rf,df->rd", grad_inner, w_one, preferred_element_type=jnp.float32)
    grad_gain_two, grad_bias_two, grad_middle_norm = norm_backward(
        grad_second_in, normed_two, factor_two, gain_two
    )
    grad_middle = grad_result + grad_middle_norm
    grad_mlp = jnp.concatenate([grad_w_one.reshape(-1), grad_w_two.reshape(-1)])
    grad_proj = grad_middle.astype(jnp.bfloat16)
    grad_w_out = jnp.einsum("rc,rd->cd", context_low, grad_proj, preferred_element_type=jnp.float32)
    grad_bias_out = jnp.sum(grad_proj, 0, dtype=jnp.float32)
    grad_context = jnp.einsum("rd,cd->rc", grad_proj, w_out, preferred_element_type=jnp.float32)
    grad_context = grad_context.astype(jnp.bfloat16).reshape(count, length, H, HD)
    probs = jnp.exp(masked_scores(query, keys, key_mask) - log_total)
    probs_again = probs.astype(jnp.bfloat16)
    grad_values = jnp.einsum(
        "shqk,sqhd->skhd", probs_again, grad_context, preferred_element_type=jnp.float32
    )
    grad_probs = jnp.einsum(
        "sqhd,skhd->shqk", grad_context, values, preferred_element_type=jnp.float32
    )
    inner_sum = jnp.sum(grad_probs * probs, -1, keepdims=True)
    grad_scores = (probs * (grad_probs - inner_sum)).astype(jnp.bfloat16)
    grad_query = (
        jnp.einsum("shqk,skhd->sqhd", grad_scores, keys, preferred_element_type=jnp.float32) * scale
    )
    grad_keys = (
        jnp.einsum("shqk,sqhd->skhd", grad_scores, query, preferred_element_type=jnp.float32)
        * scale
    )
    grad_qkv = (
        jnp.stack([grad_query, grad_keys, grad_values], 2)
        .reshape(total_rows, 3 * D)
        .astype(jnp.bfloat16)
    )
    grad_w_qkv = jnp.einsum("rd,re->de", first_in, grad_qkv, preferred_element_type=jnp.float32)
    grad_bias_qkv = jnp.sum(grad_qkv, 0, dtype=jnp.float32)
    grad_first_in = jnp.einsum("re,de->rd", grad_qkv, w_qkv, preferred_element_type=jnp.float32)
    grad_gain_one, grad_bias_one, grad_rows_norm = norm_backward(
        grad_first_in, normed_one, factor_one, gain_one
    )
    grad_rows = grad_middle + grad_rows_norm
    grad_samples = grad_rows.reshape(count, length, D).astype(jnp.bfloat16)
    grad_attn = jnp.concatenate([grad_w_qkv.reshape(-1), grad_w_out.reshape(-1)])
    grad_small = jnp.concatenate(
        [
            grad_gain_one,
            grad_bias_one,
            grad_bias_qkv[:D],
            grad_bias_qkv[2 * D :],
            grad_bias_out,
            grad_gain_two,
            grad_bias_two,
            grad_bias_inner,
            grad_bias_outer,
        ]
    )
    summed_attn, summed_mlp, summed_small = (
        scatter_sum(grad_attn),
        scatter_sum(grad_mlp),
        lax.psum_scatter(grad_small, ("wide", "narrow"), scatter_dimension=0, tiled=True),
    )
    new_attn, new_first_attn, new_second_attn = adamw(
        master_attn, first_attn, second_attn, summed_attn, 0.1, rate_matrix
    )
    new_mlp, new_first_mlp, new_second_mlp = adamw(
        master_mlp, first_mlp, second_mlp, summed_mlp, 0.1, rate_matrix
    )
    new_small, new_first_small, new_second_small = adamw(
        master_small, first_small, second_small, summed_small, 0.0, rate_small
    )
    return (
        output,
        grad_samples,
        new_attn,
        new_first_attn,
        new_second_attn,
        new_mlp,
        new_first_mlp,
        new_second_mlp,
        new_small,
        new_first_small,
        new_second_small,
    )


bf16 = jnp.bfloat16
f32 = jnp.float32
BLOCK = 256
BIN = 128
AXES = ("wide", "narrow")
ROW = 128
SMALL_ROWS = 72


def place_of(i):
    wide, z = divmod(i, 4)
    return wide // 4, (wide // 2) % 2, wide % 2, z


def index_of(y, x, c, z):
    return ((y * 2 + x) * 2 + c) * 4 + z


def pairs_of(move):
    return [(i, index_of(*move(*place_of(i)))) for i in range(32)]


TO_X = pairs_of(lambda y, x, c, z: (y, 1 - x, c, z))
TO_Y = pairs_of(lambda y, x, c, z: (1 - y, x, c, z))
TO_CORE = pairs_of(lambda y, x, c, z: (y, x, 1 - c, z))
TO_Z = [pairs_of(lambda y, x, c, z, k=k: (y, x, c, z ^ k)) for k in range(4)]


def send(value, pairs):
    return lax.ppermute(value, AXES, pairs)


def dot(a, b, dims=((1,), (0,))):
    return lax.dot_general(a, b, (dims, ((), ())), preferred_element_type=f32)


def at_rows(ref, start, size):
    return ref[pl.ds(start, size), :]


def attn_block(core, j):
    return (j // 3) * 6 + 3 * core + j % 3


def mlp_block(core, j):
    return (j // 6) * 12 + 6 * core + j % 6


def shifted(idx, vector, out):
    lane = lax.broadcasted_iota(jnp.int32, (3, ROW), 1)
    out[...] = jnp.zeros(out.shape, f32)
    for k in range(4):

        @pl.when(idx[4] == k)
        def _():
            turned = pltpu.roll(vector[...], 32 * k, 1) if k else vector[...]
            at = 2 * k
            out[at : at + 3, :] = jnp.where(lane >= 32 * k, turned, 0.0)
            if k:
                out[at + 1 : at + 4, :] += jnp.where(lane < 32 * k, turned, 0.0)


def cut_masters(idx, attn, mlp, small, keep_a, send_a, keep_m, send_m, place, half_a, half_m):
    wide, core = idx[0], idx[3]

    @pl.when(wide < 6)
    def _():
        for c in range(2):
            for j in range(9):
                rows = attn[pl.ds(attn_block(c, j), 32, stride=18), :]
                half_a[c, j * 32 : (j + 1) * 32, :] = rows.astype(bf16)

    @pl.when(wide >= 6)
    def _():
        for j in range(6):
            rows = attn[pl.ds(j, 96, stride=6), :]
            half_a[j // 3, (j % 3) * 96 : (j % 3 + 1) * 96, :] = rows.astype(bf16)

    @pl.when(wide < 4)
    def _():
        for c in range(2):
            for j in range(12):
                rows = mlp[pl.ds(mlp_block(c, j), 48, stride=24), :]
                half_m[c, j * 48 : (j + 1) * 48, :] = rows.astype(bf16)

    @pl.when(wide >= 4)
    def _():
        for j in range(6):
            rows = mlp[pl.ds(j, 192, stride=6), :]
            half_m[j // 3, (j % 3) * 192 : (j % 3 + 1) * 192, :] = rows.astype(bf16)

    first_a = jnp.where(wide < 6, core, 0)
    first_m = jnp.where(wide < 4, core, 0)
    keep_a[0:288, :] = half_a[first_a]
    send_a[0:288, :] = half_a[1 - first_a]
    keep_m[...] = half_m[first_m]
    send_m[...] = half_m[1 - first_m]
    shifted(idx, small, place)
    keep_a[288:304, :] = place[...].astype(bf16)
    send_a[288:304, :] = place[...].astype(bf16)


def pack_rows(idx, vis_own, vis_other, x_own, x_other, cot_own, cot_other, x_out, cot_out, meta, fill):
    core = idx[3]
    for b in range(16):
        fill[b] = 0
    bins = jnp.int32(0)
    for s in range(16):
        mine = core == s // 8
        seen = jnp.where(mine, vis_own[s % 8], vis_other[s % 8])
        need = ((seen + 15) >> 4) << 4
        chosen = jnp.int32(15)
        for b in reversed(range(s + 1)):
            chosen = jnp.where(fill[b] + need <= BIN, b, chosen)
        start = chosen * BIN + fill[chosen]
        fill[chosen] = fill[chosen] + need
        bins = jnp.maximum(bins, chosen + 1)
        meta[8 + s] = start
        meta[24 + s] = seen
    blocks = (bins + 1) >> 1
    meta[0] = blocks

    def clear(b, carry):
        at = pl.ds(pl.multiple_of(b * BLOCK, BLOCK), BLOCK)
        x_out[at, :] = jnp.zeros((BLOCK, D), bf16)
        cot_out[at, :] = jnp.zeros((BLOCK, D), bf16)
        return carry

    lax.fori_loop(0, blocks, clear, 0)
    row = lax.broadcasted_iota(jnp.int32, (16, D), 0)
    for s in range(16):
        start, seen = meta[8 + s], meta[24 + s]

        def fetch(x_in, cot_in):
            def chunk(k, carry):
                src = pl.ds(pl.multiple_of(k * 16, 16), 16)
                dst = pl.ds(pl.multiple_of(start + k * 16, 16), 16)
                x_out[dst, :] = x_in[s % 8, src, :]
                grad = cot_in[s % 8, src, :].astype(f32)
                cot_out[dst, :] = jnp.where(row + k * 16 < seen, grad, 0.0).astype(bf16)
                return carry

            lax.fori_loop(0, (seen + 15) >> 4, chunk, 0)

        @pl.when(core == s // 8)
        def _():
            fetch(x_own, cot_own)

        @pl.when(core != s // 8)
        def _():
            fetch(x_other, cot_other)


def owner_of(idx, column, k):
    y, x, z = idx[1], idx[2], idx[4]
    yy = 1 - y if column >= 2 else y
    xx = 1 - x if column % 2 else x
    return yy * 2 + xx, jnp.bitwise_xor(z, k)


def pair_of(n):
    return n // 4 * 2 + n % 2


def core_of(idx, part):
    return 1 - idx[3] if part else idx[3]


def lanes_of(small, first, count):
    rows = [small[q // 9, q % 9 : q % 9 + 1, :] for q in range(first, first + count)]
    return jnp.concatenate(rows, axis=1)


def same_sample(meta, which):
    lane = lax.broadcasted_iota(jnp.int32, (8, BIN), 1)
    line = lax.broadcasted_iota(jnp.int32, (BIN, BIN), 0)
    of_key = jnp.full((8, BIN), -2, jnp.int32)
    of_query = jnp.full((BIN, BIN), -1, jnp.int32)
    for s in range(16):
        start = meta[8 + s] - which * BIN
        stop = start + meta[24 + s]
        of_key = jnp.where((lane >= start) & (lane < stop), s, of_key)
        of_query = jnp.where((line >= start) & (line < stop), s, of_query)
    return of_query == of_key[0:1, :]


def halves(pair):
    lane = lax.broadcasted_iota(jnp.int32, pair.shape, 1)
    wide = pair.astype(f32)
    return jnp.concatenate(
        [jnp.where(lane < HD, wide, 0.0), jnp.where(lane >= HD, wide, 0.0)], axis=0
    ).astype(bf16)


def probabilities(query, keys, mask):
    scores = dot(halves(query), keys, ((1,), (1,))) * (1.0 / math.sqrt(HD))
    scores = jnp.where(mask, scores, -1e30)
    expo = jnp.exp(scores - jnp.max(scores, -1, keepdims=True))
    return expo * (1.0 / jnp.sum(expo, -1, keepdims=True))


def probabilities_by_key(both, keys, mask):
    scores = dot(keys, both, ((1,), (1,))) * (1.0 / math.sqrt(HD))
    scores = jnp.where(mask, scores, -1e30)
    expo = jnp.exp(scores - jnp.max(scores, 0, keepdims=True))
    return expo * (1.0 / jnp.sum(expo, 0, keepdims=True))


def one_above_other(wide):
    return jnp.concatenate([wide[:, :BIN], wide[:, BIN:]], axis=0)


def side_by_side(stacked):
    return jnp.concatenate([stacked[:BIN], stacked[BIN:]], axis=1)


def attn_forward(phase, meta, idx, x_ref, *refs):
    pairs = refs[:8]
    qkv_ref, context_ref, part_ref, w_qkv, w_out, vecs, shift, inner_bias, small = refs[8:]

    if phase == 0:
        small[...] = jnp.zeros(small.shape, f32)
        for n in range(16):
            piece = pairs[pair_of(n)].at[n % 4 // 2]
            chip, z = owner_of(idx, n // 4, n % 4)

            @pl.when(chip < 3)
            def _():
                for part in range(2):
                    owner = (chip * 2 + core_of(idx, part)) * 4 + z
                    to = pl.ds(pl.multiple_of(owner * 32, 32), 32)
                    for j in range(9):
                        at = part * 288 + j * 32
                        w_qkv[to, j * ROW : (j + 1) * ROW] = piece[at : at + 32, :]

            @pl.when(chip == 3)
            def _():
                to = pl.ds(pl.multiple_of(z * 96, 32), 96)
                for j in range(6):
                    w_out[to, j * ROW : (j + 1) * ROW] = piece[j * 96 : (j + 1) * 96, :]

            for part in range(2):
                group = chip * 2 + core_of(idx, part)
                at = 576 + part * 16
                small[group] = small[group] + piece[at : at + 16, :].astype(f32)
        for n, first in enumerate((0, 6, 24, 30, 36, 66)):
            vecs[n : n + 1, :] = lanes_of(small, first, 6)
        vecs[6:8, :] = jnp.zeros((2, D), f32)
        own = idx[3] == 0
        query_bias = jnp.where(own, lanes_of(small, 12, 3), lanes_of(small, 15, 3))
        value_bias = jnp.where(own, lanes_of(small, 18, 3), lanes_of(small, 21, 3))
        shift[...] = jnp.concatenate([query_bias, jnp.zeros((1, D // 2), f32), value_bias], axis=1)
        low = jnp.where(own, lanes_of(small, 42, 6), lanes_of(small, 48, 6))
        high = jnp.where(own, lanes_of(small, 54, 6), lanes_of(small, 60, 6))
        inner_bias[...] = jnp.concatenate([low, high], axis=1)

    if phase == 1:
        normed, _ = standard(x_ref[...].astype(f32))
        first_in = (normed * vecs[0:1, :] + vecs[1:2, :]).astype(bf16)
        qkv_ref[...] = (dot(first_in, w_qkv[...]) + shift[...]).astype(bf16)
        for b in range(BLOCK // BIN):
            mask = same_sample(meta, pl.program_id(0) * (BLOCK // BIN) + b)
            mask = jnp.concatenate([mask, mask], axis=0)
            rows = slice(b * BIN, (b + 1) * BIN)
            for h in range(3):
                query, keys, values = (
                    qkv_ref[rows, (3 * t + h) * ROW : (3 * t + h + 1) * ROW] for t in range(3)
                )
                probs = probabilities(query, keys, mask).astype(bf16)
                context = dot(side_by_side(probs), halves(values))
                context_ref[rows, h * ROW : (h + 1) * ROW] = context.astype(bf16)
        part_ref[...] = dot(context_ref[...], w_out[...]).astype(bf16)


ERF_TOP = (0.00022905065861350646, 0.0034082910107109506, 0.050955695062380861, 0.18520832239976145, 1.128379143519084)
ERF_BOTTOM = (-1.1791602954361697e-7, 0.000023547966471313185, 0.0010179625278914885, 0.014070470171167667,
              0.11098505178285362, 0.49746925110067538, 1.0)


def error_function(v):
    v = jnp.clip(v, -3.832506856900711, 3.832506856900711)
    square = v * v
    top, bottom = jnp.full_like(v, ERF_TOP[0]), jnp.full_like(v, ERF_BOTTOM[0])
    for a in ERF_TOP[1:]:
        top = top * square + a
    for b in ERF_BOTTOM[1:]:
        bottom = bottom * square + b
    return v * top / bottom


def middle_of(x_ref, part_own, part_other, vecs):
    parts = part_own[...].astype(f32) + part_other[...].astype(f32)
    return x_ref[...].astype(f32) + parts + vecs[2:3, :]


def mlp_both(phase, meta, idx, x_ref, part_own, part_other, cot_ref, vecs, inner_bias, *refs):
    pieces = refs[:16]
    (active_ref, back_ref, w_two, sums, inner_sum) = refs[16:21]
    outs = refs[21:29]
    w_one, acc_one, acc_two = refs[29:]

    if phase == 0:
        acc_one[...] = jnp.zeros(acc_one.shape, f32)
        acc_two[...] = jnp.zeros(acc_two.shape, f32)
        sums[...] = jnp.zeros(sums.shape, f32)
        inner_sum[...] = jnp.zeros(inner_sum.shape, f32)
        for n, piece in enumerate(pieces):
            chip, z = owner_of(idx, n // 4, n % 4)

            @pl.when(chip < 2)
            def _():
                for part in range(2):
                    owner = (chip * 2 + core_of(idx, part)) * 4 + z
                    to = pl.ds(pl.multiple_of(owner * 48, 16), 48)
                    for j in range(12):
                        at = part * 576 + j * 48
                        w_one[to, j * ROW : (j + 1) * ROW] = piece[at : at + 48, :]

            @pl.when(chip >= 2)
            def _():
                to = pl.ds(pl.multiple_of((chip - 2) * D + z * 192, 64), 192)
                for j in range(6):
                    w_two[to, j * ROW : (j + 1) * ROW] = piece[j * 192 : (j + 1) * 192, :]

    if phase == 1:
        normed, _ = standard(middle_of(x_ref, part_own, part_other, vecs))
        second_in = (normed * vecs[3:4, :] + vecs[4:5, :]).astype(bf16)
        grad = cot_ref[...]
        back = jnp.zeros((BLOCK, D), f32)
        for n in range(2):
            cols = slice(n * D, (n + 1) * D)
            inner = dot(second_in, w_one[:, cols]) + inner_bias[:, cols]
            bell = 0.5 * (1.0 + error_function(inner * inv_root_two))
            active = (inner * bell).astype(bf16)
            active_ref[:, cols] = active
            slope = bell + inner * jnp.exp(-0.5 * inner * inner) * inv_root_tau
            grad_inner = (dot(grad, w_two[cols, :], ((1,), (1,))) * slope).astype(bf16)
            acc_two[cols, :] += dot(active, grad, ((0,), (0,)))
            acc_one[:, cols] += dot(second_in, grad_inner, ((0,), (0,)))
            inner_sum[:, cols] += jnp.sum(grad_inner.astype(f32), 0, keepdims=True)
            back = back + dot(grad_inner, w_one[:, cols], ((1,), (1,)))
        back_ref[...] = back.astype(bf16)
        sums[0:1, :] += jnp.sum(back * normed, 0, keepdims=True)
        sums[1:2, :] += jnp.sum(back, 0, keepdims=True)
        sums[2:3, :] += jnp.sum(grad.astype(f32), 0, keepdims=True)

    if phase == 2:
        for n in range(16):
            chip, z = owner_of(idx, n // 4, n % 4)
            out, k = outs[pair_of(n)], n % 4 // 2

            @pl.when(chip < 2)
            def _():
                for part in range(2):
                    owner = (chip * 2 + core_of(idx, part)) * 4 + z
                    rows = pl.ds(pl.multiple_of(owner * 48, 16), 48)
                    for j in range(12):
                        at = part * 576 + j * 48
                        out[k, at : at + 48, :] = acc_one[rows, j * ROW : (j + 1) * ROW].astype(bf16)

            @pl.when(chip >= 2)
            def _():
                rows = pl.ds(pl.multiple_of((chip - 2) * D + z * 192, 64), 192)
                for j in range(6):
                    out[k, j * 192 : (j + 1) * 192, :] = acc_two[rows, j * ROW : (j + 1) * ROW].astype(bf16)


def hand_on(phase, meta, idx, source, target):
    if phase == 1:
        target[...] = source[...]


def mlp_out(phase, meta, idx, active_ref, w_two, part_ref):
    if phase == 1:
        part_ref[...] = dot(active_ref[...], w_two[...]).astype(bf16)


def middle_backward(phase, meta, idx, x_ref, part_own, part_other, cot_ref, back_own, back_other, context_ref, w_out, vecs,
                    grad_ref, grad_context_ref, acc_out, sums):
    if phase == 0:
        acc_out[...] = jnp.zeros(acc_out.shape, f32)
        sums[...] = jnp.zeros(sums.shape, f32)

    if phase == 1:
        normed, factor = standard(middle_of(x_ref, part_own, part_other, vecs))
        scaled = (back_own[...].astype(f32) + back_other[...].astype(f32)) * vecs[3:4, :]
        through = scaled - jnp.mean(scaled, -1, keepdims=True)
        through = through - normed * jnp.mean(scaled * normed, -1, keepdims=True)
        grad_middle = cot_ref[...].astype(f32) + factor * through
        grad_ref[...] = grad_middle
        grad_proj = grad_middle.astype(bf16)
        acc_out[...] += dot(context_ref[...], grad_proj, ((0,), (0,)))
        sums[0:1, :] += jnp.sum(grad_proj.astype(f32), 0, keepdims=True)
        grad_context_ref[...] = dot(grad_proj, w_out[...], ((1,), (1,))).astype(bf16)


def heads_backward(phase, meta, idx, qkv_ref, grad_context_ref, grads):
    if phase == 1:
        scale = 1.0 / math.sqrt(HD)
        for b in range(BLOCK // BIN):
            mask = same_sample(meta, pl.program_id(0) * (BLOCK // BIN) + b)
            mask = jnp.concatenate([mask, mask], axis=1)
            rows = slice(b * BIN, (b + 1) * BIN)
            for h in range(3):
                cols = [slice((3 * t + h) * ROW, (3 * t + h + 1) * ROW) for t in range(3)]
                query, keys, values = (qkv_ref[rows, cols[t]] for t in range(3))
                both = halves(query)
                probs = probabilities_by_key(both, keys, mask)
                grad_out = halves(grad_context_ref[rows, h * ROW : (h + 1) * ROW])
                grad_values = dot(probs.astype(bf16), grad_out)
                grad_probs = dot(values, grad_out, ((1,), (1,)))
                total = jnp.sum(grad_probs * probs, 0, keepdims=True)
                grad_scores = (probs * (grad_probs - total)).astype(bf16)
                grad_keys = dot(grad_scores, both) * scale
                grad_query = dot(one_above_other(grad_scores), halves(keys), ((0,), (0,))) * scale
                grads[rows, cols[0]] = grad_query.astype(bf16)
                grads[rows, cols[1]] = grad_keys.astype(bf16)
                grads[rows, cols[2]] = grad_values.astype(bf16)


def first_backward(phase, meta, idx, x_ref, grads, w_qkv, acc_out, vecs, sums_in, inner_sum, sums_out, *refs):
    back_ref = refs[0]
    outs = refs[1:9]
    acc_qkv, sums, small = refs[9:]

    if phase == 0:
        acc_qkv[...] = jnp.zeros(acc_qkv.shape, f32)
        sums[...] = jnp.zeros(sums.shape, f32)

    if phase == 1:
        normed, _ = standard(x_ref[...].astype(f32))
        first_in = (normed * vecs[0:1, :] + vecs[1:2, :]).astype(bf16)
        grad_qkv = grads[...]
        acc_qkv[...] += dot(first_in, grad_qkv, ((0,), (0,)))
        back = dot(grad_qkv, w_qkv[...], ((1,), (1,)))
        back_ref[...] = back.astype(bf16)
        sums[0:1, :] += jnp.sum(back * normed, 0, keepdims=True)
        sums[1:2, :] += jnp.sum(back, 0, keepdims=True)
        sums[3:4, 0 : D // 2] += jnp.sum(grad_qkv[:, 0 : D // 2].astype(f32), 0, keepdims=True)
        sums[3:4, D // 2 : D] += jnp.sum(grad_qkv[:, D : D + D // 2].astype(f32), 0, keepdims=True)

    if phase == 2:
        small[...] = jnp.zeros(small.shape, f32)
        once = jnp.where(idx[3] == 0, 1.0, 0.0)

        def put(at, rows):
            for j in range(rows.shape[1] // ROW):
                q = at + j
                small[q // 9, q % 9 : q % 9 + 1, :] = rows[:, j * ROW : (j + 1) * ROW]

        put(0, sums[0:1, :])
        put(6, sums[1:2, :])
        put(24, sums_out[0:1, :] * once)
        put(30, sums_in[0:1, :])
        put(36, sums_in[1:2, :])
        put(66, sums_in[2:3, :] * once)
        for c in range(2):

            @pl.when(idx[3] == c)
            def _():
                put(12 + 3 * c, sums[3:4, 0 : D // 2])
                put(18 + 3 * c, sums[3:4, D // 2 : D])
                put(42 + 6 * c, inner_sum[:, 0:D])
                put(54 + 6 * c, inner_sum[:, D : 2 * D])

        for n in range(16):
            chip, z = owner_of(idx, n // 4, n % 4)
            out, k = outs[pair_of(n)], n % 4 // 2

            @pl.when(chip < 3)
            def _():
                for part in range(2):
                    owner = (chip * 2 + core_of(idx, part)) * 4 + z
                    rows = pl.ds(pl.multiple_of(owner * 32, 32), 32)
                    for j in range(9):
                        at = part * 288 + j * 32
                        out[k, at : at + 32, :] = acc_qkv[rows, j * ROW : (j + 1) * ROW].astype(bf16)

            @pl.when(chip == 3)
            def _():
                rows = pl.ds(pl.multiple_of(z * 96, 32), 96)
                for j in range(6):
                    out[k, j * 96 : (j + 1) * 96, :] = acc_out[rows, j * ROW : (j + 1) * ROW].astype(bf16)

            for part in range(2):
                group = chip * 2 + core_of(idx, part)
                out[k, 576 + part * 16 : 592 + part * 16, :] = small[group].astype(bf16)


def finish_rows(phase, meta, idx, x_ref, part_own, part_other, out_own, out_other, grad_ref, back_own, back_other, vecs,
                output, grad_samples, packed_out, packed_grad):
    if phase == 1:
        at = pl.ds(pl.multiple_of(pl.program_id(0) * BLOCK, BLOCK), BLOCK)
        parts = out_own[...].astype(f32) + out_other[...].astype(f32)
        result = middle_of(x_ref, part_own, part_other, vecs) + parts + vecs[5:6, :]
        packed_out[at, :] = result.astype(bf16)
        normed, factor = standard(x_ref[...].astype(f32))
        scaled = (back_own[...].astype(f32) + back_other[...].astype(f32)) * vecs[0:1, :]
        through = scaled - jnp.mean(scaled, -1, keepdims=True)
        through = through - normed * jnp.mean(scaled * normed, -1, keepdims=True)
        packed_grad[at, :] = (grad_ref[...] + factor * through).astype(bf16)

    if phase == 2:
        output[...] = jnp.zeros(output.shape, bf16)
        grad_samples[...] = jnp.zeros(grad_samples.shape, bf16)
        row = lax.broadcasted_iota(jnp.int32, (16, D), 0)
        for s in range(8):
            start, seen = meta[8 + idx[3] * 8 + s], meta[24 + idx[3] * 8 + s]

            def chunk(k, carry):
                src = pl.ds(pl.multiple_of(start + k * 16, 16), 16)
                dst = pl.ds(pl.multiple_of(k * 16, 16), 16)
                keep = row + k * 16 < seen
                for packed, out in ((packed_out, output), (packed_grad, grad_samples)):
                    out[s, dst, :] = jnp.where(keep, packed[src, :].astype(f32), 0.0).astype(bf16)
                return carry

            lax.fori_loop(0, (seen + 15) >> 4, chunk, 0)


def update_refs(master, first, second, grad, outs, decay, step_rate):
    for out, new in zip(outs, adamw(master[...], first[...], second[...], grad, decay, step_rate)):
        out[...] = new


def step_mlp(idx, master, first, second, keep, mine, other, new, new_first, new_second, half, grad):
    wide, core = idx[0], idx[3]
    at = jnp.where(wide < 4, core, 0)
    half[at] = keep[...]

    @pl.when(wide < 4)
    def _():
        half[1 - at] = other[...]

    @pl.when(wide >= 4)
    def _():
        half[1 - at] = mine[...]

    @pl.when(wide < 4)
    def _():
        for c in range(2):
            for j in range(12):
                grad[pl.ds(mlp_block(c, j), 48, stride=24), :] = half[c, j * 48 : (j + 1) * 48, :]

    @pl.when(wide >= 4)
    def _():
        for j in range(6):
            grad[pl.ds(j, 192, stride=6), :] = half[j // 3, (j % 3) * 192 : (j % 3 + 1) * 192, :]

    update_refs(master, first, second, grad[...], (new, new_first, new_second), 0.1, rate_matrix)


def step_attn(idx, master, first, second, keep, mine, other, master_s, first_s, second_s, keep_s, other_s,
              new, new_first, new_second, new_s, new_first_s, new_second_s, half, grad, place, small_grad):
    wide, core = idx[0], idx[3]
    at = jnp.where(wide < 6, core, 0)
    half[at] = keep[...]

    @pl.when(wide < 6)
    def _():
        half[1 - at] = other[...]

    @pl.when(wide >= 6)
    def _():
        half[1 - at] = mine[...]

    @pl.when(wide < 6)
    def _():
        for c in range(2):
            for j in range(9):
                grad[pl.ds(attn_block(c, j), 32, stride=18), :] = half[c, j * 32 : (j + 1) * 32, :]

    @pl.when(wide >= 6)
    def _():
        for j in range(6):
            grad[pl.ds(j, 96, stride=6), :] = half[j // 3, (j % 3) * 96 : (j % 3 + 1) * 96, :]

    update_refs(master, first, second, grad[...], (new, new_first, new_second), 0.1, rate_matrix)
    place[...] = keep_s[...] + other_s[...]
    lane = lax.broadcasted_iota(jnp.int32, (3, ROW), 1)
    for k in range(4):

        @pl.when(idx[4] == k)
        def _():
            at = 2 * k
            both = jnp.where(lane >= 32 * k, place[at : at + 3, :], place[at + 1 : at + 4, :])
            small_grad[...] = pltpu.roll(both, ROW - 32 * k, 1) if k else both

    update_refs(master_s, first_s, second_s, small_grad[...], (new_s, new_first_s, new_second_s), 0.0, rate_small)


def plus(*terms):
    return sum(t.astype(f32) for t in terms)


def nothing(idx, out):
    out[...] = jnp.zeros(out.shape, f32)


def lay_attn(idx, keep, mine, other, piece):
    piece[0:288, :] = keep[0:288, :]
    piece[576:592, :] = keep[288:304, :]
    piece[592:608, :] = other[288:304, :]

    @pl.when(idx[0] < 6)
    def _():
        piece[288:576, :] = other[0:288, :]

    @pl.when(idx[0] >= 6)
    def _():
        piece[288:576, :] = mine[0:288, :]


def lay_mlp(idx, keep, mine, other, piece):
    piece[0:576, :] = keep[...]

    @pl.when(idx[0] < 4)
    def _():
        piece[576:1152, :] = other[...]

    @pl.when(idx[0] >= 4)
    def _():
        piece[576:1152, :] = mine[...]


def lay_out(*refs):
    at = 0
    for ref in refs[:-1]:
        refs[-1][at : at + ref.shape[0], :] = ref[...]
        at += ref.shape[0]


def pair_up(first, second, pair):
    pair[0] = first[...]
    pair[1] = second[...]


def add_low(*refs):
    refs[-1][...] = plus(*(r[...] for r in refs[:-1])).astype(bf16)


def add_near_far(*refs):
    terms, (near, far) = refs[:-2], refs[-2:]
    near[...] = plus(*(r[0] for r in terms))
    far[...] = plus(*(r[1] for r in terms)).astype(bf16)


def add_last(half, near, other, *outs):
    total = near[...] + other[...].astype(f32)
    outs[0][...] = total[:half]
    outs[1][...] = total[half : 2 * half]
    for n, out in enumerate(outs[2:]):
        out[...] = total[2 * half + 16 * n : 2 * half + 16 * n + 16]


SENDS = {
    "cv": ("visible", TO_CORE),
    "cs": ("samples", TO_CORE),
    "cc": ("cotangent", TO_CORE),
    "sa": ("send_a", TO_CORE),
    "sm": ("send_m", TO_CORE),
    "z2a": ("pa", TO_Z[2]),
    "zOa": ("Ea", TO_Z[1]),
    "xEa": ("Ea", TO_X),
    "yEa": ("Ea", TO_Y),
    "xOa": ("zOa", TO_X),
    "yOa": ("zOa", TO_Y),
    "dEa": ("yEa", TO_X),
    "dOa": ("xOa", TO_Y),
    "z1m": ("pm", TO_Z[1]),
    "z2m": ("pm2", TO_Z[2]),
    "z3m": ("z2m", TO_Z[1]),
    "x0m": ("pm", TO_X),
    "y0m": ("pm", TO_Y),
    "x1m": ("h1m", TO_X),
    "y1m": ("h1m", TO_Y),
    "x2m": ("z2m", TO_X),
    "y2m": ("z2m", TO_Y),
    "x3m": ("z3m", TO_X),
    "y3m": ("z3m", TO_Y),
    "d0m": ("h0m", TO_X),
    "d1m": ("d0m", TO_Z[1]),
    "d2m": ("x2m", TO_Y),
    "d3m": ("d2m", TO_Z[1]),
    "pt": ("part", TO_CORE),
    "bk": ("back", TO_CORE),
    "ot": ("out_part", TO_CORE),
    "fb": ("first_back_2", TO_CORE),
}
for group in "am":
    SENDS |= {
        "rE" + group: ("dE" + group + "_grad", TO_X),
        "rO" + group: ("dO" + group + "_grad", TO_Y),
        "pE" + group: ("xE" + group + "_grad", TO_X),
        "pO" + group: ("yO" + group + "_grad", TO_Y),
        "qE" + group: ("aE" + group, TO_Y),
        "qO" + group: ("aO" + group, TO_X),
        "wO" + group: ("so" + group, TO_Z[1]),
        "w2" + group: ("far" + group, TO_Z[2]),
        "g" + group: ("other" + group, TO_CORE),
    }
SENDS["gs"] = ("other_small", TO_CORE)
PAIR_NAMES = ("E{}_grad", "O{}_grad", "xE{}_grad", "xO{}_grad", "yE{}_grad", "yO{}_grad", "dE{}_grad", "dO{}_grad")

IN_HBM = ("first_back", "out_part", "grad_context", "output")
AFTER = {
    "pa": ("cs", "cc", "cv"),
    "pm": ("pa",),
    "Ea": ("meta",),
    "pm2": ("Ea",),
    "h1m": ("xOa",),
    "h0m": ("xOa",),
    "fwd": ("x0m", "y0m", "z2m"),
    "there": ("x3m", "y3m", "d1m", "d2m", "d3m", "x2m", "d0m", "vecs"),
    "mlp": ("there",),
    "bw1": ("out_part",),
    "aEm": ("grad_context",),
    "aOm": ("grad_context",),
    "bw2": ("aEm", "aOm"),
    "bw3": ("ot",),
    "som": ("first_back", "qEm", "pEm"),
    "hand": ("som",),
    "aEa": ("farm",),
    "fin": ("soa",),
    "sza": ("output",),
    "sua": ("done_m",),
}

ORDER = (
    "+cv", "+cs", "+cc", "=cut", "+sa", "+sm", "=pack", "=pa", "+z2a", "=pm", "+z1m", "+x0m", "+y0m",
    "=Ea", "=pm2", "+z2m", "+zOa", "+xEa", "+yEa", "+dEa", "+yOa", "+z3m", "+xOa", "=h1m", "=h0m", "+x1m", "+y1m", "+y2m", "+x2m",
    "+d0m", "+dOa", "+y3m", "+x3m", "+d2m", "=fwd", "+pt", "+d1m", "+d3m", "=there",
    "=mlp", "+rEm", "+rOm", "+bk", "=mout", "+ot", "=bw1", "=aEm", "=aOm", "+qOm", "+qEm", "+pEm", "+pOm", "=bw2",
    "=bw3", "+rEa", "+rOa", "=som", "=hand", "+fb", "+wOm", "=szm", "+w2m", "=aEa", "=aOa", "+qOa", "+qEa", "+pEa", "+pOa",
    "=soa", "+wOa", "=fin", "=sum", "+gm", "=om", "=sza", "+w2a", "=sua", "+ga", "+gs", "=oa",
)


SMEM = pl.BlockSpec(memory_space=pltpu.SMEM)
VMEM = pl.BlockSpec(memory_space=pltpu.VMEM)
ANY = pl.BlockSpec(memory_space=pl.ANY)


def array(shape, dtype=bf16):
    return jax.ShapeDtypeStruct(shape, dtype)


def large(shape, dtype=bf16):
    return pltpu.HBM(shape, dtype)


def params(mib):
    return pltpu.CompilerParams(vmem_limit_bytes=mib << 20)


SCALE = 10**9
COSTS = {
    "attn_forward": 11, "mlp_both": 23, "mlp_out": 20, "middle_backward": 8, "heads_backward": 25, "first_backward": 25,
    "finish_rows": 8, "pack_rows": 6, "all_there": 60,
}


def cost(name):
    return pl.CostEstimate(flops=COSTS.get(name, 1) * SCALE, bytes_accessed=1, transcendentals=0)


def in_hbm(value):
    return pltpu.with_memory_space_constraint(value, pltpu.HBM)


def full(value):
    return pl.BlockSpec(value.shape, lambda i: (0,) * len(value.shape))


def over_blocks(body, rows_in, fixed_in, rows_out, fixed_out, scratch, mib, name, after=()):
    many = rows_in + [w for w, _, _ in rows_out]
    n_in, n_out = len(rows_in), len(rows_out)

    def kernel(meta, idx, *refs):
        refs = refs[: n_in + fixed_in] + refs[n_in + fixed_in + len(after) :]
        rows, fixed, lines, rest = (
            refs[:n_in], refs[n_in : n_in + fixed_in], refs[n_in + fixed_in :][:n_out], refs[n_in + fixed_in + n_out :]
        )
        body(0, meta, idx, *rows, *fixed, *lines, *rest)

        def one(*blocks):
            body(1, meta, idx, *blocks[:n_in], *fixed, *blocks[n_in:], *rest)

        specs = [pl.BlockSpec((BLOCK, w), lambda i: (i, 0)) for w in many]
        pltpu.emit_pipeline(one, grid=(meta[0],), in_specs=specs[:n_in], out_specs=specs[n_in:])(*rows, *lines)
        body(2, meta, idx, *rows, *fixed, *lines, *rest)

    def called(meta, idx, *args):
        return pl.pallas_call(
            kernel,
            grid=(1,),
            in_specs=[SMEM, SMEM] + [ANY] * n_in + [full(a) for a in args[n_in:]] + [ANY] * len(after),
            out_specs=[ANY] * n_out + [full(a) for a in fixed_out],
            out_shape=[large((n, w), t) for w, t, n in rows_out] + fixed_out,
            scratch_shapes=scratch,
            compiler_params=params(mib),
            cost_estimate=cost(name),
            name=name,
        )(meta, idx, *args, *after)

    return called


def at_once(body, scalars, outs, scratch, mib, name, after=(), copied=False):
    def kernel(*refs):
        n = len(refs) - len(scratch) - len(outs) - len(after)
        body(*refs[:n], *refs[n + len(after) :])

    def called(*args):
        grid = {"grid": (1,)} if copied else {}
        blocks = [full(a) if copied else VMEM for a in args[scalars:]]
        arrays = [in_hbm(a) for a in args[scalars:]] if copied else args[scalars:]
        return pl.pallas_call(
            kernel,
            in_specs=[SMEM] * scalars + blocks + [ANY] * len(after),
            out_specs=[SMEM if a.dtype == jnp.int32 else full(a) if copied else VMEM for a in outs],
            out_shape=outs,
            scratch_shapes=scratch,
            compiler_params=params(mib),
            cost_estimate=cost(name),
            name=name,
            **grid,
        )(*args[:scalars], *arrays, *after)

    return called


def on_core(
    samples,
    cotangent,
    visible,
    master_attn,
    first_attn,
    second_attn,
    master_mlp,
    first_mlp,
    second_mlp,
    master_small,
    first_small,
    second_small,
):
    count, length, _ = samples.shape
    rows = 2 * count * length
    wide, z = lax.axis_index("wide"), lax.axis_index("narrow")
    idx = jnp.stack([wide, wide // 4, (wide // 2) % 2, wide % 2, z]).astype(jnp.int32)

    def lanes(flat):
        return flat.reshape(-1, ROW)

    def three_rows(vector):
        return lanes(jnp.pad(vector, (0, 3 * ROW - vector.shape[0])))

    half_a, half_m = (288, ROW), (576, ROW)
    shape_m, shape_a, shape_s = (1152, ROW), (576, ROW), (16, ROW)
    pair_a, pair_m = (2, 608, ROW), (2, 1152, ROW)

    def after(name):
        return tuple(in_hbm(v[n]) if n in IN_HBM else v[n] for n in AFTER.get(name, ()))

    v = {"visible": visible, "samples": samples, "cotangent": cotangent}

    def hbm(*names):
        return tuple(v[n] if n in SENDS else in_hbm(v[n]) for n in names)

    def cut():
        swap_a = (304, ROW)
        v["keep_a"], v["send_a"], v["keep_m"], v["send_m"] = at_once(
            cut_masters, 1, [array(swap_a), array(swap_a), array(half_m), array(half_m)],
            [pltpu.VMEM(shape_s, f32), pltpu.VMEM((2, *half_a), bf16), pltpu.VMEM((2, *half_m), bf16)], 8, "cut_masters", after("cut"), True,
        )(idx, lanes(master_attn), lanes(master_mlp), three_rows(master_small))

    def piece_a():
        v["pa"] = at_once(lay_attn, 1, [array((608, ROW))], [], 8, "piece_attn", after("pa"))(
            idx, v["keep_a"], v["send_a"], v["sa"]
        )[0]

    def even_a():
        v["Ea"] = at_once(
            pair_up, 0, [array(pair_a)], [], 8, "pair_up", after("Ea")
        )(v["pa"], v["z2a"])[0]

    def piece_m():
        v["pm"] = at_once(lay_mlp, 1, [array(shape_m)], [], 8, "piece_mlp", after("pm"))(
            idx, v["keep_m"], v["send_m"], v["sm"]
        )[0]

    def again_m():
        v["pm2"] = at_once(lay_out, 0, [array(shape_m)], [], 8, "piece_again", after("pm2"))(v["pm"])[0]

    def pack():
        v["x"], v["cot"], v["meta"] = at_once(
            pack_rows, 3, [large((rows, D)), large((rows, D)), array((64,), jnp.int32)],
            [pltpu.SMEM((16,), jnp.int32)], 32, "pack_rows", after("pack"),
        )(idx, visible, v["cv"], in_hbm(samples), v["cs"], in_hbm(cotangent), v["cc"])

    def forward():
        outs = [large((D, 3 * D // 2)), large((D // 2, D)), array((8, D), f32), array((1, 3 * D // 2), f32), array((1, FF // 2), f32)]
        (v["qkv"], v["context"], v["part"], v["w_qkv"], v["w_out"], v["vecs"], shift, v["inner_bias"]) = over_blocks(
            attn_forward, [D], 8, [(3 * D // 2, bf16, rows), (D // 2, bf16, rows), (D, bf16, rows)], outs,
            [pltpu.VMEM((8, 16, ROW), f32)], 24, "attn_forward", after("fwd"),
        )(v["meta"], idx, *hbm("x"), v["Ea"], *(v[n] for n in ("zOa", "xEa", "xOa", "yEa", "yOa", "dEa", "dOa")))

    def hold_1():
        v["h1m"] = at_once(lay_out, 0, [array(shape_m)], [], 8, "hold_first", after("h1m"))(v["z1m"])[0]

    def hold_0():
        v["h0m"] = at_once(lay_out, 0, [array(shape_m)], [], 8, "hold_own", after("h0m"))(v["y0m"])[0]

    def there():
        v["there"] = at_once(nothing, 1, [array((8, ROW), f32)], [], 4, "all_there", after("there"))(idx)[0]

    def middle():
        return hbm("x", "part", "pt")

    def mlp():
        pieces = [v["pm"] if c + k == "z0" else v[c + k + "m"] for c in "zxyd" for k in "0123"]
        done = over_blocks(
            mlp_both, [D] * 4, 18, [(FF // 2, bf16, rows), (D, bf16, rows)],
            [large((FF // 2, D)), array((8, D), f32), array((1, FF // 2), f32)] + [array(pair_m)] * 8,
            [pltpu.VMEM((D, FF // 2), bf16), pltpu.VMEM((D, FF // 2), f32), pltpu.VMEM((FF // 2, D), f32)],
            48, "mlp_both", after("mlp"),
        )(v["meta"], idx, *middle(), *hbm("cot"), v["vecs"], v["inner_bias"], *pieces)
        v["active"], v["back"], v["w_two"], v["sums"], v["inner_sum"] = done[:5]
        v.update(zip((n.format("m") for n in PAIR_NAMES), done[5:]))

    def out_rows():
        v["out_part"] = over_blocks(mlp_out, [FF // 2], 1, [(D, bf16, rows)], [], [], 16, "mlp_out", after("mout"))(
            v["meta"], idx, *hbm("active", "w_two")
        )[0]

    def backward_1():
        v["grad_middle"], v["grad_context"], v["acc_out"], v["sums_out"] = over_blocks(
            middle_backward, [D] * 6 + [D // 2], 2, [(D, f32, rows), (D // 2, bf16, rows)],
            [large((D // 2, D), f32), array((8, D), f32)], [], 16, "middle_backward", after("bw1"),
        )(v["meta"], idx, *middle(), *hbm("cot", "back", "bk", "context", "w_out"), v["vecs"])

    def backward_2():
        v["grad_qkv"] = over_blocks(
            heads_backward, [3 * D // 2, D // 2], 0, [(3 * D // 2, bf16, rows)], [], [], 16, "heads_backward", after("bw2"),
        )(v["meta"], idx, *hbm("qkv", "grad_context"))[0]

    def backward_3():
        done = over_blocks(
            first_backward, [D, 3 * D // 2], 6, [(D, bf16, rows)], [array(pair_a)] * 8,
            [pltpu.VMEM((D, 3 * D // 2), f32), pltpu.VMEM((8, D), f32), pltpu.VMEM((8, 16, ROW), f32)],
            20, "first_backward", after("bw3"),
        )(v["meta"], idx, *hbm("x", "grad_qkv"), *hbm("w_qkv", "acc_out"), *(v[n] for n in ("vecs", "sums", "inner_sum", "sums_out")))
        v["first_back"] = done[0]
        v.update(zip((n.format("a") for n in PAIR_NAMES), done[1:]))

    def again_back():
        v["first_back_2"] = over_blocks(hand_on, [D], 0, [(D, bf16, rows)], [], [], 8, "hand_on", after("hand"))(
            v["meta"], idx, *hbm("first_back")
        )[0]

    def finish():
        v["output"], v["grad_samples"] = over_blocks(
            finish_rows, [D] * 8, 1, [], [large((count, length, D))] * 2, [pltpu.VMEM((rows, D), bf16)] * 2, 24, "finish_rows", after("fin"),
        )(v["meta"], idx, *middle(), *hbm("out_part", "ot", "grad_middle", "first_back", "fb"), v["vecs"])

    def adds(g):
        pair, half = (pair_a, 288) if g == "a" else (pair_m, 576)

        def add(body, terms, outs, name):
            return at_once(
                body, 0, outs, [], 24, name + g, after(name + g)
            )(*(v[t] for t in terms))

        def even_in():
            v["aE" + g] = add(add_low, [f"yE{g}_grad", "rE" + g], [array(pair)], "aE")[0]

        def odd_in():
            v["aO" + g] = add(add_low, [f"xO{g}_grad", "rO" + g], [array(pair)], "aO")[0]

        def odd_sum():
            v["so" + g] = add(add_low, [f"O{g}_grad", "pO" + g, "qO" + g], [array(pair)], "so")[0]

        def even_sum():
            v["near" + g], v["far" + g] = add(
                add_near_far, [f"E{g}_grad", "pE" + g, "qE" + g, "wO" + g], [array(pair[1:], f32), array(pair[1:])], "sz"
            )

        def last_sum():
            outs = [array((half, ROW), f32)] * 2 + ([array(shape_s, f32)] * 2 if g == "a" else [])
            done = add(functools.partial(add_last, half), ["near" + g, "w2" + g], outs, "su")
            v["own" + g], v["other" + g] = done[:2]
            if g == "a":
                v["own_small"], v["other_small"] = done[2:]

        return {"aE" + g: even_in, "aO" + g: odd_in, "so" + g: odd_sum, "sz" + g: even_sum, "su" + g: last_sum}

    def optimize_m():
        v["new_mlp"] = at_once(
            step_mlp, 1, [array(shape_m, f32)] * 3,
            [pltpu.VMEM((2, *half_m), f32), pltpu.VMEM(shape_m, f32)], 16, "step_mlp", after("om"),
        )(idx, lanes(master_mlp), lanes(first_mlp), lanes(second_mlp), v["ownm"], v["otherm"], v["gm"])
        v["done_m"] = v["new_mlp"][0]

    def optimize_a():
        v["new_attn"] = at_once(
            step_attn, 1, [array(shape_a, f32)] * 3 + [array((3, ROW), f32)] * 3,
            [pltpu.VMEM((2, *half_a), f32), pltpu.VMEM(shape_a, f32), pltpu.VMEM(shape_s, f32), pltpu.VMEM((3, ROW), f32)], 16, "step_attn", after("oa"),
        )(idx, lanes(master_attn), lanes(first_attn), lanes(second_attn), v["owna"], v["othera"], v["ga"],
          three_rows(master_small), three_rows(first_small), three_rows(second_small), v["own_small"], v["gs"])

    works = {"cut": cut, "pa": piece_a, "Ea": even_a, "pm": piece_m, "pm2": again_m, "pack": pack, "there": there, "h1m": hold_1, "h0m": hold_0, "fwd": forward, "mlp": mlp, "mout": out_rows,
             "bw1": backward_1, "bw2": backward_2, "bw3": backward_3, "hand": again_back, "fin": finish, "om": optimize_m, "oa": optimize_a, **adds("m"), **adds("a")}
    todo = list(ORDER)
    while todo:
        left = []
        for step in todo:
            kind, name = step[0], step[1:]
            try:
                if kind == "+":
                    source, pairs = SENDS[name]
                    v[name] = send(v[source], pairs)
                else:
                    works[name]()
            except KeyError:
                left.append(step)
        assert len(left) < len(todo), left
        todo = left

    new_mlp, new_attn, output, grad_samples = v["new_mlp"], v["new_attn"], v["output"], v["grad_samples"]
    new_small = [a.reshape(-1)[:288] for a in new_attn[3:]]
    return (output, grad_samples, *(v.reshape(-1) for v in new_attn[:3]), *(v.reshape(-1) for v in new_mlp), *new_small)


def solution(mesh):
    in_specs = (
        P(("wide", "narrow"), None, None),
        P(("wide", "narrow"), None, None),
        P(("wide", "narrow")),
        P(("wide", "narrow")),
        P(("wide", "narrow")),
        P(("wide", "narrow")),
        P(("wide", "narrow")),
        P(("wide", "narrow")),
        P(("wide", "narrow")),
        P(("wide", "narrow")),
        P(("wide", "narrow")),
        P(("wide", "narrow")),
    )
    out_specs = (
        P(("wide", "narrow"), None, None),
        P(("wide", "narrow"), None, None),
        P(("wide", "narrow")),
        P(("wide", "narrow")),
        P(("wide", "narrow")),
        P(("wide", "narrow")),
        P(("wide", "narrow")),
        P(("wide", "narrow")),
        P(("wide", "narrow")),
        P(("wide", "narrow")),
        P(("wide", "narrow")),
    )
    small_slice = mesh.shape["wide"] == 8 and mesh.shape["narrow"] == 4
    return jax.shard_map(
        on_core if small_slice else on_device, mesh=mesh, in_specs=in_specs, out_specs=out_specs, check_vma=False
    )
```

```python
import functools
import math

import jax
import jax.numpy as jnp
from jax import lax
from jax.experimental import pallas as pl
from jax.experimental.pallas import tpu as pltpu
from jax.sharding import PartitionSpec as P

D = 768
FF = 3072
H = 12
HD = 64
STEP = 10


eps_norm = 1e-06
rate_matrix = 0.03
rate_small = 0.2
eps_adam = 1e-08
inv_root_two = 0.7071067811865476
inv_root_tau = 0.3989422804014327


def split_small(small):
    edges = [0, D, 2 * D, 3 * D, 4 * D, 5 * D, 6 * D, 7 * D, 7 * D + FF, 8 * D + FF]
    return [small[edges[i] : edges[i + 1]] for i in range(9)]


def standard(values):
    centre = values - jnp.mean(values, -1, keepdims=True)
    factor = lax.rsqrt(jnp.mean(centre * centre, -1, keepdims=True) + eps_norm)
    return (centre * factor, factor)


def norm_backward(grad, normed, factor, gain):
    grad_gain = jnp.sum(grad * normed, 0)
    grad_bias = jnp.sum(grad, 0)
    scaled = grad * gain
    inner_mean = jnp.mean(scaled * normed, -1, keepdims=True)
    grad_input = factor * (scaled - jnp.mean(scaled, -1, keepdims=True) - normed * inner_mean)
    return (grad_gain, grad_bias, grad_input)


def masked_scores(query, keys, key_mask):
    raw = jnp.einsum("sqhd,skhd->shqk", query, keys, preferred_element_type=jnp.float32) * (
        1.0 / math.sqrt(HD)
    )
    return jnp.where(key_mask, raw, -1e30)


def adamw(master, first, second, grad, decay, step_rate):
    first_new = 0.5 * first + 0.5 * grad
    second_new = 0.5 * second + 0.5 * grad * grad
    first_hat = first_new / (1.0 - 0.5**STEP)
    second_hat = second_new / (1.0 - 0.5**STEP)
    master_new = master - step_rate * (
        first_hat / (jnp.sqrt(second_hat) + eps_adam) + decay * master
    )
    return (master_new, first_new, second_new)


def scatter_sum(grad):
    lanes = grad.astype(jnp.bfloat16).reshape(-1, 128)
    own = lax.psum_scatter(lanes, ("wide", "narrow"), scatter_dimension=0, tiled=True)
    return own.reshape(-1).astype(jnp.float32)


def on_device(
    samples,
    cotangent,
    visible,
    master_attn,
    first_attn,
    second_attn,
    master_mlp,
    first_mlp,
    second_mlp,
    master_small,
    first_small,
    second_small,
):
    count, length, width = samples.shape
    total_rows = count * length
    scale = 1.0 / math.sqrt(HD)
    attn_full, mlp_full, small_full = (
        lax.all_gather(master_attn.astype(jnp.bfloat16), ("wide", "narrow"), axis=0, tiled=True),
        lax.all_gather(master_mlp.astype(jnp.bfloat16), ("wide", "narrow"), axis=0, tiled=True),
        lax.all_gather(master_small.astype(jnp.bfloat16), ("wide", "narrow"), axis=0, tiled=True),
    )
    w_qkv = attn_full[: 3 * D * D].reshape(D, 3 * D)
    w_out = attn_full[3 * D * D :].reshape(D, D)
    (
        gain_one,
        bias_one,
        bias_query,
        bias_value,
        bias_out,
        gain_two,
        bias_two,
        bias_inner,
        bias_outer,
    ) = split_small(small_full.astype(jnp.float32))
    valid = jnp.arange(length)[None, :] < visible[:, None]
    key_mask = valid[:, None, None, :]
    row_mask = valid.reshape(total_rows, 1)
    rows = samples.astype(jnp.float32).reshape(total_rows, D)
    normed_one, factor_one = standard(rows)
    first_in = (normed_one * gain_one + bias_one).astype(jnp.bfloat16)
    shift = jnp.concatenate([bias_query, jnp.zeros_like(bias_query), bias_value])
    qkv = jnp.dot(first_in, w_qkv, preferred_element_type=jnp.float32) + shift
    qkv_low = qkv.astype(jnp.bfloat16).reshape(count, length, 3, H, HD)
    query = qkv_low[:, :, 0]
    keys = qkv_low[:, :, 1]
    values = qkv_low[:, :, 2]
    scores = masked_scores(query, keys, key_mask)
    top = jnp.max(scores, -1, keepdims=True)
    expo = jnp.exp(scores - top)
    totals = jnp.sum(expo, -1, keepdims=True)
    log_total = top + jnp.log(totals)
    probs_low = (expo / totals).astype(jnp.bfloat16)
    context = jnp.einsum("shqk,skhd->sqhd", probs_low, values, preferred_element_type=jnp.float32)
    context_low = context.astype(jnp.bfloat16).reshape(total_rows, D)
    middle = rows + jnp.dot(context_low, w_out, preferred_element_type=jnp.float32) + bias_out
    w_one = mlp_full[: D * FF].reshape(D, FF)
    w_two = mlp_full[D * FF :].reshape(FF, D)
    normed_two, factor_two = standard(middle)
    second_in = (normed_two * gain_two + bias_two).astype(jnp.bfloat16)
    inner = jnp.dot(second_in, w_one, preferred_element_type=jnp.float32) + bias_inner
    active = jax.nn.gelu(inner, approximate=False).astype(jnp.bfloat16)
    result = middle + jnp.dot(active, w_two, preferred_element_type=jnp.float32) + bias_outer
    output = jnp.where(row_mask, result, 0.0).reshape(count, length, D).astype(jnp.bfloat16)
    grad_result = jnp.where(row_mask, cotangent.astype(jnp.float32).reshape(total_rows, D), 0.0)
    grad_branch = grad_result.astype(jnp.bfloat16)
    grad_w_two = jnp.einsum("rf,rd->fd", active, grad_branch, preferred_element_type=jnp.float32)
    grad_bias_outer = jnp.sum(grad_branch, 0, dtype=jnp.float32)
    grad_active = jnp.einsum("rd,fd->rf", grad_branch, w_two, preferred_element_type=jnp.float32)
    slope = (
        0.5 * (1.0 + jax.scipy.special.erf(inner * inv_root_two))
        + inner * jnp.exp(-0.5 * inner * inner) * inv_root_tau
    )
    grad_inner = (grad_active * slope).astype(jnp.bfloat16)
    grad_w_one = jnp.einsum("rd,rf->df", second_in, grad_inner, preferred_element_type=jnp.float32)
    grad_bias_inner = jnp.sum(grad_inner, 0, dtype=jnp.float32)
    grad_second_in = jnp.einsum("rf,df->rd", grad_inner, w_one, preferred_element_type=jnp.float32)
    grad_gain_two, grad_bias_two, grad_middle_norm = norm_backward(
        grad_second_in, normed_two, factor_two, gain_two
    )
    grad_middle = grad_result + grad_middle_norm
    grad_mlp = jnp.concatenate([grad_w_one.reshape(-1), grad_w_two.reshape(-1)])
    grad_proj = grad_middle.astype(jnp.bfloat16)
    grad_w_out = jnp.einsum("rc,rd->cd", context_low, grad_proj, preferred_element_type=jnp.float32)
    grad_bias_out = jnp.sum(grad_proj, 0, dtype=jnp.float32)
    grad_context = jnp.einsum("rd,cd->rc", grad_proj, w_out, preferred_element_type=jnp.float32)
    grad_context = grad_context.astype(jnp.bfloat16).reshape(count, length, H, HD)
    probs = jnp.exp(masked_scores(query, keys, key_mask) - log_total)
    probs_again = probs.astype(jnp.bfloat16)
    grad_values = jnp.einsum(
        "shqk,sqhd->skhd", probs_again, grad_context, preferred_element_type=jnp.float32
    )
    grad_probs = jnp.einsum(
        "sqhd,skhd->shqk", grad_context, values, preferred_element_type=jnp.float32
    )
    inner_sum = jnp.sum(grad_probs * probs, -1, keepdims=True)
    grad_scores = (probs * (grad_probs - inner_sum)).astype(jnp.bfloat16)
    grad_query = (
        jnp.einsum("shqk,skhd->sqhd", grad_scores, keys, preferred_element_type=jnp.float32) * scale
    )
    grad_keys = (
        jnp.einsum("shqk,sqhd->skhd", grad_scores, query, preferred_element_type=jnp.float32)
        * scale
    )
    grad_qkv = (
        jnp.stack([grad_query, grad_keys, grad_values], 2)
        .reshape(total_rows, 3 * D)
        .astype(jnp.bfloat16)
    )
    grad_w_qkv = jnp.einsum("rd,re->de", first_in, grad_qkv, preferred_element_type=jnp.float32)
    grad_bias_qkv = jnp.sum(grad_qkv, 0, dtype=jnp.float32)
    grad_first_in = jnp.einsum("re,de->rd", grad_qkv, w_qkv, preferred_element_type=jnp.float32)
    grad_gain_one, grad_bias_one, grad_rows_norm = norm_backward(
        grad_first_in, normed_one, factor_one, gain_one
    )
    grad_rows = grad_middle + grad_rows_norm
    grad_samples = grad_rows.reshape(count, length, D).astype(jnp.bfloat16)
    grad_attn = jnp.concatenate([grad_w_qkv.reshape(-1), grad_w_out.reshape(-1)])
    grad_small = jnp.concatenate(
        [
            grad_gain_one,
            grad_bias_one,
            grad_bias_qkv[:D],
            grad_bias_qkv[2 * D :],
            grad_bias_out,
            grad_gain_two,
            grad_bias_two,
            grad_bias_inner,
            grad_bias_outer,
        ]
    )
    summed_attn, summed_mlp, summed_small = (
        scatter_sum(grad_attn),
        scatter_sum(grad_mlp),
        lax.psum_scatter(grad_small, ("wide", "narrow"), scatter_dimension=0, tiled=True),
    )
    new_attn, new_first_attn, new_second_attn = adamw(
        master_attn, first_attn, second_attn, summed_attn, 0.1, rate_matrix
    )
    new_mlp, new_first_mlp, new_second_mlp = adamw(
        master_mlp, first_mlp, second_mlp, summed_mlp, 0.1, rate_matrix
    )
    new_small, new_first_small, new_second_small = adamw(
        master_small, first_small, second_small, summed_small, 0.0, rate_small
    )
    return (
        output,
        grad_samples,
        new_attn,
        new_first_attn,
        new_second_attn,
        new_mlp,
        new_first_mlp,
        new_second_mlp,
        new_small,
        new_first_small,
        new_second_small,
    )


bf16 = jnp.bfloat16
f32 = jnp.float32
BLOCK = 256
BIN = 128
AXES = ("wide", "narrow")
ROW = 128
SMALL_ROWS = 72


def place_of(i):
    wide, z = divmod(i, 4)
    return wide // 4, (wide // 2) % 2, wide % 2, z


def index_of(y, x, c, z):
    return ((y * 2 + x) * 2 + c) * 4 + z


def pairs_of(move):
    return [(i, index_of(*move(*place_of(i)))) for i in range(32)]


TO_X = pairs_of(lambda y, x, c, z: (y, 1 - x, c, z))
TO_Y = pairs_of(lambda y, x, c, z: (1 - y, x, c, z))
TO_CORE = pairs_of(lambda y, x, c, z: (y, x, 1 - c, z))
TO_Z = [pairs_of(lambda y, x, c, z, k=k: (y, x, c, z ^ k)) for k in range(4)]


def send(value, pairs):
    return lax.ppermute(value, AXES, pairs)


def dot(a, b, dims=((1,), (0,))):
    return lax.dot_general(a, b, (dims, ((), ())), preferred_element_type=f32)


def at_rows(ref, start, size):
    return ref[pl.ds(start, size), :]


def attn_block(core, j):
    return (j // 3) * 6 + 3 * core + j % 3


def mlp_block(core, j):
    return (j // 6) * 12 + 6 * core + j % 6


def shifted(idx, vector, out):
    lane = lax.broadcasted_iota(jnp.int32, (3, ROW), 1)
    out[...] = jnp.zeros(out.shape, f32)
    for k in range(4):

        @pl.when(idx[4] == k)
        def _():
            turned = pltpu.roll(vector[...], 32 * k, 1) if k else vector[...]
            at = 2 * k
            out[at : at + 3, :] = jnp.where(lane >= 32 * k, turned, 0.0)
            if k:
                out[at + 1 : at + 4, :] += jnp.where(lane < 32 * k, turned, 0.0)


def cut_masters(idx, attn, mlp, small, keep_a, send_a, keep_m, send_m, place, half_a, half_m):
    wide, core = idx[0], idx[3]

    @pl.when(wide < 6)
    def _():
        for c in range(2):
            for j in range(9):
                rows = attn[pl.ds(attn_block(c, j), 32, stride=18), :]
                half_a[c, j * 32 : (j + 1) * 32, :] = rows.astype(bf16)

    @pl.when(wide >= 6)
    def _():
        for j in range(6):
            rows = attn[pl.ds(j, 96, stride=6), :]
            half_a[j // 3, (j % 3) * 96 : (j % 3 + 1) * 96, :] = rows.astype(bf16)

    @pl.when(wide < 4)
    def _():
        for c in range(2):
            for j in range(12):
                rows = mlp[pl.ds(mlp_block(c, j), 48, stride=24), :]
                half_m[c, j * 48 : (j + 1) * 48, :] = rows.astype(bf16)

    @pl.when(wide >= 4)
    def _():
        for j in range(6):
            rows = mlp[pl.ds(j, 192, stride=6), :]
            half_m[j // 3, (j % 3) * 192 : (j % 3 + 1) * 192, :] = rows.astype(bf16)

    first_a = jnp.where(wide < 6, core, 0)
    first_m = jnp.where(wide < 4, core, 0)
    keep_a[0:288, :] = half_a[first_a]
    send_a[0:288, :] = half_a[1 - first_a]
    keep_m[...] = half_m[first_m]
    send_m[...] = half_m[1 - first_m]
    shifted(idx, small, place)
    keep_a[288:304, :] = place[...].astype(bf16)
    send_a[288:304, :] = place[...].astype(bf16)


def pack_rows(idx, vis_own, vis_other, x_own, x_other, cot_own, cot_other, x_out, cot_out, meta, fill):
    core = idx[3]
    for b in range(16):
        fill[b] = 0
    bins = jnp.int32(0)
    for s in range(16):
        mine = core == s // 8
        seen = jnp.where(mine, vis_own[s % 8], vis_other[s % 8])
        need = ((seen + 15) >> 4) << 4
        chosen = jnp.int32(15)
        for b in reversed(range(s + 1)):
            chosen = jnp.where(fill[b] + need <= BIN, b, chosen)
        start = chosen * BIN + fill[chosen]
        fill[chosen] = fill[chosen] + need
        bins = jnp.maximum(bins, chosen + 1)
        meta[8 + s] = start
        meta[24 + s] = seen
    blocks = (bins + 1) >> 1
    meta[0] = blocks

    def clear(b, carry):
        at = pl.ds(pl.multiple_of(b * BLOCK, BLOCK), BLOCK)
        x_out[at, :] = jnp.zeros((BLOCK, D), bf16)
        cot_out[at, :] = jnp.zeros((BLOCK, D), bf16)
        return carry

    lax.fori_loop(0, blocks, clear, 0)
    row = lax.broadcasted_iota(jnp.int32, (16, D), 0)
    for s in range(16):
        start, seen = meta[8 + s], meta[24 + s]

        def fetch(x_in, cot_in):
            def chunk(k, carry):
                src = pl.ds(pl.multiple_of(k * 16, 16), 16)
                dst = pl.ds(pl.multiple_of(start + k * 16, 16), 16)
                x_out[dst, :] = x_in[s % 8, src, :]
                grad = cot_in[s % 8, src, :].astype(f32)
                cot_out[dst, :] = jnp.where(row + k * 16 < seen, grad, 0.0).astype(bf16)
                return carry

            lax.fori_loop(0, (seen + 15) >> 4, chunk, 0)

        @pl.when(core == s // 8)
        def _():
            fetch(x_own, cot_own)

        @pl.when(core != s // 8)
        def _():
            fetch(x_other, cot_other)


def owner_of(idx, column, k):
    y, x, z = idx[1], idx[2], idx[4]
    yy = 1 - y if column >= 2 else y
    xx = 1 - x if column % 2 else x
    return yy * 2 + xx, jnp.bitwise_xor(z, k)


def pair_of(n):
    return n // 4 * 2 + n % 2


def core_of(idx, part):
    return 1 - idx[3] if part else idx[3]


def lanes_of(small, first, count):
    rows = [small[q // 9, q % 9 : q % 9 + 1, :] for q in range(first, first + count)]
    return jnp.concatenate(rows, axis=1)


def same_sample(meta, which):
    lane = lax.broadcasted_iota(jnp.int32, (8, BIN), 1)
    line = lax.broadcasted_iota(jnp.int32, (BIN, BIN), 0)
    of_key = jnp.full((8, BIN), -2, jnp.int32)
    of_query = jnp.full((BIN, BIN), -1, jnp.int32)
    for s in range(16):
        start = meta[8 + s] - which * BIN
        stop = start + meta[24 + s]
        of_key = jnp.where((lane >= start) & (lane < stop), s, of_key)
        of_query = jnp.where((line >= start) & (line < stop), s, of_query)
    return of_query == of_key[0:1, :]


def halves(pair):
    lane = lax.broadcasted_iota(jnp.int32, pair.shape, 1)
    wide = pair.astype(f32)
    return jnp.concatenate(
        [jnp.where(lane < HD, wide, 0.0), jnp.where(lane >= HD, wide, 0.0)], axis=0
    ).astype(bf16)


def probabilities(query, keys, mask):
    scores = dot(halves(query), keys, ((1,), (1,))) * (1.0 / math.sqrt(HD))
    scores = jnp.where(mask, scores, -1e30)
    expo = jnp.exp(scores - jnp.max(scores, -1, keepdims=True))
    return expo * (1.0 / jnp.sum(expo, -1, keepdims=True))


def probabilities_by_key(both, keys, mask):
    scores = dot(keys, both, ((1,), (1,))) * (1.0 / math.sqrt(HD))
    scores = jnp.where(mask, scores, -1e30)
    expo = jnp.exp(scores - jnp.max(scores, 0, keepdims=True))
    return expo * (1.0 / jnp.sum(expo, 0, keepdims=True))


def one_above_other(wide):
    return jnp.concatenate([wide[:, :BIN], wide[:, BIN:]], axis=0)


def side_by_side(stacked):
    return jnp.concatenate([stacked[:BIN], stacked[BIN:]], axis=1)


def attn_forward(phase, meta, idx, x_ref, *refs):
    pairs = refs[:8]
    qkv_ref, context_ref, part_ref, w_qkv, w_out, vecs, shift, inner_bias, small = refs[8:]

    if phase == 0:
        small[...] = jnp.zeros(small.shape, f32)
        for n in range(16):
            piece = pairs[pair_of(n)].at[n % 4 // 2]
            chip, z = owner_of(idx, n // 4, n % 4)

            @pl.when(chip < 3)
            def _():
                for part in range(2):
                    owner = (chip * 2 + core_of(idx, part)) * 4 + z
                    to = pl.ds(pl.multiple_of(owner * 32, 32), 32)
                    for j in range(9):
                        at = part * 288 + j * 32
                        w_qkv[to, j * ROW : (j + 1) * ROW] = piece[at : at + 32, :]

            @pl.when(chip == 3)
            def _():
                to = pl.ds(pl.multiple_of(z * 96, 32), 96)
                for j in range(6):
                    w_out[to, j * ROW : (j + 1) * ROW] = piece[j * 96 : (j + 1) * 96, :]

            for part in range(2):
                group = chip * 2 + core_of(idx, part)
                at = 576 + part * 16
                small[group] = small[group] + piece[at : at + 16, :].astype(f32)
        for n, first in enumerate((0, 6, 24, 30, 36, 66)):
            vecs[n : n + 1, :] = lanes_of(small, first, 6)
        vecs[6:8, :] = jnp.zeros((2, D), f32)
        own = idx[3] == 0
        query_bias = jnp.where(own, lanes_of(small, 12, 3), lanes_of(small, 15, 3))
        value_bias = jnp.where(own, lanes_of(small, 18, 3), lanes_of(small, 21, 3))
        shift[...] = jnp.concatenate([query_bias, jnp.zeros((1, D // 2), f32), value_bias], axis=1)
        low = jnp.where(own, lanes_of(small, 42, 6), lanes_of(small, 48, 6))
        high = jnp.where(own, lanes_of(small, 54, 6), lanes_of(small, 60, 6))
        inner_bias[...] = jnp.concatenate([low, high], axis=1)

    if phase == 1:
        normed, _ = standard(x_ref[...].astype(f32))
        first_in = (normed * vecs[0:1, :] + vecs[1:2, :]).astype(bf16)
        qkv_ref[...] = (dot(first_in, w_qkv[...]) + shift[...]).astype(bf16)
        for b in range(BLOCK // BIN):
            mask = same_sample(meta, pl.program_id(0) * (BLOCK // BIN) + b)
            mask = jnp.concatenate([mask, mask], axis=0)
            rows = slice(b * BIN, (b + 1) * BIN)
            for h in range(3):
                query, keys, values = (
                    qkv_ref[rows, (3 * t + h) * ROW : (3 * t + h + 1) * ROW] for t in range(3)
                )
                probs = probabilities(query, keys, mask).astype(bf16)
                context = dot(side_by_side(probs), halves(values))
                context_ref[rows, h * ROW : (h + 1) * ROW] = context.astype(bf16)
        part_ref[...] = dot(context_ref[...], w_out[...]).astype(bf16)


TAIL = (0.5 * 0.254829592, 0.5 * -0.284496736, 0.5 * 1.421413741, 0.5 * -1.453152027, 0.5 * 1.061405429)


def normal_curves(u):
    t = 1.0 / (1.0 + (0.3275911 * inv_root_two) * jnp.abs(u))
    expo = jnp.exp(-0.5 * u * u)
    series = TAIL[4]
    for a in TAIL[3::-1]:
        series = series * t + a
    tail = series * t * expo
    return jnp.where(u < 0.0, tail, 1.0 - tail), expo * inv_root_tau


def block_of(rows):
    return rows.at[pl.ds(pl.multiple_of(pl.program_id(0) * BLOCK, BLOCK), BLOCK), :]


def middle_of(x_ref, part_own, part_other, vecs):
    parts = part_own[...].astype(f32) + part_other[...].astype(f32)
    return x_ref[...].astype(f32) + parts + vecs[2:3, :]


def mlp_both(phase, meta, idx, x_ref, part_own, cot_ref, vecs, inner_bias, other_rows, *refs):
    pieces = refs[:16]
    active_ref, back_ref, w_two_out, sums, inner_sum = refs[16:21]
    outs = refs[21:29]
    w_one, w_two, acc_one, acc_two, stage, arrived, written = refs[29:]

    def to_stage(n):
        return pltpu.make_async_copy(pieces[n], stage.at[n], arrived.at[n])

    def to_output():
        return pltpu.make_async_copy(w_two, w_two_out, written)

    if phase == 0:
        for n in range(16):
            to_stage(n).start()
        acc_one[...] = jnp.zeros(acc_one.shape, f32)
        acc_two[...] = jnp.zeros(acc_two.shape, f32)
        sums[...] = jnp.zeros(sums.shape, f32)
        inner_sum[...] = jnp.zeros(inner_sum.shape, f32)
        for n in range(16):
            to_stage(n).wait()
            piece = stage.at[n]
            chip, z = owner_of(idx, n // 4, n % 4)

            @pl.when(chip < 2)
            def _():
                for part in range(2):
                    owner = (chip * 2 + core_of(idx, part)) * 4 + z
                    to = pl.ds(pl.multiple_of(owner * 48, 16), 48)
                    for j in range(12):
                        at = part * 576 + j * 48
                        w_one[to, j * ROW : (j + 1) * ROW] = piece[at : at + 48, :]

            @pl.when(chip >= 2)
            def _():
                to = pl.ds(pl.multiple_of((chip - 2) * D + z * 192, 64), 192)
                for j in range(6):
                    w_two[to, j * ROW : (j + 1) * ROW] = piece[j * 192 : (j + 1) * 192, :]

        to_output().start()

    if phase == 1:
        normed, _ = standard(middle_of(x_ref, part_own, block_of(other_rows), vecs))
        second_in = (normed * vecs[3:4, :] + vecs[4:5, :]).astype(bf16)
        grad = cot_ref[...]
        back = jnp.zeros((BLOCK, D), f32)
        inner_grads = []
        for n in range(2):
            cols = slice(n * D, (n + 1) * D)
            inner = dot(second_in, w_one[:, cols]) + inner_bias[:, cols]
            bell, bump = normal_curves(inner)
            active = (inner * bell).astype(bf16)
            active_ref[:, cols] = active
            slope = bell + inner * bump
            grad_inner = (dot(grad, w_two[cols, :], ((1,), (1,))) * slope).astype(bf16)
            inner_grads.append(grad_inner)
            acc_two[cols, :] += dot(active, grad, ((0,), (0,)))
            inner_sum[:, cols] += jnp.sum(grad_inner.astype(f32), 0, keepdims=True)
            back = back + dot(grad_inner, w_one[:, cols], ((1,), (1,)))
        acc_one[...] += dot(second_in, jnp.concatenate(inner_grads, axis=1), ((0,), (0,)))
        back_ref[...] = back.astype(bf16)
        sums[0:1, :] += jnp.sum(back * normed, 0, keepdims=True)
        sums[1:2, :] += jnp.sum(back, 0, keepdims=True)
        sums[2:3, :] += jnp.sum(grad.astype(f32), 0, keepdims=True)

    if phase == 2:
        to_output().wait()
        for n in range(16):
            chip, z = owner_of(idx, n // 4, n % 4)
            out, k = outs[pair_of(n)], n % 4 // 2

            @pl.when(chip < 2)
            def _():
                for part in range(2):
                    owner = (chip * 2 + core_of(idx, part)) * 4 + z
                    rows = pl.ds(pl.multiple_of(owner * 48, 16), 48)
                    for j in range(12):
                        at = part * 576 + j * 48
                        out[k, at : at + 48, :] = acc_one[rows, j * ROW : (j + 1) * ROW].astype(bf16)

            @pl.when(chip >= 2)
            def _():
                rows = pl.ds(pl.multiple_of((chip - 2) * D + z * 192, 64), 192)
                for j in range(6):
                    out[k, j * 192 : (j + 1) * 192, :] = acc_two[rows, j * ROW : (j + 1) * ROW].astype(bf16)


def mlp_out(phase, meta, idx, active_ref, w_two, part_ref):
    if phase == 1:
        part_ref[...] = dot(active_ref[...], w_two[...]).astype(bf16)


def middle_backward(phase, meta, idx, x_ref, part_own, part_other, cot_ref, back_own, context_ref, w_out, vecs, other_rows,
                    grad_ref, grad_context_ref, acc_out, sums):
    if phase == 0:
        acc_out[...] = jnp.zeros(acc_out.shape, f32)
        sums[...] = jnp.zeros(sums.shape, f32)

    if phase == 1:
        normed, factor = standard(middle_of(x_ref, part_own, part_other, vecs))
        scaled = (back_own[...].astype(f32) + block_of(other_rows)[...].astype(f32)) * vecs[3:4, :]
        through = scaled - jnp.mean(scaled, -1, keepdims=True)
        through = through - normed * jnp.mean(scaled * normed, -1, keepdims=True)
        grad_middle = cot_ref[...].astype(f32) + factor * through
        grad_ref[...] = grad_middle
        grad_proj = grad_middle.astype(bf16)
        acc_out[...] += dot(context_ref[...], grad_proj, ((0,), (0,)))
        sums[0:1, :] += jnp.sum(grad_proj.astype(f32), 0, keepdims=True)
        grad_context_ref[...] = dot(grad_proj, w_out[...], ((1,), (1,))).astype(bf16)


def heads_backward(phase, meta, idx, qkv_ref, grad_context_ref, grads):
    if phase == 1:
        scale = 1.0 / math.sqrt(HD)
        for b in range(BLOCK // BIN):
            mask = same_sample(meta, pl.program_id(0) * (BLOCK // BIN) + b)
            mask = jnp.concatenate([mask, mask], axis=1)
            rows = slice(b * BIN, (b + 1) * BIN)
            for h in range(3):
                cols = [slice((3 * t + h) * ROW, (3 * t + h + 1) * ROW) for t in range(3)]
                query, keys, values = (qkv_ref[rows, cols[t]] for t in range(3))
                both = halves(query)
                probs = probabilities_by_key(both, keys, mask)
                grad_out = halves(grad_context_ref[rows, h * ROW : (h + 1) * ROW])
                grad_values = dot(probs.astype(bf16), grad_out)
                grad_probs = dot(values, grad_out, ((1,), (1,)))
                total = jnp.sum(grad_probs * probs, 0, keepdims=True)
                grad_scores = (probs * (grad_probs - total)).astype(bf16)
                grad_keys = dot(grad_scores, both) * scale
                grad_query = dot(one_above_other(grad_scores), halves(keys), ((0,), (0,))) * scale
                grads[rows, cols[0]] = grad_query.astype(bf16)
                grads[rows, cols[1]] = grad_keys.astype(bf16)
                grads[rows, cols[2]] = grad_values.astype(bf16)


def first_backward(phase, meta, idx, x_ref, grads, w_qkv, acc_out, vecs, sums_in, inner_sum, sums_out, *refs):
    back_ref = refs[0]
    outs = refs[1:9]
    acc_qkv, sums, small = refs[9:]

    if phase == 0:
        acc_qkv[...] = jnp.zeros(acc_qkv.shape, f32)
        sums[...] = jnp.zeros(sums.shape, f32)

    if phase == 1:
        normed, _ = standard(x_ref[...].astype(f32))
        first_in = (normed * vecs[0:1, :] + vecs[1:2, :]).astype(bf16)
        grad_qkv = grads[...]
        acc_qkv[...] += dot(first_in, grad_qkv, ((0,), (0,)))
        back = dot(grad_qkv, w_qkv[...], ((1,), (1,)))
        back_ref[...] = back.astype(bf16)
        sums[0:1, :] += jnp.sum(back * normed, 0, keepdims=True)
        sums[1:2, :] += jnp.sum(back, 0, keepdims=True)
        sums[3:4, 0 : D // 2] += jnp.sum(grad_qkv[:, 0 : D // 2].astype(f32), 0, keepdims=True)
        sums[3:4, D // 2 : D] += jnp.sum(grad_qkv[:, D : D + D // 2].astype(f32), 0, keepdims=True)

    if phase == 2:
        small[...] = jnp.zeros(small.shape, f32)
        once = jnp.where(idx[3] == 0, 1.0, 0.0)

        def put(at, rows):
            for j in range(rows.shape[1] // ROW):
                q = at + j
                small[q // 9, q % 9 : q % 9 + 1, :] = rows[:, j * ROW : (j + 1) * ROW]

        put(0, sums[0:1, :])
        put(6, sums[1:2, :])
        put(24, sums_out[0:1, :] * once)
        put(30, sums_in[0:1, :])
        put(36, sums_in[1:2, :])
        put(66, sums_in[2:3, :] * once)
        for c in range(2):

            @pl.when(idx[3] == c)
            def _():
                put(12 + 3 * c, sums[3:4, 0 : D // 2])
                put(18 + 3 * c, sums[3:4, D // 2 : D])
                put(42 + 6 * c, inner_sum[:, 0:D])
                put(54 + 6 * c, inner_sum[:, D : 2 * D])

        for n in range(16):
            chip, z = owner_of(idx, n // 4, n % 4)
            out, k = outs[pair_of(n)], n % 4 // 2

            @pl.when(chip < 3)
            def _():
                for part in range(2):
                    owner = (chip * 2 + core_of(idx, part)) * 4 + z
                    rows = pl.ds(pl.multiple_of(owner * 32, 32), 32)
                    for j in range(9):
                        at = part * 288 + j * 32
                        out[k, at : at + 32, :] = acc_qkv[rows, j * ROW : (j + 1) * ROW].astype(bf16)

            @pl.when(chip == 3)
            def _():
                rows = pl.ds(pl.multiple_of(z * 96, 32), 96)
                for j in range(6):
                    out[k, j * 96 : (j + 1) * 96, :] = acc_out[rows, j * ROW : (j + 1) * ROW].astype(bf16)

            for part in range(2):
                group = chip * 2 + core_of(idx, part)
                out[k, 576 + part * 16 : 592 + part * 16, :] = small[group].astype(bf16)


def finish_rows(phase, meta, idx, x_ref, part_own, part_other, out_own, out_other, grad_ref, back_own, back_other, vecs,
                output, grad_samples, packed_out, packed_grad):
    if phase == 1:
        at = pl.ds(pl.multiple_of(pl.program_id(0) * BLOCK, BLOCK), BLOCK)
        parts = out_own[...].astype(f32) + out_other[...].astype(f32)
        result = middle_of(x_ref, part_own, part_other, vecs) + parts + vecs[5:6, :]
        packed_out[at, :] = result.astype(bf16)
        normed, factor = standard(x_ref[...].astype(f32))
        scaled = (back_own[...].astype(f32) + back_other[...].astype(f32)) * vecs[0:1, :]
        through = scaled - jnp.mean(scaled, -1, keepdims=True)
        through = through - normed * jnp.mean(scaled * normed, -1, keepdims=True)
        packed_grad[at, :] = (grad_ref[...] + factor * through).astype(bf16)

    if phase == 2:
        output[...] = jnp.zeros(output.shape, bf16)
        grad_samples[...] = jnp.zeros(grad_samples.shape, bf16)
        row = lax.broadcasted_iota(jnp.int32, (16, D), 0)
        for s in range(8):
            start, seen = meta[8 + idx[3] * 8 + s], meta[24 + idx[3] * 8 + s]

            def chunk(k, carry):
                src = pl.ds(pl.multiple_of(start + k * 16, 16), 16)
                dst = pl.ds(pl.multiple_of(k * 16, 16), 16)
                keep = row + k * 16 < seen
                for packed, out in ((packed_out, output), (packed_grad, grad_samples)):
                    out[s, dst, :] = jnp.where(keep, packed[src, :].astype(f32), 0.0).astype(bf16)
                return carry

            lax.fori_loop(0, (seen + 15) >> 4, chunk, 0)


def update_refs(master, first, second, grad, outs, decay, step_rate):
    for out, new in zip(outs, adamw(master[...], first[...], second[...], grad, decay, step_rate)):
        out[...] = new


def step_mlp(idx, master, first, second, keep, mine, other, new, new_first, new_second, half, grad):
    wide, core = idx[0], idx[3]
    at = jnp.where(wide < 4, core, 0)
    half[at] = keep[...]

    @pl.when(wide < 4)
    def _():
        half[1 - at] = other[...]

    @pl.when(wide >= 4)
    def _():
        half[1 - at] = mine[...]

    @pl.when(wide < 4)
    def _():
        for c in range(2):
            for j in range(12):
                grad[pl.ds(mlp_block(c, j), 48, stride=24), :] = half[c, j * 48 : (j + 1) * 48, :]

    @pl.when(wide >= 4)
    def _():
        for j in range(6):
            grad[pl.ds(j, 192, stride=6), :] = half[j // 3, (j % 3) * 192 : (j % 3 + 1) * 192, :]

    update_refs(master, first, second, grad[...], (new, new_first, new_second), 0.1, rate_matrix)


def step_attn(idx, master, first, second, keep, mine, other, master_s, first_s, second_s, keep_s, other_s,
              new, new_first, new_second, new_s, new_first_s, new_second_s, half, grad, place, small_grad):
    wide, core = idx[0], idx[3]
    at = jnp.where(wide < 6, core, 0)
    half[at] = keep[...]

    @pl.when(wide < 6)
    def _():
        half[1 - at] = other[...]

    @pl.when(wide >= 6)
    def _():
        half[1 - at] = mine[...]

    @pl.when(wide < 6)
    def _():
        for c in range(2):
            for j in range(9):
                grad[pl.ds(attn_block(c, j), 32, stride=18), :] = half[c, j * 32 : (j + 1) * 32, :]

    @pl.when(wide >= 6)
    def _():
        for j in range(6):
            grad[pl.ds(j, 96, stride=6), :] = half[j // 3, (j % 3) * 96 : (j % 3 + 1) * 96, :]

    update_refs(master, first, second, grad[...], (new, new_first, new_second), 0.1, rate_matrix)
    place[...] = keep_s[...] + other_s[...]
    lane = lax.broadcasted_iota(jnp.int32, (3, ROW), 1)
    for k in range(4):

        @pl.when(idx[4] == k)
        def _():
            at = 2 * k
            both = jnp.where(lane >= 32 * k, place[at : at + 3, :], place[at + 1 : at + 4, :])
            small_grad[...] = pltpu.roll(both, ROW - 32 * k, 1) if k else both

    update_refs(master_s, first_s, second_s, small_grad[...], (new_s, new_first_s, new_second_s), 0.0, rate_small)


def plus(*terms):
    return sum(t.astype(f32) for t in terms)


def nothing(idx, out):
    out[...] = jnp.zeros(out.shape, f32)


def lay_attn(idx, keep, mine, other, piece):
    piece[0:288, :] = keep[0:288, :]
    piece[576:592, :] = keep[288:304, :]
    piece[592:608, :] = other[288:304, :]

    @pl.when(idx[0] < 6)
    def _():
        piece[288:576, :] = other[0:288, :]

    @pl.when(idx[0] >= 6)
    def _():
        piece[288:576, :] = mine[0:288, :]


def lay_mlp(idx, keep, mine, other, piece):
    piece[0:576, :] = keep[...]

    @pl.when(idx[0] < 4)
    def _():
        piece[576:1152, :] = other[...]

    @pl.when(idx[0] >= 4)
    def _():
        piece[576:1152, :] = mine[...]


def lay_out(*refs):
    at = 0
    for ref in refs[:-1]:
        refs[-1][at : at + ref.shape[0], :] = ref[...]
        at += ref.shape[0]


def pair_up(first, second, pair):
    pair[0] = first[...]
    pair[1] = second[...]


def add_low(*refs):
    refs[-1][...] = plus(*(r[...] for r in refs[:-1])).astype(bf16)


def add_near_far(*refs):
    terms, (near, far) = refs[:-2], refs[-2:]
    near[...] = plus(*(r[0] for r in terms))
    far[...] = plus(*(r[1] for r in terms)).astype(bf16)


def add_last(half, near, other, *outs):
    total = near[...] + other[...].astype(f32)
    outs[0][...] = total[:half]
    outs[1][...] = total[half : 2 * half]
    for n, out in enumerate(outs[2:]):
        out[...] = total[2 * half + 16 * n : 2 * half + 16 * n + 16]


SENDS = {
    "cv": ("visible", TO_CORE),
    "cs": ("samples", TO_CORE),
    "cc": ("cotangent", TO_CORE),
    "sa": ("send_a", TO_CORE),
    "sm": ("send_m", TO_CORE),
    "z2a": ("pa", TO_Z[2]),
    "zOa": ("Ea", TO_Z[1]),
    "xEa": ("Ea", TO_X),
    "yEa": ("Ea", TO_Y),
    "xOa": ("zOa", TO_X),
    "yOa": ("zOa", TO_Y),
    "dEa": ("yEa", TO_X),
    "dOa": ("xOa", TO_Y),
    "z1m": ("pm", TO_Z[1]),
    "z2m": ("pm2", TO_Z[2]),
    "z3m": ("z2m", TO_Z[1]),
    "x0m": ("pm", TO_X),
    "y0m": ("pm", TO_Y),
    "x1m": ("h1m", TO_X),
    "y1m": ("h1m", TO_Y),
    "x2m": ("z2m", TO_X),
    "y2m": ("z2m", TO_Y),
    "x3m": ("z3m", TO_X),
    "y3m": ("z3m", TO_Y),
    "d0m": ("h0m", TO_X),
    "d1m": ("d0m", TO_Z[1]),
    "d2m": ("x2m", TO_Y),
    "d3m": ("d2m", TO_Z[1]),
    "pt": ("part", TO_CORE),
    "bk": ("back", TO_CORE),
    "ot": ("out_part", TO_CORE),
    "fb": ("first_back_2", TO_CORE),
}
for group in "am":
    SENDS |= {
        "rE" + group: ("dE" + group + "_grad", TO_X),
        "rO" + group: ("dO" + group + "_grad", TO_Y),
        "pE" + group: ("xE" + group + "_grad", TO_X),
        "pO" + group: ("yO" + group + "_grad", TO_Y),
        "qE" + group: ("aE" + group, TO_Y),
        "qO" + group: ("aO" + group, TO_X),
        "wO" + group: ("so" + group, TO_Z[1]),
        "w2" + group: ("far" + group, TO_Z[2]),
        "g" + group: ("other" + group, TO_CORE),
    }
SENDS["gs"] = ("other_small", TO_CORE)
PAIR_NAMES = ("E{}_grad", "O{}_grad", "xE{}_grad", "xO{}_grad", "yE{}_grad", "yO{}_grad", "dE{}_grad", "dO{}_grad")

IN_HBM = ("first_back", "out_part", "grad_context", "output", "done_m")
AFTER = {
    "sum": ("fara",),
    "szm": ("aEa",),
    "soa": ("aEa",),
    "aOa": ("rEa",),
    "pa": ("cs", "cc", "cv"),
    "pm": ("pa",),
    "Ea": ("meta",),
    "pm2": ("Ea",),
    "h1m": ("xOa",),
    "h0m": ("xOa",),
    "fwd": ("x0m", "y0m", "z2m"),
    "there": ("x3m", "y3m", "d1m", "d2m", "d3m", "x2m", "d0m", "vecs"),
    "mlp": ("there",),
    "bw1": ("out_part",),
    "aEm": ("grad_context",),
    "aOm": ("grad_context",),
    "bw2": ("aEm", "aOm"),
    "bw3": ("ot",),
    "som": ("qEm", "pEm"),
    "fin": ("soa",),
    "sza": ("output",),
    "sua": ("done_m",),
}

ORDER = (
    "+cv", "+cs", "+cc", "=cut", "+sa", "+sm", "=pack", "=pa", "+z2a", "=pm", "+z1m", "+x0m", "+y0m", "=Ea", "=pm2", "+z2m",
    "+zOa", "+xEa", "+yEa", "+dEa", "+yOa", "+z3m", "+xOa", "=h1m", "=h0m", "+x1m", "+y1m", "+y2m", "+x2m", "+d0m", "+dOa", "+y3m",
    "+x3m", "+d2m", "=fwd", "+pt", "+d1m", "+d3m", "=there", "=mlp", "+rEm", "+rOm", "+bk", "=mout", "+ot", "=bw1", "=aEm", "=aOm",
    "+qOm", "+qEm", "+pEm", "+pOm", "=bw2", "=bw3", "+rEa", "+rOa", "=som", "+fb", "+wOm", "=aEa", "=aOa", "+qOa", "+qEa", "+pEa",
    "+pOa", "=soa", "+wOa", "=fin", "=sza", "+w2a", "=szm", "+w2m", "=sum", "+gm", "=om", "=sua", "+ga", "+gs", "=oa",
)


SMEM = pl.BlockSpec(memory_space=pltpu.SMEM)
VMEM = pl.BlockSpec(memory_space=pltpu.VMEM)
ANY = pl.BlockSpec(memory_space=pl.ANY)


def array(shape, dtype=bf16):
    return jax.ShapeDtypeStruct(shape, dtype)


def large(shape, dtype=bf16):
    return pltpu.HBM(shape, dtype)


def params(mib):
    return pltpu.CompilerParams(vmem_limit_bytes=mib << 20)


SCALE = 10**9
COSTS = {
    "attn_forward": 11, "mlp_both": 23, "mlp_out": 20, "middle_backward": 8, "heads_backward": 25, "first_backward": 25,
    "finish_rows": 8, "pack_rows": 6, "all_there": 60,
}


def cost(name):
    return pl.CostEstimate(flops=COSTS.get(name, 1) * SCALE, bytes_accessed=1, transcendentals=0)


def in_hbm(value):
    return pltpu.with_memory_space_constraint(value, pltpu.HBM)


def full(value):
    return pl.BlockSpec(value.shape, lambda i: (0,) * len(value.shape))


def over_blocks(body, rows_in, fixed_in, rows_out, fixed_out, scratch, mib, name, after=(), far=None):
    many = rows_in + [w for w, _, _ in rows_out]
    n_in, n_out = len(rows_in), len(rows_out)

    def kernel(meta, idx, *refs):
        refs = refs[: n_in + fixed_in] + refs[n_in + fixed_in + len(after) :]
        rows, fixed, lines, rest = (
            refs[:n_in], refs[n_in : n_in + fixed_in], refs[n_in + fixed_in :][:n_out], refs[n_in + fixed_in + n_out :]
        )
        body(0, meta, idx, *rows, *fixed, *lines, *rest)

        def one(*blocks):
            body(1, meta, idx, *blocks[:n_in], *fixed, *blocks[n_in:], *rest)

        specs = [pl.BlockSpec((BLOCK, w), lambda i: (i, 0)) for w in many]
        pltpu.emit_pipeline(one, grid=(meta[0],), in_specs=specs[:n_in], out_specs=specs[n_in:])(*rows, *lines)
        body(2, meta, idx, *rows, *fixed, *lines, *rest)

    def fixed_specs(arrays, first):
        if far is None:
            return [full(a) for a in arrays]
        return [ANY if first + n in far else VMEM for n in range(len(arrays))]

    def called(meta, idx, *args):
        return pl.pallas_call(
            kernel,
            in_specs=[SMEM, SMEM] + [ANY] * n_in + fixed_specs(args[n_in:], 0) + [ANY] * len(after),
            out_specs=[ANY] * n_out + fixed_specs(fixed_out, fixed_in),
            out_shape=[large((n, w), t) for w, t, n in rows_out] + fixed_out,
            scratch_shapes=scratch,
            compiler_params=params(mib),
            cost_estimate=cost(name),
            name=name,
            **({"grid": (1,)} if far is None else {}),
        )(meta, idx, *args, *after)

    return called


def at_once(body, scalars, outs, scratch, mib, name, after=(), copied=False):
    def kernel(*refs):
        n = len(refs) - len(scratch) - len(outs) - len(after)
        body(*refs[:n], *refs[n + len(after) :])

    def called(*args):
        grid = {"grid": (1,)} if copied else {}
        blocks = [full(a) if copied else VMEM for a in args[scalars:]]
        arrays = [in_hbm(a) for a in args[scalars:]] if copied else args[scalars:]
        return pl.pallas_call(
            kernel,
            in_specs=[SMEM] * scalars + blocks + [ANY] * len(after),
            out_specs=[SMEM if a.dtype == jnp.int32 else full(a) if copied else VMEM for a in outs],
            out_shape=outs,
            scratch_shapes=scratch,
            compiler_params=params(mib),
            cost_estimate=cost(name),
            name=name,
            **grid,
        )(*args[:scalars], *arrays, *after)

    return called


def on_core(
    samples,
    cotangent,
    visible,
    master_attn,
    first_attn,
    second_attn,
    master_mlp,
    first_mlp,
    second_mlp,
    master_small,
    first_small,
    second_small,
):
    count, length, _ = samples.shape
    rows = 2 * count * length
    wide, z = lax.axis_index("wide"), lax.axis_index("narrow")
    idx = jnp.stack([wide, wide // 4, (wide // 2) % 2, wide % 2, z]).astype(jnp.int32)

    def lanes(flat):
        return flat.reshape(-1, ROW)

    def three_rows(vector):
        return lanes(jnp.pad(vector, (0, 3 * ROW - vector.shape[0])))

    half_a, half_m = (288, ROW), (576, ROW)
    shape_m, shape_a, shape_s = (1152, ROW), (576, ROW), (16, ROW)
    pair_a, pair_m = (2, 608, ROW), (2, 1152, ROW)

    def after(name):
        return tuple(in_hbm(v[n]) if n in IN_HBM else v[n] for n in AFTER.get(name, ()))

    v = {"visible": visible, "samples": samples, "cotangent": cotangent}

    def hbm(*names):
        return tuple(v[n] if n in SENDS else in_hbm(v[n]) for n in names)

    def cut():
        swap_a = (304, ROW)
        v["keep_a"], v["send_a"], v["keep_m"], v["send_m"] = at_once(
            cut_masters, 1, [array(swap_a), array(swap_a), array(half_m), array(half_m)],
            [pltpu.VMEM(shape_s, f32), pltpu.VMEM((2, *half_a), bf16), pltpu.VMEM((2, *half_m), bf16)], 8, "cut_masters", after("cut"), True,
        )(idx, lanes(master_attn), lanes(master_mlp), three_rows(master_small))

    def piece_a():
        v["pa"] = at_once(lay_attn, 1, [array((608, ROW))], [], 8, "piece_attn", after("pa"))(
            idx, v["keep_a"], v["send_a"], v["sa"]
        )[0]

    def even_a():
        v["Ea"] = at_once(
            pair_up, 0, [array(pair_a)], [], 8, "pair_up", after("Ea")
        )(v["pa"], v["z2a"])[0]

    def piece_m():
        v["pm"] = at_once(lay_mlp, 1, [array(shape_m)], [], 8, "piece_mlp", after("pm"))(
            idx, v["keep_m"], v["send_m"], v["sm"]
        )[0]

    def again_m():
        v["pm2"] = at_once(lay_out, 0, [array(shape_m)], [], 8, "piece_again", after("pm2"))(v["pm"])[0]

    def pack():
        v["x"], v["cot"], v["meta"] = at_once(
            pack_rows, 3, [large((rows, D)), large((rows, D)), array((64,), jnp.int32)],
            [pltpu.SMEM((16,), jnp.int32)], 32, "pack_rows", after("pack"),
        )(idx, visible, v["cv"], in_hbm(samples), v["cs"], in_hbm(cotangent), v["cc"])

    def forward():
        outs = [large((D, 3 * D // 2)), large((D // 2, D)), array((8, D), f32), array((1, 3 * D // 2), f32), array((1, FF // 2), f32)]
        (v["qkv"], v["context"], v["part"], v["w_qkv"], v["w_out"], v["vecs"], shift, v["inner_bias"]) = over_blocks(
            attn_forward, [D], 8, [(3 * D // 2, bf16, rows), (D // 2, bf16, rows), (D, bf16, rows)], outs,
            [pltpu.VMEM((8, 16, ROW), f32)], 24, "attn_forward", after("fwd"),
        )(v["meta"], idx, *hbm("x"), v["Ea"], *(v[n] for n in ("zOa", "xEa", "xOa", "yEa", "yOa", "dEa", "dOa")))

    def hold_1():
        v["h1m"] = at_once(lay_out, 0, [array(shape_m)], [], 8, "hold_first", after("h1m"))(v["z1m"])[0]

    def hold_0():
        v["h0m"] = at_once(lay_out, 0, [array(shape_m)], [], 8, "hold_own", after("h0m"))(v["y0m"])[0]

    def there():
        v["there"] = at_once(nothing, 1, [array((8, ROW), f32)], [], 4, "all_there", after("there"))(idx)[0]

    def middle():
        return hbm("x", "part", "pt")

    def mlp():
        pieces = [v["pm"] if c + k == "z0" else v[c + k + "m"] for c in "zxyd" for k in "0123"]
        done = over_blocks(
            mlp_both, [D] * 3, 19, [(FF // 2, bf16, rows), (D, bf16, rows)],
            [large((FF // 2, D)), array((8, D), f32), array((1, FF // 2), f32)] + [array(pair_m)] * 8,
            [pltpu.VMEM((D, FF // 2), bf16), pltpu.VMEM((FF // 2, D), bf16), pltpu.VMEM((D, FF // 2), f32), pltpu.VMEM((FF // 2, D), f32),
             pltpu.VMEM((16, *shape_m), bf16), pltpu.SemaphoreType.DMA((16,)), pltpu.SemaphoreType.DMA],
            40, "mlp_both", after("mlp"), {*range(3, 19), 19},
        )(v["meta"], idx, *hbm("x", "part", "cot"), v["vecs"], v["inner_bias"], v["pt"], *pieces)
        v["active"], v["back"], v["w_two"], v["sums"], v["inner_sum"] = done[:5]
        v.update(zip((n.format("m") for n in PAIR_NAMES), done[5:]))

    def out_rows():
        v["out_part"] = over_blocks(mlp_out, [FF // 2], 1, [(D, bf16, rows)], [], [], 16, "mlp_out", after("mout"))(
            v["meta"], idx, *hbm("active", "w_two")
        )[0]

    def backward_1():
        v["grad_middle"], v["grad_context"], v["acc_out"], v["sums_out"] = over_blocks(
            middle_backward, [D] * 5 + [D // 2], 3, [(D, f32, rows), (D // 2, bf16, rows)],
            [large((D // 2, D), f32), array((8, D), f32)], [], 16, "middle_backward", after("bw1"),
        )(v["meta"], idx, *middle(), *hbm("cot", "back", "context", "w_out"), v["vecs"], v["bk"])

    def backward_2():
        v["grad_qkv"] = over_blocks(
            heads_backward, [3 * D // 2, D // 2], 0, [(3 * D // 2, bf16, rows)], [], [], 16, "heads_backward", after("bw2"),
        )(v["meta"], idx, *hbm("qkv", "grad_context"))[0]

    def backward_3():
        done = over_blocks(
            first_backward, [D, 3 * D // 2], 6, [(D, bf16, rows)], [array(pair_a)] * 8,
            [pltpu.VMEM((D, 3 * D // 2), f32), pltpu.VMEM((8, D), f32), pltpu.VMEM((8, 16, ROW), f32)],
            20, "first_backward", after("bw3"),
        )(v["meta"], idx, *hbm("x", "grad_qkv"), *hbm("w_qkv", "acc_out"), *(v[n] for n in ("vecs", "sums", "inner_sum", "sums_out")))
        v["first_back"] = done[0]
        v.update(zip((n.format("a") for n in PAIR_NAMES), done[1:]))

    def finish():
        v["output"], v["grad_samples"] = over_blocks(
            finish_rows, [D] * 8, 1, [], [large((count, length, D))] * 2, [pltpu.VMEM((rows, D), bf16)] * 2, 24, "finish_rows", after("fin"),
        )(v["meta"], idx, *middle(), *hbm("out_part", "ot", "grad_middle", "first_back_2", "fb"), v["vecs"])

    def adds(g):
        pair, half = (pair_a, 288) if g == "a" else (pair_m, 576)

        def add(body, terms, outs, name):
            return at_once(
                body, 0, outs, [], 24, name + g, after(name + g)
            )(*(v[t] for t in terms))

        def even_in():
            v["aE" + g] = add(add_low, [f"yE{g}_grad", "rE" + g], [array(pair)], "aE")[0]

        def odd_in():
            v["aO" + g] = add(add_low, [f"xO{g}_grad", "rO" + g], [array(pair)], "aO")[0]

        def odd_sum():
            terms = [f"O{g}_grad", "pO" + g, "qO" + g]
            if g == "a":
                v["so" + g] = add(add_low, terms, [array(pair)], "so")[0]
                return
            waited = after("som")
            v["som"], v["first_back_2"] = pl.pallas_call(
                lambda a, b, c, *refs: add_low(a, b, c, refs[-2]),
                in_specs=[VMEM] * 3 + [ANY] * (1 + len(waited)),
                out_specs=[VMEM, ANY],
                out_shape=[array(pair), large((rows, D))],
                input_output_aliases={3: 1},
                compiler_params=params(24),
                cost_estimate=cost("som"),
                name="som",
            )(*(v[t] for t in terms), in_hbm(v["first_back"]), *waited)

        def even_sum():
            v["near" + g], v["far" + g] = add(
                add_near_far, [f"E{g}_grad", "pE" + g, "qE" + g, "wO" + g], [array(pair[1:], f32), array(pair[1:])], "sz"
            )

        def last_sum():
            outs = [array((half, ROW), f32)] * 2 + ([array(shape_s, f32)] * 2 if g == "a" else [])
            done = add(functools.partial(add_last, half), ["near" + g, "w2" + g], outs, "su")
            v["own" + g], v["other" + g] = done[:2]
            if g == "a":
                v["own_small"], v["other_small"] = done[2:]

        return {"aE" + g: even_in, "aO" + g: odd_in, "so" + g: odd_sum, "sz" + g: even_sum, "su" + g: last_sum}

    def optimize_m():
        v["new_mlp"] = at_once(
            step_mlp, 1, [large(shape_m, f32)] * 3,
            [pltpu.VMEM((2, *half_m), f32), pltpu.VMEM(shape_m, f32)], 16, "step_mlp", after("om"),
        )(idx, lanes(master_mlp), lanes(first_mlp), lanes(second_mlp), v["ownm"], v["otherm"], v["gm"])
        v["done_m"] = v["new_mlp"][0]

    def optimize_a():
        v["new_attn"] = at_once(
            step_attn, 1, [array(shape_a, f32)] * 3 + [array((3, ROW), f32)] * 3,
            [pltpu.VMEM((2, *half_a), f32), pltpu.VMEM(shape_a, f32), pltpu.VMEM(shape_s, f32), pltpu.VMEM((3, ROW), f32)], 16, "step_attn", after("oa"),
        )(idx, lanes(master_attn), lanes(first_attn), lanes(second_attn), v["owna"], v["othera"], v["ga"],
          three_rows(master_small), three_rows(first_small), three_rows(second_small), v["own_small"], v["gs"])

    works = {"cut": cut, "pa": piece_a, "Ea": even_a, "pm": piece_m, "pm2": again_m, "pack": pack, "there": there, "h1m": hold_1, "h0m": hold_0, "fwd": forward, "mlp": mlp, "mout": out_rows,
             "bw1": backward_1, "bw2": backward_2, "bw3": backward_3, "fin": finish, "om": optimize_m, "oa": optimize_a, **adds("m"), **adds("a")}
    for step in ORDER:
        kind, name = step[0], step[1:]
        if kind == "+":
            source, pairs = SENDS[name]
            v[name] = send(v[source], pairs)
        else:
            works[name]()

    new_mlp, new_attn, output, grad_samples = v["new_mlp"], v["new_attn"], v["output"], v["grad_samples"]
    new_small = [a.reshape(-1)[:288] for a in new_attn[3:]]
    return (output, grad_samples, *(v.reshape(-1) for v in new_attn[:3]), *(v.reshape(-1) for v in new_mlp), *new_small)


def solution(mesh):
    in_specs = (
        P(("wide", "narrow"), None, None),
        P(("wide", "narrow"), None, None),
        P(("wide", "narrow")),
        P(("wide", "narrow")),
        P(("wide", "narrow")),
        P(("wide", "narrow")),
        P(("wide", "narrow")),
        P(("wide", "narrow")),
        P(("wide", "narrow")),
        P(("wide", "narrow")),
        P(("wide", "narrow")),
        P(("wide", "narrow")),
    )
    out_specs = (
        P(("wide", "narrow"), None, None),
        P(("wide", "narrow"), None, None),
        P(("wide", "narrow")),
        P(("wide", "narrow")),
        P(("wide", "narrow")),
        P(("wide", "narrow")),
        P(("wide", "narrow")),
        P(("wide", "narrow")),
        P(("wide", "narrow")),
        P(("wide", "narrow")),
        P(("wide", "narrow")),
    )
    small_slice = mesh.shape["wide"] == 8 and mesh.shape["narrow"] == 4
    return jax.shard_map(
        on_core if small_slice else on_device, mesh=mesh, in_specs=in_specs, out_specs=out_specs, check_vma=False
    )
```

```python
import functools
import math

import jax
import jax.numpy as jnp
from jax import lax
from jax.experimental import pallas as pl
from jax.experimental.pallas import tpu as pltpu
from jax.sharding import PartitionSpec as P

D = 768
FF = 3072
H = 12
HD = 64
STEP = 10


eps_norm = 1e-06
rate_matrix = 0.03
rate_small = 0.2
eps_adam = 1e-08
inv_root_two = 0.7071067811865476
inv_root_tau = 0.3989422804014327


def split_small(small):
    edges = [0, D, 2 * D, 3 * D, 4 * D, 5 * D, 6 * D, 7 * D, 7 * D + FF, 8 * D + FF]
    return [small[edges[i] : edges[i + 1]] for i in range(9)]


def standard(values):
    centre = values - jnp.mean(values, -1, keepdims=True)
    factor = lax.rsqrt(jnp.mean(centre * centre, -1, keepdims=True) + eps_norm)
    return (centre * factor, factor)


def norm_backward(grad, normed, factor, gain):
    grad_gain = jnp.sum(grad * normed, 0)
    grad_bias = jnp.sum(grad, 0)
    scaled = grad * gain
    inner_mean = jnp.mean(scaled * normed, -1, keepdims=True)
    grad_input = factor * (scaled - jnp.mean(scaled, -1, keepdims=True) - normed * inner_mean)
    return (grad_gain, grad_bias, grad_input)


def masked_scores(query, keys, key_mask):
    raw = jnp.einsum("sqhd,skhd->shqk", query, keys, preferred_element_type=jnp.float32) * (
        1.0 / math.sqrt(HD)
    )
    return jnp.where(key_mask, raw, -1e30)


def adamw(master, first, second, grad, decay, step_rate):
    first_new = 0.5 * first + 0.5 * grad
    second_new = 0.5 * second + 0.5 * grad * grad
    first_hat = first_new / (1.0 - 0.5**STEP)
    second_hat = second_new / (1.0 - 0.5**STEP)
    master_new = master - step_rate * (
        first_hat / (jnp.sqrt(second_hat) + eps_adam) + decay * master
    )
    return (master_new, first_new, second_new)


def scatter_sum(grad):
    lanes = grad.astype(jnp.bfloat16).reshape(-1, 128)
    own = lax.psum_scatter(lanes, ("wide", "narrow"), scatter_dimension=0, tiled=True)
    return own.reshape(-1).astype(jnp.float32)


def on_device(
    samples,
    cotangent,
    visible,
    master_attn,
    first_attn,
    second_attn,
    master_mlp,
    first_mlp,
    second_mlp,
    master_small,
    first_small,
    second_small,
):
    count, length, width = samples.shape
    total_rows = count * length
    scale = 1.0 / math.sqrt(HD)
    attn_full, mlp_full, small_full = (
        lax.all_gather(master_attn.astype(jnp.bfloat16), ("wide", "narrow"), axis=0, tiled=True),
        lax.all_gather(master_mlp.astype(jnp.bfloat16), ("wide", "narrow"), axis=0, tiled=True),
        lax.all_gather(master_small.astype(jnp.bfloat16), ("wide", "narrow"), axis=0, tiled=True),
    )
    w_qkv = attn_full[: 3 * D * D].reshape(D, 3 * D)
    w_out = attn_full[3 * D * D :].reshape(D, D)
    (
        gain_one,
        bias_one,
        bias_query,
        bias_value,
        bias_out,
        gain_two,
        bias_two,
        bias_inner,
        bias_outer,
    ) = split_small(small_full.astype(jnp.float32))
    valid = jnp.arange(length)[None, :] < visible[:, None]
    key_mask = valid[:, None, None, :]
    row_mask = valid.reshape(total_rows, 1)
    rows = samples.astype(jnp.float32).reshape(total_rows, D)
    normed_one, factor_one = standard(rows)
    first_in = (normed_one * gain_one + bias_one).astype(jnp.bfloat16)
    shift = jnp.concatenate([bias_query, jnp.zeros_like(bias_query), bias_value])
    qkv = jnp.dot(first_in, w_qkv, preferred_element_type=jnp.float32) + shift
    qkv_low = qkv.astype(jnp.bfloat16).reshape(count, length, 3, H, HD)
    query = qkv_low[:, :, 0]
    keys = qkv_low[:, :, 1]
    values = qkv_low[:, :, 2]
    scores = masked_scores(query, keys, key_mask)
    top = jnp.max(scores, -1, keepdims=True)
    expo = jnp.exp(scores - top)
    totals = jnp.sum(expo, -1, keepdims=True)
    log_total = top + jnp.log(totals)
    probs_low = (expo / totals).astype(jnp.bfloat16)
    context = jnp.einsum("shqk,skhd->sqhd", probs_low, values, preferred_element_type=jnp.float32)
    context_low = context.astype(jnp.bfloat16).reshape(total_rows, D)
    middle = rows + jnp.dot(context_low, w_out, preferred_element_type=jnp.float32) + bias_out
    w_one = mlp_full[: D * FF].reshape(D, FF)
    w_two = mlp_full[D * FF :].reshape(FF, D)
    normed_two, factor_two = standard(middle)
    second_in = (normed_two * gain_two + bias_two).astype(jnp.bfloat16)
    inner = jnp.dot(second_in, w_one, preferred_element_type=jnp.float32) + bias_inner
    active = jax.nn.gelu(inner, approximate=False).astype(jnp.bfloat16)
    result = middle + jnp.dot(active, w_two, preferred_element_type=jnp.float32) + bias_outer
    output = jnp.where(row_mask, result, 0.0).reshape(count, length, D).astype(jnp.bfloat16)
    grad_result = jnp.where(row_mask, cotangent.astype(jnp.float32).reshape(total_rows, D), 0.0)
    grad_branch = grad_result.astype(jnp.bfloat16)
    grad_w_two = jnp.einsum("rf,rd->fd", active, grad_branch, preferred_element_type=jnp.float32)
    grad_bias_outer = jnp.sum(grad_branch, 0, dtype=jnp.float32)
    grad_active = jnp.einsum("rd,fd->rf", grad_branch, w_two, preferred_element_type=jnp.float32)
    slope = (
        0.5 * (1.0 + jax.scipy.special.erf(inner * inv_root_two))
        + inner * jnp.exp(-0.5 * inner * inner) * inv_root_tau
    )
    grad_inner = (grad_active * slope).astype(jnp.bfloat16)
    grad_w_one = jnp.einsum("rd,rf->df", second_in, grad_inner, preferred_element_type=jnp.float32)
    grad_bias_inner = jnp.sum(grad_inner, 0, dtype=jnp.float32)
    grad_second_in = jnp.einsum("rf,df->rd", grad_inner, w_one, preferred_element_type=jnp.float32)
    grad_gain_two, grad_bias_two, grad_middle_norm = norm_backward(
        grad_second_in, normed_two, factor_two, gain_two
    )
    grad_middle = grad_result + grad_middle_norm
    grad_mlp = jnp.concatenate([grad_w_one.reshape(-1), grad_w_two.reshape(-1)])
    grad_proj = grad_middle.astype(jnp.bfloat16)
    grad_w_out = jnp.einsum("rc,rd->cd", context_low, grad_proj, preferred_element_type=jnp.float32)
    grad_bias_out = jnp.sum(grad_proj, 0, dtype=jnp.float32)
    grad_context = jnp.einsum("rd,cd->rc", grad_proj, w_out, preferred_element_type=jnp.float32)
    grad_context = grad_context.astype(jnp.bfloat16).reshape(count, length, H, HD)
    probs = jnp.exp(masked_scores(query, keys, key_mask) - log_total)
    probs_again = probs.astype(jnp.bfloat16)
    grad_values = jnp.einsum(
        "shqk,sqhd->skhd", probs_again, grad_context, preferred_element_type=jnp.float32
    )
    grad_probs = jnp.einsum(
        "sqhd,skhd->shqk", grad_context, values, preferred_element_type=jnp.float32
    )
    inner_sum = jnp.sum(grad_probs * probs, -1, keepdims=True)
    grad_scores = (probs * (grad_probs - inner_sum)).astype(jnp.bfloat16)
    grad_query = (
        jnp.einsum("shqk,skhd->sqhd", grad_scores, keys, preferred_element_type=jnp.float32) * scale
    )
    grad_keys = (
        jnp.einsum("shqk,sqhd->skhd", grad_scores, query, preferred_element_type=jnp.float32)
        * scale
    )
    grad_qkv = (
        jnp.stack([grad_query, grad_keys, grad_values], 2)
        .reshape(total_rows, 3 * D)
        .astype(jnp.bfloat16)
    )
    grad_w_qkv = jnp.einsum("rd,re->de", first_in, grad_qkv, preferred_element_type=jnp.float32)
    grad_bias_qkv = jnp.sum(grad_qkv, 0, dtype=jnp.float32)
    grad_first_in = jnp.einsum("re,de->rd", grad_qkv, w_qkv, preferred_element_type=jnp.float32)
    grad_gain_one, grad_bias_one, grad_rows_norm = norm_backward(
        grad_first_in, normed_one, factor_one, gain_one
    )
    grad_rows = grad_middle + grad_rows_norm
    grad_samples = grad_rows.reshape(count, length, D).astype(jnp.bfloat16)
    grad_attn = jnp.concatenate([grad_w_qkv.reshape(-1), grad_w_out.reshape(-1)])
    grad_small = jnp.concatenate(
        [
            grad_gain_one,
            grad_bias_one,
            grad_bias_qkv[:D],
            grad_bias_qkv[2 * D :],
            grad_bias_out,
            grad_gain_two,
            grad_bias_two,
            grad_bias_inner,
            grad_bias_outer,
        ]
    )
    summed_attn, summed_mlp, summed_small = (
        scatter_sum(grad_attn),
        scatter_sum(grad_mlp),
        lax.psum_scatter(grad_small, ("wide", "narrow"), scatter_dimension=0, tiled=True),
    )
    new_attn, new_first_attn, new_second_attn = adamw(
        master_attn, first_attn, second_attn, summed_attn, 0.1, rate_matrix
    )
    new_mlp, new_first_mlp, new_second_mlp = adamw(
        master_mlp, first_mlp, second_mlp, summed_mlp, 0.1, rate_matrix
    )
    new_small, new_first_small, new_second_small = adamw(
        master_small, first_small, second_small, summed_small, 0.0, rate_small
    )
    return (
        output,
        grad_samples,
        new_attn,
        new_first_attn,
        new_second_attn,
        new_mlp,
        new_first_mlp,
        new_second_mlp,
        new_small,
        new_first_small,
        new_second_small,
    )


bf16 = jnp.bfloat16
f32 = jnp.float32
BLOCK = 256
BIN = 128
AXES = ("wide", "narrow")
ROW = 128
SMALL_ROWS = 72


def place_of(i):
    wide, z = divmod(i, 4)
    return wide // 4, (wide // 2) % 2, wide % 2, z


def index_of(y, x, c, z):
    return ((y * 2 + x) * 2 + c) * 4 + z


def pairs_of(move):
    return [(i, index_of(*move(*place_of(i)))) for i in range(32)]


TO_X = pairs_of(lambda y, x, c, z: (y, 1 - x, c, z))
TO_Y = pairs_of(lambda y, x, c, z: (1 - y, x, c, z))
TO_CORE = pairs_of(lambda y, x, c, z: (y, x, 1 - c, z))
TO_Z = [pairs_of(lambda y, x, c, z, k=k: (y, x, c, z ^ k)) for k in range(4)]


def send(value, pairs):
    return lax.ppermute(value, AXES, pairs)


def dot(a, b, dims=((1,), (0,))):
    return lax.dot_general(a, b, (dims, ((), ())), preferred_element_type=f32)


def at_rows(ref, start, size):
    return ref[pl.ds(start, size), :]


def attn_block(core, j):
    return (j // 3) * 6 + 3 * core + j % 3


def mlp_block(core, j):
    return (j // 6) * 12 + 6 * core + j % 6


def shifted(idx, vector, out):
    lane = lax.broadcasted_iota(jnp.int32, (3, ROW), 1)
    out[...] = jnp.zeros(out.shape, f32)
    for k in range(4):

        @pl.when(idx[4] == k)
        def _():
            turned = pltpu.roll(vector[...], 32 * k, 1) if k else vector[...]
            at = 2 * k
            out[at : at + 3, :] = jnp.where(lane >= 32 * k, turned, 0.0)
            if k:
                out[at + 1 : at + 4, :] += jnp.where(lane < 32 * k, turned, 0.0)


def cut_masters(idx, attn, mlp, small, keep_a, send_a, keep_m, send_m, place, half_a, half_m):
    wide, core = idx[0], idx[3]

    @pl.when(wide < 6)
    def _():
        for c in range(2):
            for j in range(9):
                rows = attn[pl.ds(attn_block(c, j), 32, stride=18), :]
                half_a[c, j * 32 : (j + 1) * 32, :] = rows.astype(bf16)

    @pl.when(wide >= 6)
    def _():
        for j in range(6):
            rows = attn[pl.ds(j, 96, stride=6), :]
            half_a[j // 3, (j % 3) * 96 : (j % 3 + 1) * 96, :] = rows.astype(bf16)

    @pl.when(wide < 4)
    def _():
        for c in range(2):
            for j in range(12):
                rows = mlp[pl.ds(mlp_block(c, j), 48, stride=24), :]
                half_m[c, j * 48 : (j + 1) * 48, :] = rows.astype(bf16)

    @pl.when(wide >= 4)
    def _():
        for j in range(6):
            rows = mlp[pl.ds(j, 192, stride=6), :]
            half_m[j // 3, (j % 3) * 192 : (j % 3 + 1) * 192, :] = rows.astype(bf16)

    first_a = jnp.where(wide < 6, core, 0)
    first_m = jnp.where(wide < 4, core, 0)
    keep_a[0:288, :] = half_a[first_a]
    send_a[0:288, :] = half_a[1 - first_a]
    keep_m[...] = half_m[first_m]
    send_m[...] = half_m[1 - first_m]
    shifted(idx, small, place)
    keep_a[288:304, :] = place[...].astype(bf16)
    send_a[288:304, :] = place[...].astype(bf16)


def pack_rows(idx, vis_own, vis_other, x_own, x_other, cot_own, cot_other, x_out, cot_out, meta, fill):
    core = idx[3]
    for b in range(16):
        fill[b] = 0
    bins = jnp.int32(0)
    for s in range(16):
        mine = core == s // 8
        seen = jnp.where(mine, vis_own[s % 8], vis_other[s % 8])
        need = ((seen + 15) >> 4) << 4
        chosen = jnp.int32(15)
        for b in reversed(range(s + 1)):
            chosen = jnp.where(fill[b] + need <= BIN, b, chosen)
        start = chosen * BIN + fill[chosen]
        fill[chosen] = fill[chosen] + need
        bins = jnp.maximum(bins, chosen + 1)
        meta[8 + s] = start
        meta[24 + s] = seen
    blocks = (bins + 1) >> 1
    meta[0] = blocks

    def clear(b, carry):
        at = pl.ds(pl.multiple_of(b * BLOCK, BLOCK), BLOCK)
        x_out[at, :] = jnp.zeros((BLOCK, D), bf16)
        cot_out[at, :] = jnp.zeros((BLOCK, D), bf16)
        return carry

    lax.fori_loop(0, blocks, clear, 0)
    row = lax.broadcasted_iota(jnp.int32, (16, D), 0)
    for s in range(16):
        start, seen = meta[8 + s], meta[24 + s]

        def fetch(x_in, cot_in):
            def chunk(k, carry):
                src = pl.ds(pl.multiple_of(k * 16, 16), 16)
                dst = pl.ds(pl.multiple_of(start + k * 16, 16), 16)
                x_out[dst, :] = x_in[s % 8, src, :]
                grad = cot_in[s % 8, src, :].astype(f32)
                cot_out[dst, :] = jnp.where(row + k * 16 < seen, grad, 0.0).astype(bf16)
                return carry

            lax.fori_loop(0, (seen + 15) >> 4, chunk, 0)

        @pl.when(core == s // 8)
        def _():
            fetch(x_own, cot_own)

        @pl.when(core != s // 8)
        def _():
            fetch(x_other, cot_other)


def owner_of(idx, column, k):
    y, x, z = idx[1], idx[2], idx[4]
    yy = 1 - y if column >= 2 else y
    xx = 1 - x if column % 2 else x
    return yy * 2 + xx, jnp.bitwise_xor(z, k)


def pair_of(n):
    return n // 4 * 2 + n % 2


def core_of(idx, part):
    return 1 - idx[3] if part else idx[3]


def lanes_of(small, first, count):
    rows = [small[q // 9, q % 9 : q % 9 + 1, :] for q in range(first, first + count)]
    return jnp.concatenate(rows, axis=1)


def same_sample(meta, which):
    lane = lax.broadcasted_iota(jnp.int32, (8, BIN), 1)
    line = lax.broadcasted_iota(jnp.int32, (BIN, BIN), 0)
    of_key = jnp.full((8, BIN), -2, jnp.int32)
    of_query = jnp.full((BIN, BIN), -1, jnp.int32)
    for s in range(16):
        start = meta[8 + s] - which * BIN
        stop = start + meta[24 + s]
        of_key = jnp.where((lane >= start) & (lane < stop), s, of_key)
        of_query = jnp.where((line >= start) & (line < stop), s, of_query)
    return of_query == of_key[0:1, :]


def halves(pair):
    lane = lax.broadcasted_iota(jnp.int32, pair.shape, 1)
    wide = pair.astype(f32)
    return jnp.concatenate(
        [jnp.where(lane < HD, wide, 0.0), jnp.where(lane >= HD, wide, 0.0)], axis=0
    ).astype(bf16)


def probabilities(query, keys, mask):
    scores = dot(halves(query), keys, ((1,), (1,))) * (1.0 / math.sqrt(HD))
    scores = jnp.where(mask, scores, -1e30)
    expo = jnp.exp(scores - jnp.max(scores, -1, keepdims=True))
    return expo * (1.0 / jnp.sum(expo, -1, keepdims=True))


def probabilities_by_key(both, keys, mask):
    scores = dot(keys, both, ((1,), (1,))) * (1.0 / math.sqrt(HD))
    scores = jnp.where(mask, scores, -1e30)
    expo = jnp.exp(scores - jnp.max(scores, 0, keepdims=True))
    return expo * (1.0 / jnp.sum(expo, 0, keepdims=True))


def one_above_other(wide):
    return jnp.concatenate([wide[:, :BIN], wide[:, BIN:]], axis=0)


def side_by_side(stacked):
    return jnp.concatenate([stacked[:BIN], stacked[BIN:]], axis=1)


def attn_forward(phase, meta, idx, x_ref, *refs):
    pairs = refs[:8]
    qkv_ref, context_ref, part_ref, w_qkv, w_out, vecs, shift, inner_bias, small = refs[8:]

    if phase == 0:
        small[...] = jnp.zeros(small.shape, f32)
        for n in range(16):
            piece = pairs[pair_of(n)].at[n % 4 // 2]
            chip, z = owner_of(idx, n // 4, n % 4)

            @pl.when(chip < 3)
            def _():
                for part in range(2):
                    owner = (chip * 2 + core_of(idx, part)) * 4 + z
                    to = pl.ds(pl.multiple_of(owner * 32, 32), 32)
                    for j in range(9):
                        at = part * 288 + j * 32
                        w_qkv[to, j * ROW : (j + 1) * ROW] = piece[at : at + 32, :]

            @pl.when(chip == 3)
            def _():
                to = pl.ds(pl.multiple_of(z * 96, 32), 96)
                for j in range(6):
                    w_out[to, j * ROW : (j + 1) * ROW] = piece[j * 96 : (j + 1) * 96, :]

            for part in range(2):
                group = chip * 2 + core_of(idx, part)
                at = 576 + part * 16
                small[group] = small[group] + piece[at : at + 16, :].astype(f32)
        for n, first in enumerate((0, 6, 24, 30, 36, 66)):
            vecs[n : n + 1, :] = lanes_of(small, first, 6)
        vecs[6:8, :] = jnp.zeros((2, D), f32)
        own = idx[3] == 0
        query_bias = jnp.where(own, lanes_of(small, 12, 3), lanes_of(small, 15, 3))
        value_bias = jnp.where(own, lanes_of(small, 18, 3), lanes_of(small, 21, 3))
        shift[...] = jnp.concatenate([query_bias, jnp.zeros((1, D // 2), f32), value_bias], axis=1)
        low = jnp.where(own, lanes_of(small, 42, 6), lanes_of(small, 48, 6))
        high = jnp.where(own, lanes_of(small, 54, 6), lanes_of(small, 60, 6))
        inner_bias[...] = jnp.concatenate([low, high], axis=1)

    if phase == 1:
        normed, _ = standard(x_ref[...].astype(f32))
        first_in = (normed * vecs[0:1, :] + vecs[1:2, :]).astype(bf16)
        qkv_ref[...] = (dot(first_in, w_qkv[...]) + shift[...]).astype(bf16)
        for b in range(BLOCK // BIN):
            mask = same_sample(meta, pl.program_id(0) * (BLOCK // BIN) + b)
            mask = jnp.concatenate([mask, mask], axis=0)
            rows = slice(b * BIN, (b + 1) * BIN)
            for h in range(3):
                query, keys, values = (
                    qkv_ref[rows, (3 * t + h) * ROW : (3 * t + h + 1) * ROW] for t in range(3)
                )
                probs = probabilities(query, keys, mask).astype(bf16)
                context = dot(side_by_side(probs), halves(values))
                context_ref[rows, h * ROW : (h + 1) * ROW] = context.astype(bf16)
        part_ref[...] = dot(context_ref[...], w_out[...]).astype(bf16)


TAIL = (0.5 * 0.254829592, 0.5 * -0.284496736, 0.5 * 1.421413741, 0.5 * -1.453152027, 0.5 * 1.061405429)


def normal_curves(u):
    t = 1.0 / (1.0 + (0.3275911 * inv_root_two) * jnp.abs(u))
    expo = jnp.exp(-0.5 * u * u)
    series = TAIL[4]
    for a in TAIL[3::-1]:
        series = series * t + a
    tail = series * t * expo
    return jnp.where(u < 0.0, tail, 1.0 - tail), expo * inv_root_tau


def block_of(rows):
    return rows.at[pl.ds(pl.multiple_of(pl.program_id(0) * BLOCK, BLOCK), BLOCK), :]


def middle_of(x_ref, part_own, part_other, vecs):
    parts = part_own[...].astype(f32) + part_other[...].astype(f32)
    return x_ref[...].astype(f32) + parts + vecs[2:3, :]


def mlp_both(phase, meta, idx, x_ref, part_own, cot_ref, vecs, inner_bias, other_rows, *refs):
    pieces = refs[:16]
    active_ref, back_ref, w_two_out, sums, inner_sum = refs[16:21]
    outs = refs[21:29]
    w_one, w_two, acc_one, acc_two, stage, arrived, written = refs[29:]

    def to_stage(n):
        return pltpu.make_async_copy(pieces[n], stage.at[n], arrived.at[n])

    def to_output():
        return pltpu.make_async_copy(w_two, w_two_out, written)

    if phase == 0:
        for n in range(16):
            to_stage(n).start()
        acc_one[...] = jnp.zeros(acc_one.shape, f32)
        acc_two[...] = jnp.zeros(acc_two.shape, f32)
        sums[...] = jnp.zeros(sums.shape, f32)
        inner_sum[...] = jnp.zeros(inner_sum.shape, f32)
        for n in range(16):
            to_stage(n).wait()
            piece = stage.at[n]
            chip, z = owner_of(idx, n // 4, n % 4)

            @pl.when(chip < 2)
            def _():
                for part in range(2):
                    owner = (chip * 2 + core_of(idx, part)) * 4 + z
                    to = pl.ds(pl.multiple_of(owner * 48, 16), 48)
                    for j in range(12):
                        at = part * 576 + j * 48
                        w_one[to, j * ROW : (j + 1) * ROW] = piece[at : at + 48, :]

            @pl.when(chip >= 2)
            def _():
                to = pl.ds(pl.multiple_of((chip - 2) * D + z * 192, 64), 192)
                for j in range(6):
                    w_two[to, j * ROW : (j + 1) * ROW] = piece[j * 192 : (j + 1) * 192, :]

        to_output().start()

    if phase == 1:
        normed, _ = standard(middle_of(x_ref, part_own, block_of(other_rows), vecs))
        second_in = (normed * vecs[3:4, :] + vecs[4:5, :]).astype(bf16)
        grad = cot_ref[...]
        back = jnp.zeros((BLOCK, D), f32)
        inner_grads = []
        for n in range(2):
            cols = slice(n * D, (n + 1) * D)
            inner = dot(second_in, w_one[:, cols]) + inner_bias[:, cols]
            bell, bump = normal_curves(inner)
            active = (inner * bell).astype(bf16)
            active_ref[:, cols] = active
            slope = bell + inner * bump
            grad_inner = (dot(grad, w_two[cols, :], ((1,), (1,))) * slope).astype(bf16)
            inner_grads.append(grad_inner)
            acc_two[cols, :] += dot(active, grad, ((0,), (0,)))
            inner_sum[:, cols] += jnp.sum(grad_inner.astype(f32), 0, keepdims=True)
            back = back + dot(grad_inner, w_one[:, cols], ((1,), (1,)))
        acc_one[...] += dot(second_in, jnp.concatenate(inner_grads, axis=1), ((0,), (0,)))
        back_ref[...] = back.astype(bf16)
        sums[0:1, :] += jnp.sum(back * normed, 0, keepdims=True)
        sums[1:2, :] += jnp.sum(back, 0, keepdims=True)
        sums[2:3, :] += jnp.sum(grad.astype(f32), 0, keepdims=True)

    if phase == 2:
        to_output().wait()
        for n in range(16):
            chip, z = owner_of(idx, n // 4, n % 4)
            out, k = outs[pair_of(n)], n % 4 // 2

            @pl.when(chip < 2)
            def _():
                for part in range(2):
                    owner = (chip * 2 + core_of(idx, part)) * 4 + z
                    rows = pl.ds(pl.multiple_of(owner * 48, 16), 48)
                    for j in range(12):
                        at = part * 576 + j * 48
                        out[k, at : at + 48, :] = acc_one[rows, j * ROW : (j + 1) * ROW].astype(bf16)

            @pl.when(chip >= 2)
            def _():
                rows = pl.ds(pl.multiple_of((chip - 2) * D + z * 192, 64), 192)
                for j in range(6):
                    out[k, j * 192 : (j + 1) * 192, :] = acc_two[rows, j * ROW : (j + 1) * ROW].astype(bf16)


def mlp_out(phase, meta, idx, active_ref, w_two, part_ref):
    if phase == 1:
        part_ref[...] = dot(active_ref[...], w_two[...]).astype(bf16)


def middle_backward(phase, meta, idx, x_ref, part_own, part_other, cot_ref, back_own, context_ref, w_out, vecs, other_rows,
                    grad_ref, grad_context_ref, acc_out, sums):
    if phase == 0:
        acc_out[...] = jnp.zeros(acc_out.shape, f32)
        sums[...] = jnp.zeros(sums.shape, f32)

    if phase == 1:
        normed, factor = standard(middle_of(x_ref, part_own, part_other, vecs))
        scaled = (back_own[...].astype(f32) + block_of(other_rows)[...].astype(f32)) * vecs[3:4, :]
        through = scaled - jnp.mean(scaled, -1, keepdims=True)
        through = through - normed * jnp.mean(scaled * normed, -1, keepdims=True)
        grad_middle = cot_ref[...].astype(f32) + factor * through
        grad_ref[...] = grad_middle
        grad_proj = grad_middle.astype(bf16)
        acc_out[...] += dot(context_ref[...], grad_proj, ((0,), (0,)))
        sums[0:1, :] += jnp.sum(grad_proj.astype(f32), 0, keepdims=True)
        grad_context_ref[...] = dot(grad_proj, w_out[...], ((1,), (1,))).astype(bf16)


def heads_backward(phase, meta, idx, qkv_ref, grad_context_ref, grads):
    if phase == 1:
        scale = 1.0 / math.sqrt(HD)
        for b in range(BLOCK // BIN):
            mask = same_sample(meta, pl.program_id(0) * (BLOCK // BIN) + b)
            mask = jnp.concatenate([mask, mask], axis=1)
            rows = slice(b * BIN, (b + 1) * BIN)
            cols = [[slice((3 * t + h) * ROW, (3 * t + h + 1) * ROW) for t in range(3)] for h in range(3)]
            both = [halves(qkv_ref[rows, cols[h][0]]) for h in range(3)]
            outs = [halves(grad_context_ref[rows, h * ROW : (h + 1) * ROW]) for h in range(3)]
            probs = [probabilities_by_key(both[h], qkv_ref[rows, cols[h][1]], mask) for h in range(3)]
            grad_probs = [dot(qkv_ref[rows, cols[h][2]], outs[h], ((1,), (1,))) for h in range(3)]
            for h in range(3):
                grads[rows, cols[h][2]] = dot(probs[h].astype(bf16), outs[h]).astype(bf16)
            scores = []
            for h in range(3):
                total = jnp.sum(grad_probs[h] * probs[h], 0, keepdims=True)
                scores.append((probs[h] * (grad_probs[h] - total)).astype(bf16))
            for h in range(3):
                grads[rows, cols[h][1]] = (dot(scores[h], both[h]) * scale).astype(bf16)
            for h in range(3):
                keys = halves(qkv_ref[rows, cols[h][1]])
                grads[rows, cols[h][0]] = (dot(one_above_other(scores[h]), keys, ((0,), (0,))) * scale).astype(bf16)


def first_backward(phase, meta, idx, x_ref, grads, w_qkv, acc_out, vecs, sums_in, inner_sum, sums_out, *refs):
    back_ref = refs[0]
    outs = refs[1:9]
    acc_qkv, sums, small = refs[9:]

    if phase == 0:
        acc_qkv[...] = jnp.zeros(acc_qkv.shape, f32)
        sums[...] = jnp.zeros(sums.shape, f32)

    if phase == 1:
        normed, _ = standard(x_ref[...].astype(f32))
        first_in = (normed * vecs[0:1, :] + vecs[1:2, :]).astype(bf16)
        grad_qkv = grads[...]
        acc_qkv[...] += dot(first_in, grad_qkv, ((0,), (0,)))
        back = dot(grad_qkv, w_qkv[...], ((1,), (1,)))
        back_ref[...] = back.astype(bf16)
        sums[0:1, :] += jnp.sum(back * normed, 0, keepdims=True)
        sums[1:2, :] += jnp.sum(back, 0, keepdims=True)
        sums[3:4, 0 : D // 2] += jnp.sum(grad_qkv[:, 0 : D // 2].astype(f32), 0, keepdims=True)
        sums[3:4, D // 2 : D] += jnp.sum(grad_qkv[:, D : D + D // 2].astype(f32), 0, keepdims=True)

    if phase == 2:
        small[...] = jnp.zeros(small.shape, f32)
        once = jnp.where(idx[3] == 0, 1.0, 0.0)

        def put(at, rows):
            for j in range(rows.shape[1] // ROW):
                q = at + j
                small[q // 9, q % 9 : q % 9 + 1, :] = rows[:, j * ROW : (j + 1) * ROW]

        put(0, sums[0:1, :])
        put(6, sums[1:2, :])
        put(24, sums_out[0:1, :] * once)
        put(30, sums_in[0:1, :])
        put(36, sums_in[1:2, :])
        put(66, sums_in[2:3, :] * once)
        for c in range(2):

            @pl.when(idx[3] == c)
            def _():
                put(12 + 3 * c, sums[3:4, 0 : D // 2])
                put(18 + 3 * c, sums[3:4, D // 2 : D])
                put(42 + 6 * c, inner_sum[:, 0:D])
                put(54 + 6 * c, inner_sum[:, D : 2 * D])

        for n in range(16):
            chip, z = owner_of(idx, n // 4, n % 4)
            out, k = outs[pair_of(n)], n % 4 // 2

            @pl.when(chip < 3)
            def _():
                for part in range(2):
                    owner = (chip * 2 + core_of(idx, part)) * 4 + z
                    rows = pl.ds(pl.multiple_of(owner * 32, 32), 32)
                    for j in range(9):
                        at = part * 288 + j * 32
                        out[k, at : at + 32, :] = acc_qkv[rows, j * ROW : (j + 1) * ROW].astype(bf16)

            @pl.when(chip == 3)
            def _():
                rows = pl.ds(pl.multiple_of(z * 96, 32), 96)
                for j in range(6):
                    out[k, j * 96 : (j + 1) * 96, :] = acc_out[rows, j * ROW : (j + 1) * ROW].astype(bf16)

            for part in range(2):
                group = chip * 2 + core_of(idx, part)
                out[k, 576 + part * 16 : 592 + part * 16, :] = small[group].astype(bf16)


def finish_rows(phase, meta, idx, x_ref, part_own, part_other, out_own, out_other, grad_ref, back_own, back_other, vecs,
                output, grad_samples, packed_out, packed_grad):
    if phase == 1:
        at = pl.ds(pl.multiple_of(pl.program_id(0) * BLOCK, BLOCK), BLOCK)
        parts = out_own[...].astype(f32) + out_other[...].astype(f32)
        result = middle_of(x_ref, part_own, part_other, vecs) + parts + vecs[5:6, :]
        packed_out[at, :] = result.astype(bf16)
        normed, factor = standard(x_ref[...].astype(f32))
        scaled = (back_own[...].astype(f32) + back_other[...].astype(f32)) * vecs[0:1, :]
        through = scaled - jnp.mean(scaled, -1, keepdims=True)
        through = through - normed * jnp.mean(scaled * normed, -1, keepdims=True)
        packed_grad[at, :] = (grad_ref[...] + factor * through).astype(bf16)

    if phase == 2:
        output[...] = jnp.zeros(output.shape, bf16)
        grad_samples[...] = jnp.zeros(grad_samples.shape, bf16)
        row = lax.broadcasted_iota(jnp.int32, (16, D), 0)
        for s in range(8):
            start, seen = meta[8 + idx[3] * 8 + s], meta[24 + idx[3] * 8 + s]

            def chunk(k, carry):
                src = pl.ds(pl.multiple_of(start + k * 16, 16), 16)
                dst = pl.ds(pl.multiple_of(k * 16, 16), 16)
                keep = row + k * 16 < seen
                for packed, out in ((packed_out, output), (packed_grad, grad_samples)):
                    out[s, dst, :] = jnp.where(keep, packed[src, :].astype(f32), 0.0).astype(bf16)
                return carry

            lax.fori_loop(0, (seen + 15) >> 4, chunk, 0)


def update_refs(master, first, second, grad, outs, decay, step_rate):
    for out, new in zip(outs, adamw(master[...], first[...], second[...], grad, decay, step_rate)):
        out[...] = new


def step_mlp(idx, master, first, second, keep, mine, other, new, new_first, new_second, half, grad):
    wide, core = idx[0], idx[3]
    at = jnp.where(wide < 4, core, 0)
    half[at] = keep[...]

    @pl.when(wide < 4)
    def _():
        half[1 - at] = other[...]

    @pl.when(wide >= 4)
    def _():
        half[1 - at] = mine[...]

    @pl.when(wide < 4)
    def _():
        for c in range(2):
            for j in range(12):
                grad[pl.ds(mlp_block(c, j), 48, stride=24), :] = half[c, j * 48 : (j + 1) * 48, :]

    @pl.when(wide >= 4)
    def _():
        for j in range(6):
            grad[pl.ds(j, 192, stride=6), :] = half[j // 3, (j % 3) * 192 : (j % 3 + 1) * 192, :]

    update_refs(master, first, second, grad[...], (new, new_first, new_second), 0.1, rate_matrix)


def step_attn(idx, master, first, second, keep, mine, other, master_s, first_s, second_s, keep_s, other_s,
              new, new_first, new_second, new_s, new_first_s, new_second_s, half, grad, place, small_grad):
    wide, core = idx[0], idx[3]
    at = jnp.where(wide < 6, core, 0)
    half[at] = keep[...]

    @pl.when(wide < 6)
    def _():
        half[1 - at] = other[...]

    @pl.when(wide >= 6)
    def _():
        half[1 - at] = mine[...]

    @pl.when(wide < 6)
    def _():
        for c in range(2):
            for j in range(9):
                grad[pl.ds(attn_block(c, j), 32, stride=18), :] = half[c, j * 32 : (j + 1) * 32, :]

    @pl.when(wide >= 6)
    def _():
        for j in range(6):
            grad[pl.ds(j, 96, stride=6), :] = half[j // 3, (j % 3) * 96 : (j % 3 + 1) * 96, :]

    update_refs(master, first, second, grad[...], (new, new_first, new_second), 0.1, rate_matrix)
    place[...] = keep_s[...] + other_s[...]
    lane = lax.broadcasted_iota(jnp.int32, (3, ROW), 1)
    for k in range(4):

        @pl.when(idx[4] == k)
        def _():
            at = 2 * k
            both = jnp.where(lane >= 32 * k, place[at : at + 3, :], place[at + 1 : at + 4, :])
            small_grad[...] = pltpu.roll(both, ROW - 32 * k, 1) if k else both

    update_refs(master_s, first_s, second_s, small_grad[...], (new_s, new_first_s, new_second_s), 0.0, rate_small)


def plus(*terms):
    return sum(t.astype(f32) for t in terms)


def nothing(idx, out):
    out[...] = jnp.zeros(out.shape, f32)


def lay_attn(idx, keep, mine, other, piece):
    piece[0:288, :] = keep[0:288, :]
    piece[576:592, :] = keep[288:304, :]
    piece[592:608, :] = other[288:304, :]

    @pl.when(idx[0] < 6)
    def _():
        piece[288:576, :] = other[0:288, :]

    @pl.when(idx[0] >= 6)
    def _():
        piece[288:576, :] = mine[0:288, :]


def lay_mlp(idx, keep, mine, other, piece):
    piece[0:576, :] = keep[...]

    @pl.when(idx[0] < 4)
    def _():
        piece[576:1152, :] = other[...]

    @pl.when(idx[0] >= 4)
    def _():
        piece[576:1152, :] = mine[...]


def lay_out(*refs):
    at = 0
    for ref in refs[:-1]:
        refs[-1][at : at + ref.shape[0], :] = ref[...]
        at += ref.shape[0]


def pair_up(first, second, pair):
    pair[0] = first[...]
    pair[1] = second[...]


def add_low(*refs):
    refs[-1][...] = plus(*(r[...] for r in refs[:-1])).astype(bf16)


def add_near_far(*refs):
    terms, (near, far) = refs[:-2], refs[-2:]
    near[...] = plus(*(r[0] for r in terms))
    far[...] = plus(*(r[1] for r in terms)).astype(bf16)


def add_last(half, near, other, *outs):
    total = near[...] + other[...].astype(f32)
    outs[0][...] = total[:half]
    outs[1][...] = total[half : 2 * half]
    for n, out in enumerate(outs[2:]):
        out[...] = total[2 * half + 16 * n : 2 * half + 16 * n + 16]


SENDS = {
    "cv": ("visible", TO_CORE),
    "cs": ("samples", TO_CORE),
    "cc": ("cotangent", TO_CORE),
    "sa": ("send_a", TO_CORE),
    "sm": ("send_m", TO_CORE),
    "z2a": ("pa", TO_Z[2]),
    "zOa": ("Ea", TO_Z[1]),
    "xEa": ("Ea", TO_X),
    "yEa": ("Ea", TO_Y),
    "xOa": ("zOa", TO_X),
    "yOa": ("zOa", TO_Y),
    "dEa": ("yEa", TO_X),
    "dOa": ("xOa", TO_Y),
    "z1m": ("pm", TO_Z[1]),
    "z2m": ("pm2", TO_Z[2]),
    "z3m": ("z2m", TO_Z[1]),
    "x0m": ("pm", TO_X),
    "y0m": ("pm", TO_Y),
    "x1m": ("h1m", TO_X),
    "y1m": ("h1m", TO_Y),
    "x2m": ("z2m", TO_X),
    "y2m": ("z2m", TO_Y),
    "x3m": ("z3m", TO_X),
    "y3m": ("z3m", TO_Y),
    "d0m": ("h0m", TO_X),
    "d1m": ("d0m", TO_Z[1]),
    "d2m": ("x2m", TO_Y),
    "d3m": ("d2m", TO_Z[1]),
    "pt": ("part", TO_CORE),
    "bk": ("back", TO_CORE),
    "ot": ("out_part", TO_CORE),
    "fb": ("first_back_2", TO_CORE),
}
for group in "am":
    SENDS |= {
        "rE" + group: ("dE" + group + "_grad", TO_X),
        "rO" + group: ("dO" + group + "_grad", TO_Y),
        "pE" + group: ("xE" + group + "_grad", TO_X),
        "pO" + group: ("yO" + group + "_grad", TO_Y),
        "qE" + group: ("aE" + group, TO_Y),
        "qO" + group: ("aO" + group, TO_X),
        "wO" + group: ("so" + group, TO_Z[1]),
        "w2" + group: ("far" + group, TO_Z[2]),
        "g" + group: ("other" + group, TO_CORE),
    }
SENDS["gs"] = ("other_small", TO_CORE)
PAIR_NAMES = ("E{}_grad", "O{}_grad", "xE{}_grad", "xO{}_grad", "yE{}_grad", "yO{}_grad", "dE{}_grad", "dO{}_grad")

IN_HBM = ("first_back", "out_part", "grad_context", "output", "done_m")
AFTER = {
    "sum": ("fara",),
    "szm": ("aEa",),
    "soa": ("aEa",),
    "aOa": ("rEa",),
    "pa": ("cs", "cc", "cv"),
    "pm": ("pa",),
    "Ea": ("meta",),
    "pm2": ("Ea",),
    "h1m": ("xOa",),
    "h0m": ("xOa",),
    "fwd": ("x0m", "y0m", "z2m"),
    "there": ("x3m", "y3m", "d1m", "d2m", "d3m", "x2m", "d0m", "vecs"),
    "mlp": ("there",),
    "bw1": ("out_part",),
    "aEm": ("grad_context",),
    "aOm": ("grad_context",),
    "bw2": ("aEm", "aOm"),
    "bw3": ("ot",),
    "som": ("qEm", "pEm"),
    "fin": ("soa",),
    "sza": ("output",),
    "sua": ("done_m",),
}

ORDER = (
    "+cv", "+cs", "+cc", "=cut", "+sa", "+sm", "=pack", "=pa", "+z2a", "=pm", "+z1m", "+x0m", "+y0m", "=Ea", "=pm2", "+z2m",
    "+zOa", "+xEa", "+yEa", "+dEa", "+yOa", "+z3m", "+xOa", "=h1m", "=h0m", "+x1m", "+y1m", "+y2m", "+x2m", "+d0m", "+dOa", "+y3m",
    "+x3m", "+d2m", "=fwd", "+pt", "+d1m", "+d3m", "=there", "=mlp", "+rEm", "+rOm", "+bk", "=mout", "+ot", "=bw1", "=aEm", "=aOm",
    "+qOm", "+qEm", "+pEm", "+pOm", "=bw2", "=bw3", "+rEa", "+rOa", "=som", "+fb", "+wOm", "=aEa", "=aOa", "+qOa", "+qEa", "+pEa",
    "+pOa", "=soa", "+wOa", "=fin", "=sza", "+w2a", "=szm", "+w2m", "=sum", "+gm", "=om", "=sua", "+ga", "+gs", "=oa",
)


SMEM = pl.BlockSpec(memory_space=pltpu.SMEM)
VMEM = pl.BlockSpec(memory_space=pltpu.VMEM)
ANY = pl.BlockSpec(memory_space=pl.ANY)


def array(shape, dtype=bf16):
    return jax.ShapeDtypeStruct(shape, dtype)


def large(shape, dtype=bf16):
    return pltpu.HBM(shape, dtype)


def params(mib):
    return pltpu.CompilerParams(vmem_limit_bytes=mib << 20)


SCALE = 10**9
COSTS = {
    "attn_forward": 11, "mlp_both": 23, "mlp_out": 20, "middle_backward": 8, "heads_backward": 25, "first_backward": 25,
    "finish_rows": 8, "pack_rows": 6, "all_there": 60,
}


def cost(name):
    return pl.CostEstimate(flops=COSTS.get(name, 1) * SCALE, bytes_accessed=1, transcendentals=0)


def in_hbm(value):
    return pltpu.with_memory_space_constraint(value, pltpu.HBM)


def full(value):
    return pl.BlockSpec(value.shape, lambda i: (0,) * len(value.shape))


def over_blocks(body, rows_in, fixed_in, rows_out, fixed_out, scratch, mib, name, after=(), far=None):
    many = rows_in + [w for w, _, _ in rows_out]
    n_in, n_out = len(rows_in), len(rows_out)

    def kernel(meta, idx, *refs):
        refs = refs[: n_in + fixed_in] + refs[n_in + fixed_in + len(after) :]
        rows, fixed, lines, rest = (
            refs[:n_in], refs[n_in : n_in + fixed_in], refs[n_in + fixed_in :][:n_out], refs[n_in + fixed_in + n_out :]
        )
        body(0, meta, idx, *rows, *fixed, *lines, *rest)

        def one(*blocks):
            body(1, meta, idx, *blocks[:n_in], *fixed, *blocks[n_in:], *rest)

        specs = [pl.BlockSpec((BLOCK, w), lambda i: (i, 0)) for w in many]
        pltpu.emit_pipeline(one, grid=(meta[0],), in_specs=specs[:n_in], out_specs=specs[n_in:])(*rows, *lines)
        body(2, meta, idx, *rows, *fixed, *lines, *rest)

    def fixed_specs(arrays, first):
        if far is None:
            return [full(a) for a in arrays]
        return [ANY if first + n in far else VMEM for n in range(len(arrays))]

    def called(meta, idx, *args):
        return pl.pallas_call(
            kernel,
            in_specs=[SMEM, SMEM] + [ANY] * n_in + fixed_specs(args[n_in:], 0) + [ANY] * len(after),
            out_specs=[ANY] * n_out + fixed_specs(fixed_out, fixed_in),
            out_shape=[large((n, w), t) for w, t, n in rows_out] + fixed_out,
            scratch_shapes=scratch,
            compiler_params=params(mib),
            cost_estimate=cost(name),
            name=name,
            **({"grid": (1,)} if far is None else {}),
        )(meta, idx, *args, *after)

    return called


def at_once(body, scalars, outs, scratch, mib, name, after=(), copied=False):
    def kernel(*refs):
        n = len(refs) - len(scratch) - len(outs) - len(after)
        body(*refs[:n], *refs[n + len(after) :])

    def called(*args):
        grid = {"grid": (1,)} if copied else {}
        blocks = [full(a) if copied else VMEM for a in args[scalars:]]
        arrays = [in_hbm(a) for a in args[scalars:]] if copied else args[scalars:]
        return pl.pallas_call(
            kernel,
            in_specs=[SMEM] * scalars + blocks + [ANY] * len(after),
            out_specs=[SMEM if a.dtype == jnp.int32 else full(a) if copied else VMEM for a in outs],
            out_shape=outs,
            scratch_shapes=scratch,
            compiler_params=params(mib),
            cost_estimate=cost(name),
            name=name,
            **grid,
        )(*args[:scalars], *arrays, *after)

    return called


def on_core(
    samples,
    cotangent,
    visible,
    master_attn,
    first_attn,
    second_attn,
    master_mlp,
    first_mlp,
    second_mlp,
    master_small,
    first_small,
    second_small,
):
    count, length, _ = samples.shape
    rows = 2 * count * length
    wide, z = lax.axis_index("wide"), lax.axis_index("narrow")
    idx = jnp.stack([wide, wide // 4, (wide // 2) % 2, wide % 2, z]).astype(jnp.int32)

    def lanes(flat):
        return flat.reshape(-1, ROW)

    def three_rows(vector):
        return lanes(jnp.pad(vector, (0, 3 * ROW - vector.shape[0])))

    half_a, half_m = (288, ROW), (576, ROW)
    shape_m, shape_a, shape_s = (1152, ROW), (576, ROW), (16, ROW)
    pair_a, pair_m = (2, 608, ROW), (2, 1152, ROW)

    def after(name):
        return tuple(in_hbm(v[n]) if n in IN_HBM else v[n] for n in AFTER.get(name, ()))

    v = {"visible": visible, "samples": samples, "cotangent": cotangent}

    def hbm(*names):
        return tuple(v[n] if n in SENDS else in_hbm(v[n]) for n in names)

    def cut():
        swap_a = (304, ROW)
        v["keep_a"], v["send_a"], v["keep_m"], v["send_m"] = at_once(
            cut_masters, 1, [array(swap_a), array(swap_a), array(half_m), array(half_m)],
            [pltpu.VMEM(shape_s, f32), pltpu.VMEM((2, *half_a), bf16), pltpu.VMEM((2, *half_m), bf16)], 8, "cut_masters", after("cut"), True,
        )(idx, lanes(master_attn), lanes(master_mlp), three_rows(master_small))

    def piece_a():
        v["pa"] = at_once(lay_attn, 1, [array((608, ROW))], [], 8, "piece_attn", after("pa"))(
            idx, v["keep_a"], v["send_a"], v["sa"]
        )[0]

    def even_a():
        v["Ea"] = at_once(
            pair_up, 0, [array(pair_a)], [], 8, "pair_up", after("Ea")
        )(v["pa"], v["z2a"])[0]

    def piece_m():
        v["pm"] = at_once(lay_mlp, 1, [array(shape_m)], [], 8, "piece_mlp", after("pm"))(
            idx, v["keep_m"], v["send_m"], v["sm"]
        )[0]

    def again_m():
        v["pm2"] = at_once(lay_out, 0, [array(shape_m)], [], 8, "piece_again", after("pm2"))(v["pm"])[0]

    def pack():
        v["x"], v["cot"], v["meta"] = at_once(
            pack_rows, 3, [large((rows, D)), large((rows, D)), array((64,), jnp.int32)],
            [pltpu.SMEM((16,), jnp.int32)], 32, "pack_rows", after("pack"),
        )(idx, visible, v["cv"], in_hbm(samples), v["cs"], in_hbm(cotangent), v["cc"])

    def forward():
        outs = [large((D, 3 * D // 2)), large((D // 2, D)), array((8, D), f32), array((1, 3 * D // 2), f32), array((1, FF // 2), f32)]
        (v["qkv"], v["context"], v["part"], v["w_qkv"], v["w_out"], v["vecs"], shift, v["inner_bias"]) = over_blocks(
            attn_forward, [D], 8, [(3 * D // 2, bf16, rows), (D // 2, bf16, rows), (D, bf16, rows)], outs,
            [pltpu.VMEM((8, 16, ROW), f32)], 24, "attn_forward", after("fwd"),
        )(v["meta"], idx, *hbm("x"), v["Ea"], *(v[n] for n in ("zOa", "xEa", "xOa", "yEa", "yOa", "dEa", "dOa")))

    def hold_1():
        v["h1m"] = at_once(lay_out, 0, [array(shape_m)], [], 8, "hold_first", after("h1m"))(v["z1m"])[0]

    def hold_0():
        v["h0m"] = at_once(lay_out, 0, [array(shape_m)], [], 8, "hold_own", after("h0m"))(v["y0m"])[0]

    def there():
        v["there"] = at_once(nothing, 1, [array((8, ROW), f32)], [], 4, "all_there", after("there"))(idx)[0]

    def middle():
        return hbm("x", "part", "pt")

    def mlp():
        pieces = [v["pm"] if c + k == "z0" else v[c + k + "m"] for c in "zxyd" for k in "0123"]
        done = over_blocks(
            mlp_both, [D] * 3, 19, [(FF // 2, bf16, rows), (D, bf16, rows)],
            [large((FF // 2, D)), array((8, D), f32), array((1, FF // 2), f32)] + [array(pair_m)] * 8,
            [pltpu.VMEM((D, FF // 2), bf16), pltpu.VMEM((FF // 2, D), bf16), pltpu.VMEM((D, FF // 2), f32), pltpu.VMEM((FF // 2, D), f32),
             pltpu.VMEM((16, *shape_m), bf16), pltpu.SemaphoreType.DMA((16,)), pltpu.SemaphoreType.DMA],
            40, "mlp_both", after("mlp"), {*range(3, 19), 19},
        )(v["meta"], idx, *hbm("x", "part", "cot"), v["vecs"], v["inner_bias"], v["pt"], *pieces)
        v["active"], v["back"], v["w_two"], v["sums"], v["inner_sum"] = done[:5]
        v.update(zip((n.format("m") for n in PAIR_NAMES), done[5:]))

    def out_rows():
        v["out_part"] = over_blocks(mlp_out, [FF // 2], 1, [(D, bf16, rows)], [], [], 16, "mlp_out", after("mout"))(
            v["meta"], idx, *hbm("active", "w_two")
        )[0]

    def backward_1():
        v["grad_middle"], v["grad_context"], v["acc_out"], v["sums_out"] = over_blocks(
            middle_backward, [D] * 5 + [D // 2], 3, [(D, f32, rows), (D // 2, bf16, rows)],
            [large((D // 2, D), f32), array((8, D), f32)], [], 16, "middle_backward", after("bw1"),
        )(v["meta"], idx, *middle(), *hbm("cot", "back", "context", "w_out"), v["vecs"], v["bk"])

    def backward_2():
        v["grad_qkv"] = over_blocks(
            heads_backward, [3 * D // 2, D // 2], 0, [(3 * D // 2, bf16, rows)], [], [], 16, "heads_backward", after("bw2"),
        )(v["meta"], idx, *hbm("qkv", "grad_context"))[0]

    def backward_3():
        done = over_blocks(
            first_backward, [D, 3 * D // 2], 6, [(D, bf16, rows)], [array(pair_a)] * 8,
            [pltpu.VMEM((D, 3 * D // 2), f32), pltpu.VMEM((8, D), f32), pltpu.VMEM((8, 16, ROW), f32)],
            20, "first_backward", after("bw3"),
        )(v["meta"], idx, *hbm("x", "grad_qkv"), *hbm("w_qkv", "acc_out"), *(v[n] for n in ("vecs", "sums", "inner_sum", "sums_out")))
        v["first_back"] = done[0]
        v.update(zip((n.format("a") for n in PAIR_NAMES), done[1:]))

    def finish():
        v["output"], v["grad_samples"] = over_blocks(
            finish_rows, [D] * 8, 1, [], [large((count, length, D))] * 2, [pltpu.VMEM((rows, D), bf16)] * 2, 24, "finish_rows", after("fin"),
        )(v["meta"], idx, *middle(), *hbm("out_part", "ot", "grad_middle", "first_back_2", "fb"), v["vecs"])

    def adds(g):
        pair, half = (pair_a, 288) if g == "a" else (pair_m, 576)

        def add(body, terms, outs, name):
            return at_once(
                body, 0, outs, [], 24, name + g, after(name + g)
            )(*(v[t] for t in terms))

        def even_in():
            v["aE" + g] = add(add_low, [f"yE{g}_grad", "rE" + g], [array(pair)], "aE")[0]

        def odd_in():
            v["aO" + g] = add(add_low, [f"xO{g}_grad", "rO" + g], [array(pair)], "aO")[0]

        def odd_sum():
            terms = [f"O{g}_grad", "pO" + g, "qO" + g]
            if g == "a":
                v["so" + g] = add(add_low, terms, [array(pair)], "so")[0]
                return
            waited = after("som")
            v["som"], v["first_back_2"] = pl.pallas_call(
                lambda a, b, c, *refs: add_low(a, b, c, refs[-2]),
                in_specs=[VMEM] * 3 + [ANY] * (1 + len(waited)),
                out_specs=[VMEM, ANY],
                out_shape=[array(pair), large((rows, D))],
                input_output_aliases={3: 1},
                compiler_params=params(24),
                cost_estimate=cost("som"),
                name="som",
            )(*(v[t] for t in terms), in_hbm(v["first_back"]), *waited)

        def even_sum():
            v["near" + g], v["far" + g] = add(
                add_near_far, [f"E{g}_grad", "pE" + g, "qE" + g, "wO" + g], [array(pair[1:], f32), array(pair[1:])], "sz"
            )

        def last_sum():
            outs = [array((half, ROW), f32)] * 2 + ([array(shape_s, f32)] * 2 if g == "a" else [])
            done = add(functools.partial(add_last, half), ["near" + g, "w2" + g], outs, "su")
            v["own" + g], v["other" + g] = done[:2]
            if g == "a":
                v["own_small"], v["other_small"] = done[2:]

        return {"aE" + g: even_in, "aO" + g: odd_in, "so" + g: odd_sum, "sz" + g: even_sum, "su" + g: last_sum}

    def optimize_m():
        v["new_mlp"] = at_once(
            step_mlp, 1, [large(shape_m, f32)] * 3,
            [pltpu.VMEM((2, *half_m), f32), pltpu.VMEM(shape_m, f32)], 16, "step_mlp", after("om"),
        )(idx, lanes(master_mlp), lanes(first_mlp), lanes(second_mlp), v["ownm"], v["otherm"], v["gm"])
        v["done_m"] = v["new_mlp"][0]

    def optimize_a():
        v["new_attn"] = at_once(
            step_attn, 1, [array(shape_a, f32)] * 3 + [array((3, ROW), f32)] * 3,
            [pltpu.VMEM((2, *half_a), f32), pltpu.VMEM(shape_a, f32), pltpu.VMEM(shape_s, f32), pltpu.VMEM((3, ROW), f32)], 16, "step_attn", after("oa"),
        )(idx, lanes(master_attn), lanes(first_attn), lanes(second_attn), v["owna"], v["othera"], v["ga"],
          three_rows(master_small), three_rows(first_small), three_rows(second_small), v["own_small"], v["gs"])

    works = {"cut": cut, "pa": piece_a, "Ea": even_a, "pm": piece_m, "pm2": again_m, "pack": pack, "there": there, "h1m": hold_1, "h0m": hold_0, "fwd": forward, "mlp": mlp, "mout": out_rows,
             "bw1": backward_1, "bw2": backward_2, "bw3": backward_3, "fin": finish, "om": optimize_m, "oa": optimize_a, **adds("m"), **adds("a")}
    for step in ORDER:
        kind, name = step[0], step[1:]
        if kind == "+":
            source, pairs = SENDS[name]
            v[name] = send(v[source], pairs)
        else:
            works[name]()

    new_mlp, new_attn, output, grad_samples = v["new_mlp"], v["new_attn"], v["output"], v["grad_samples"]
    new_small = [a.reshape(-1)[:288] for a in new_attn[3:]]
    return (output, grad_samples, *(v.reshape(-1) for v in new_attn[:3]), *(v.reshape(-1) for v in new_mlp), *new_small)


def solution(mesh):
    in_specs = (
        P(("wide", "narrow"), None, None),
        P(("wide", "narrow"), None, None),
        P(("wide", "narrow")),
        P(("wide", "narrow")),
        P(("wide", "narrow")),
        P(("wide", "narrow")),
        P(("wide", "narrow")),
        P(("wide", "narrow")),
        P(("wide", "narrow")),
        P(("wide", "narrow")),
        P(("wide", "narrow")),
        P(("wide", "narrow")),
    )
    out_specs = (
        P(("wide", "narrow"), None, None),
        P(("wide", "narrow"), None, None),
        P(("wide", "narrow")),
        P(("wide", "narrow")),
        P(("wide", "narrow")),
        P(("wide", "narrow")),
        P(("wide", "narrow")),
        P(("wide", "narrow")),
        P(("wide", "narrow")),
        P(("wide", "narrow")),
        P(("wide", "narrow")),
    )
    small_slice = mesh.shape["wide"] == 8 and mesh.shape["narrow"] == 4
    return jax.shard_map(
        on_core if small_slice else on_device, mesh=mesh, in_specs=in_specs, out_specs=out_specs, check_vma=False
    )
```
